32 devices in a mesh: seq: 4 (over y, x), ctx: 4 (over z), fsdp: 2 (over core).
Axes of the slice: x: 2, y: 2, z: 4, core: 2. Of those that a mesh axis runs over, the one named last changes fastest.
Arguments:
- tokens: bfloat16 [8, 2048, 1024], P(('seq', 'fsdp'), 'ctx'), may hold values from -6 to 6
- cotangent: bfloat16 [8, 2048, 1024], P(('seq', 'fsdp'), 'ctx'), may hold values from -6 to 6
- global_pos: int32 [8, 64], P(('seq', 'fsdp')), may hold values from 0 to 2047, as said below
- attn_gain: bfloat16 [1024], P('fsdp'), may hold values from 0.5 to 1.5
- attn_shift: bfloat16 [1024], P('fsdp'), may hold values from -1 to 1
- mlp_gain: bfloat16 [1024], P('fsdp'), may hold values from 0.5 to 1.5
- mlp_shift: bfloat16 [1024], P('fsdp'), may hold values from -1 to 1
- qkv_weight: bfloat16 [1024, 3072], P('fsdp'), may hold values from -0.1875 to 0.1875
- qkv_bias: bfloat16 [3072], P('fsdp'), may hold values from -1 to 1
- proj_weight: bfloat16 [1024, 1024], P('fsdp'), may hold values from -0.5 to 0.5
- proj_bias: bfloat16 [1024], P('fsdp'), may hold values from -1 to 1
- up_weight: bfloat16 [1024, 4096], P('fsdp'), may hold values from -0.1875 to 0.1875
- up_bias: bfloat16 [4096], P('fsdp'), may hold values from -1 to 1
- down_weight: bfloat16 [4096, 1024], P('fsdp'), may hold values from -0.09375 to 0.09375
- down_bias: bfloat16 [1024], P('fsdp'), may hold values from -1 to 1
Outputs:
- layer_out: bfloat16 [8, 2048, 1024], P(('seq', 'fsdp'), 'ctx')
- tokens_grad: float32 [8, 2048, 1024], P(('seq', 'fsdp'), 'ctx')
- attn_gain_grad: float32 [1024], P('fsdp')
- attn_shift_grad: float32 [1024], P('fsdp')
- mlp_gain_grad: float32 [1024], P('fsdp')
- mlp_shift_grad: float32 [1024], P('fsdp')
- qkv_weight_grad: float32 [1024, 3072], P('fsdp')
- qkv_bias_grad: float32 [3072], P('fsdp')
- proj_weight_grad: float32 [1024, 1024], P('fsdp')
- proj_bias_grad: float32 [1024], P('fsdp')
- up_weight_grad: float32 [1024, 4096], P('fsdp')
- up_bias_grad: float32 [4096], P('fsdp')
- down_weight_grad: float32 [4096, 1024], P('fsdp')
- down_bias_grad: float32 [1024], P('fsdp')
The draws below stay inside these ranges and needn't reach their ends.
Inputs may be any that keep to these rules, and one draw needn't show every extreme that they name: `global_pos`: each row rises strictly; its g-th entry lies in [g * 32, (g + 1) * 32); in some row the first entry is 0 and the last is 2047.
All inputs are finite; a program needn't handle non-finite values.
Results may differ from the reference program's by a relative error of at most 0.011.
Values may be sent and summed in bfloat16 or wider, within the bound.
No kernel may reach another device: no remote copies, remote signals or barrier semaphores. Data moves between devices by JAX's collectives and lax.ppermute only.
A program may use at most 320 MiB of HBM per device.

```python
import jax
import jax.numpy as jnp
from jax import lax

D = 1024
H = 16
HD = 64
ROT = 16
FF = 4096
WIN = 512
NG = 64
BLK = 512
SEQ_LEN = 2048
SEQS = 8


def draw_global_pos(key, part):
    key = jax.random.fold_in(key, 7)
    stride = SEQ_LEN // NG
    offsets = jax.random.randint(jax.random.fold_in(key, 1), (SEQS, NG), 0, stride)
    chosen = jax.random.randint(jax.random.fold_in(key, 2), (), 0, SEQS)
    row_ids = jnp.arange(SEQS, dtype=jnp.int32)[:, None]
    col_ids = jnp.arange(NG, dtype=jnp.int32)[None, :]
    offsets = jnp.where((row_ids == chosen) & (col_ids == 0), 0, offsets)
    offsets = jnp.where((row_ids == chosen) & (col_ids == NG - 1), stride - 1, offsets)
    return (col_ids * stride + offsets).astype(jnp.int32)


def levels(own_key, shape, cuts, low, top_value):
    loudness, own = 1.0, jax.random.fold_in(own_key, 6)
    for axis_at, blocks in cuts:
        heights = jnp.exp(jax.random.uniform(jax.random.fold_in(own, axis_at), (blocks,), jnp.float32, low / len(cuts), top_value / len(cuts)))
        loudness = loudness * jnp.repeat(heights, shape[axis_at] // blocks).reshape([-1 if axis == axis_at else 1 for axis in range(len(shape))])
    return loudness


def scatter_about(rng, shape, width, limit, pieces=(), kind=jnp.bfloat16):
    array = width * jax.random.normal(rng, shape, jnp.float32)
    if pieces:
        array = array * levels(rng, shape, pieces, -0.22, 0.18)
    return jnp.clip(array, -limit, limit).astype(kind)


def setup_inputs(seed: int = 0) -> dict:
    key_of = jax.random.split(jax.random.key(seed), 16)
    tokens = scatter_about(key_of[0], (SEQS, SEQ_LEN, D), 1.0, 6.0, ((0, 8), (1, 4)))
    cotangent = scatter_about(key_of[1], (SEQS, SEQ_LEN, D), 1.0, 6.0, ((0, 8), (1, 4)))
    global_pos = draw_global_pos(jax.random.fold_in(key_of[15], 71), 0)
    attn_gain = jnp.clip(1.0 + 0.1 * jax.random.normal(key_of[3], (D,), jnp.float32), 0.5, 1.5).astype(jnp.bfloat16)
    attn_shift = scatter_about(key_of[4], (D,), 0.2, 1.0, ((0, 2),))
    mlp_gain = jnp.clip(1.0 + 0.1 * jax.random.normal(key_of[5], (D,), jnp.float32), 0.5, 1.5).astype(jnp.bfloat16)
    mlp_shift = scatter_about(key_of[6], (D,), 0.2, 1.0, ((0, 2),))
    qkv_weight = scatter_about(key_of[7], (D, 3 * D), D ** -0.5, 0.1875, ((0, 2),))
    qkv_bias = scatter_about(key_of[8], (3 * D,), 0.2, 1.0, ((0, 2),))
    proj_weight = scatter_about(key_of[9], (D, D), (D // 8) ** -0.5, 0.5, ((0, 2),))
    proj_bias = scatter_about(key_of[10], (D,), 0.2, 1.0, ((0, 2),))
    up_weight = scatter_about(key_of[11], (D, FF), D ** -0.5, 0.1875, ((0, 2),))
    up_bias = scatter_about(key_of[12], (FF,), 0.2, 1.0, ((0, 2),))
    down_weight = scatter_about(key_of[13], (FF, D), FF ** -0.5, 0.09375, ((0, 2),))
    down_bias = scatter_about(key_of[14], (D,), 0.2, 1.0, ((0, 2),))
    return {"tokens": tokens, "cotangent": cotangent, "global_pos": global_pos, "attn_gain": attn_gain, "attn_shift": attn_shift, "mlp_gain": mlp_gain, "mlp_shift": mlp_shift, "qkv_weight": qkv_weight, "qkv_bias": qkv_bias, "proj_weight": proj_weight, "proj_bias": proj_bias, "up_weight": up_weight, "up_bias": up_bias, "down_weight": down_weight, "down_bias": down_bias}


@jax.custom_vjp
def low(v):
    return lax.optimization_barrier(v.astype(jnp.bfloat16)).astype(jnp.float32)

@jax.custom_vjp
def low_back(v):
    return v

def low_keep(v):
    return (low(v), None)

def low_pass(kept, grad):
    return (grad,)

def back_keep(v):
    return (v, None)

def back_low(kept, grad):
    return (low(grad),)
low.defvjp(low_keep, low_pass)
low_back.defvjp(back_keep, back_low)
epsilon = 1e-05
negative = -1e+30
rotary_base = 10000.0

def layer_norm_forward(values, gain, shift):
    center = values - lax.optimization_barrier(jnp.mean(values, axis=-1, keepdims=True))
    invstd = lax.rsqrt(lax.optimization_barrier(jnp.mean(center * center, axis=-1, keepdims=True)) + epsilon)
    return center * invstd * gain + shift

def rotary_tables(positions, rotary):
    half = rotary // 2
    freqs = rotary_base ** (-2.0 * jnp.arange(half, dtype=jnp.float32) / rotary)
    angles = positions.astype(jnp.float32)[:, None] * freqs[None, :]
    return (jnp.cos(angles), jnp.sin(angles))

def rotate(field, cosine, sine, direction):
    half = cosine.shape[1]
    first = field[..., :half]
    second = field[..., half:2 * half]
    remain = field[..., 2 * half:]
    cos_wide = cosine[:, None, :]
    sin_wide = sine[:, None, :] * direction
    return jnp.concatenate([first * cos_wide - second * sin_wide, second * cos_wide + first * sin_wide, remain], axis=-1)

def masked_softmax(scores, mask):
    masked = jnp.where(mask, scores, negative)
    top = lax.optimization_barrier(jnp.max(masked, axis=-1, keepdims=True))
    total = lax.optimization_barrier(jnp.sum(jnp.where(mask, jnp.exp(masked - top), 0.0), axis=-1, keepdims=True))
    return jnp.where(mask, jnp.exp(masked - (top + jnp.log(total))), 0.0)

def attend(query, keys, values, glob_pos):
    length = query.shape[0]
    scale = HD ** (-0.5)
    highest = lax.Precision.HIGHEST
    glob_keys = jnp.take(keys, glob_pos, axis=0)
    glob_values = jnp.take(values, glob_pos, axis=0)
    padding = jnp.zeros((BLK, H, HD), dtype=query.dtype)
    keys_pad = jnp.concatenate([padding, keys], axis=0)
    values_pad = jnp.concatenate([padding, values], axis=0)

    def block(index):
        start = (index * BLK).astype(jnp.int32)
        block_query = lax.dynamic_slice_in_dim(query, start, BLK, 0)
        block_keys = jnp.concatenate([lax.dynamic_slice_in_dim(keys_pad, start, 2 * BLK, 0), glob_keys], axis=0)
        block_values = jnp.concatenate([lax.dynamic_slice_in_dim(values_pad, start, 2 * BLK, 0), glob_values], axis=0)
        query_pos = start + jnp.arange(BLK, dtype=jnp.int32)
        key_pos = start - BLK + jnp.arange(2 * BLK, dtype=jnp.int32)
        offset = query_pos[:, None] - key_pos[None, :]
        near_mask = (offset >= 0) & (offset < WIN) & (key_pos[None, :] >= 0)
        far_mask = query_pos[:, None] - glob_pos[None, :] >= WIN
        mask = jnp.concatenate([near_mask, far_mask], axis=1)[None]
        scores = low_back(jnp.einsum('qhd,khd->hqk', block_query, block_keys, precision=highest) * scale)
        prob = masked_softmax(scores, mask)
        return jnp.einsum('hqk,khd->qhd', low(prob), block_values, precision=highest)
    near = lax.map(jax.checkpoint(block), jnp.arange(length // BLK, dtype=jnp.int32)).reshape(length, H, HD)
    glob_query = jnp.take(query, glob_pos, axis=0)
    positions = jnp.arange(length, dtype=jnp.int32)
    glob_scores = low_back(jnp.einsum('ghd,khd->hgk', glob_query, keys, precision=highest) * scale)
    glob_mask = (positions[None, :] <= glob_pos[:, None])[None]
    glob_prob = masked_softmax(glob_scores, glob_mask)
    glob_out = jnp.einsum('hgk,khd->ghd', low(glob_prob), values, precision=highest)
    return near.at[glob_pos].set(glob_out)

def layer(x, glob_pos, attn_gain, attn_shift, mlp_gain, mlp_shift, qkv_weight, qkv_bias, proj_weight, proj_bias, up_weight, up_bias, down_weight, down_bias):
    highest = lax.Precision.HIGHEST
    length = x.shape[0]
    positions = jnp.arange(length, dtype=jnp.int32)
    in_attn = low(layer_norm_forward(x, attn_gain, attn_shift))
    in_mlp = low(layer_norm_forward(x, mlp_gain, mlp_shift))
    linear = low_back(jnp.dot(in_attn, qkv_weight, precision=highest) + qkv_bias)
    parts = linear.reshape(length, 3, H, HD)
    cosine, sine = rotary_tables(positions, ROT)
    query = low(rotate(parts[:, 0], cosine, sine, 1.0))
    keys = low(rotate(parts[:, 1], cosine, sine, 1.0))
    values = low(parts[:, 2])
    mixed = attend(query, keys, values, glob_pos).reshape(length, D)
    mixed = low_back(low(mixed))
    attn_part = jnp.dot(mixed, proj_weight, precision=highest) + proj_bias
    upper = low_back(jnp.dot(in_mlp, up_weight, precision=highest) + up_bias)
    active = low(jax.nn.gelu(upper, approximate=False))
    mlp_part = jnp.dot(active, down_weight, precision=highest) + down_bias
    return x + attn_part + mlp_part

def reference(tokens, cotangent, global_pos, attn_gain, attn_shift, mlp_gain, mlp_shift, qkv_weight, qkv_bias, proj_weight, proj_bias, up_weight, up_bias, down_weight, down_bias):
    params = tuple((p.astype(jnp.float32) for p in (attn_gain, attn_shift, mlp_gain, mlp_shift, qkv_weight, qkv_bias, proj_weight, proj_bias, up_weight, up_bias, down_weight, down_bias)))

    def one_sequence(carry, item):
        seq_tokens, seq_grad, seq_pos = item

        def forward(values, *weights):
            return layer(values, seq_pos, *weights)
        result, pullback = jax.vjp(forward, seq_tokens.astype(jnp.float32), *params)
        grads = pullback(seq_grad.astype(jnp.float32))
        summed = tuple((c + g for c, g in zip(carry, grads[1:])))
        return (summed, (result.astype(jnp.bfloat16), grads[0]))
    start = tuple((jnp.zeros_like(p) for p in params))
    sums, outputs = lax.scan(one_sequence, start, (tokens, cotangent, global_pos))
    return (outputs[0], outputs[1], sums[0], sums[1], sums[2], sums[3], sums[4], sums[5], sums[6], sums[7], sums[8], sums[9], sums[10], sums[11])
```

```python
import functools
import math

import jax
import jax.numpy as jnp
from jax import lax
from jax.experimental import pallas as pl
from jax.experimental.pallas import tpu as pltpu
from jax.sharding import PartitionSpec as P

D = 1024
H = 16
HD = 64
ROT = 16
WIN = 512
FF = 4096
HALF = D // 2
PAIR = 2 * HD
ROW = 512
TILE = 128

epsilon = 1e-05
negative = -1e30
rotary_base = 10000.0
f32 = jnp.float32
bf16 = jnp.bfloat16
VMEM = 50 * 2**20


def shape(dims, dtype):
    return jax.ShapeDtypeStruct(dims, dtype)


def params():
    return pltpu.CompilerParams(vmem_limit_bytes=VMEM)


def cost(flops, moved):
    return pl.CostEstimate(flops=int(flops), bytes_accessed=int(moved), transcendentals=0)


def dot(left, right):
    return jnp.dot(left, right, preferred_element_type=f32)


def dot_nt(left, right):
    return lax.dot_general(left, right, (((1,), (1,)), ((), ())), preferred_element_type=f32)


def pair(block):
    return lax.ppermute(block, "fsdp", [(0, 1), (1, 0)])


def exchange(block, axis, distance):
    return lax.ppermute(block, axis, [(i, i ^ distance) for i in range(lax.axis_size(axis))])


def shifted(block, distance):
    devices = range(lax.axis_size("ctx"))
    return lax.ppermute(
        block, "ctx", [(i - distance, i) for i in devices if i - distance in devices]
    )


def doubling(axis):
    distance, out = 1, []
    while distance < lax.axis_size(axis):
        out.append(distance)
        distance *= 2
    return out


def first_axis(kind):
    distance = 1 if kind == "xy" else 2
    return lambda block: exchange(block, "seq", distance)


def second_axis(kind):
    distance = 2 if kind == "xy" else 1
    return lambda block: exchange(block, "seq", distance)


def added(*parts):
    total = parts[0].astype(f32)
    for part in parts[1:]:
        total = total + part.astype(f32)
    return total.astype(bf16)


def reduced(send, keep, kind):
    first, second = first_axis(kind), second_axis(kind)
    recv = first(send)
    other = second(added(keep[0], recv[0]))
    return added(keep[1], recv[1], other)


def swapped(tile):
    return [tile[:TILE], pair(tile[:TILE])] if False else [tile[TILE:], pair(tile[:TILE])]


def spread(piece, kind):
    first, second = first_axis(kind), second_axis(kind)
    beside = second(piece)
    return piece, beside, first(piece), first(beside)


def norm_parts(x):
    center = x - jnp.mean(x, axis=-1, keepdims=True)
    inverse = lax.rsqrt(jnp.mean(center * center, axis=-1, keepdims=True) + epsilon)
    return center * inverse, inverse


def norm_body(x_ref, gain_ref, shift_ref, a_ref, at_ref):
    normal, _ = norm_parts(x_ref[...].astype(f32))
    a = (normal * gain_ref[...] + shift_ref[...]).astype(bf16)
    a_ref[...] = a
    at_ref[...] = a.T


def norm_call(x, gain, shift):
    rows, step = x.shape[0], 256
    vector = pl.BlockSpec((1, D), lambda i: (0, 0))
    return pl.pallas_call(
        norm_body,
        grid=(rows // step,),
        in_specs=[pl.BlockSpec((step, D), lambda i: (i, 0)), vector, vector],
        out_specs=[
            pl.BlockSpec((step, D), lambda i: (i, 0)),
            pl.BlockSpec((D, step), lambda i: (0, i)),
        ],
        out_shape=[shape((rows, D), bf16), shape((D, rows), bf16)],
        compiler_params=params(),
        cost_estimate=cost(rows * D * 10, rows * D * 6),
        name="norm",
    )(x, gain, shift)


def unit_body(
    n_alias,
    idx,
    a_ref,
    at_ref,
    dy_ref,
    wu_ref,
    wd_ref,
    bu_ref,
    *rest,
):
    send_ref, keep_ref, act_ref, dup_ref, bias_ref = rest[n_alias:]
    core, one, two = idx[0], idx[1], idx[2]
    step = pl.program_id(0)
    sub = one ^ (1 - step)
    rows = a_ref.shape[0]
    chunk = 256
    bias_ref[...] = jnp.zeros_like(bias_ref)

    def tokens(i, carry):
        at = pl.ds(pl.multiple_of(i * chunk, chunk), chunk)
        up = dot(a_ref[at, :], wu_ref[...]) + bu_ref[...]
        grad = dot_nt(dy_ref[at, :], wd_ref[...])
        cdf = 0.5 * (1.0 + lax.erf(up * (0.5**0.5)))
        density = jnp.exp(-0.5 * up * up) * (1.0 / math.sqrt(2.0 * math.pi))
        act_ref[at, :] = (up * cdf).astype(bf16)
        dup = (grad * (cdf + up * density)).astype(bf16)
        dup_ref[at, :] = dup
        bias_ref[...] += jnp.sum(dup.astype(f32), axis=0, keepdims=True)
        return carry

    lax.fori_loop(0, rows // chunk, tokens, 0)
    down = dot(act_ref[...].T, dy_ref[...]).astype(bf16)

    def put_down(ref):
        for r in range(2):
            ref[jnp.where(two == r, 1, 0), 1, :, :] = down[:, r * HALF : (r + 1) * HALF]

    @pl.when(step == 0)
    def _():
        put_down(send_ref)

    @pl.when(step == 1)
    def _():
        put_down(keep_ref)

    lanes = pl.ds(pl.multiple_of(sub * chunk, chunk), chunk)
    for ref, p in ((send_ref, 1 - one), (keep_ref, one)):
        for m in range(2):
            left = at_ref[m, p].reshape(2 * TILE, rows)
            up_grad = dot(left, dup_ref[...]).astype(bf16)
            for r in range(2):
                at = pl.ds(pl.multiple_of(jnp.where(core == m, TILE, 0), TILE), TILE)
                ref[jnp.where(two == r, 1, 0), 0, at, lanes] = up_grad[
                    r * TILE : (r + 1) * TILE
                ]


def unit_call(idx, f, a, at, dy, w_up, w_down, b_up, act_all, dup_all):
    rows = a.shape[0]
    sub = lambda s, idx: 2 * f + (idx[1] ^ (1 - s))
    whole = lambda s, idx: (0, 0)
    column = pl.BlockSpec((rows, 256), lambda s, idx: (0, sub(s, idx)))
    grads = pl.BlockSpec((2, 2, 256, 512), lambda s, idx: (0, 0, 0, 0))
    alias = [] if act_all is None else [act_all, dup_all]
    return pl.pallas_call(
        functools.partial(unit_body, len(alias)),
        grid_spec=pltpu.PrefetchScalarGridSpec(
            num_scalar_prefetch=1,
            grid=(2,),
            in_specs=[
                pl.BlockSpec((rows, D), whole),
                pl.BlockSpec((2, 2, 2, TILE, rows), lambda s, idx: (0, 0, 0, 0, 0)),
                pl.BlockSpec((rows, D), whole),
                pl.BlockSpec((D, 256), lambda s, idx: (0, sub(s, idx))),
                pl.BlockSpec((256, D), lambda s, idx: (sub(s, idx), 0)),
                pl.BlockSpec((1, 256), lambda s, idx: (0, sub(s, idx))),
            ]
            + [pl.BlockSpec(memory_space=pl.ANY)] * len(alias),
            out_specs=[
                grads,
                grads,
                column,
                column,
                pl.BlockSpec((1, 256), lambda s, idx: (0, idx[1] ^ (1 - s))),
            ],
        ),
        out_shape=[
            shape((2, 2, 256, 512), bf16),
            shape((2, 2, 256, 512), bf16),
            shape((rows, FF // 2), bf16),
            shape((rows, FF // 2), bf16),
            shape((1, 512), f32),
        ],
        input_output_aliases={7: 2, 8: 3} if alias else {},
        compiler_params=params(),
        cost_estimate=cost(8 * rows * D * 512, 14 * 2**20),
        name="feed_forward",
    )(idx, a, at.reshape(2, 2, 2, TILE, rows), dy, w_up, w_down, b_up, *alias)


def rotated(field, cosine, sine, direction):
    lane = lax.broadcasted_iota(jnp.int32, field.shape, 1) % HD
    partner = jnp.where(
        lane < ROT // 2,
        pltpu.roll(field, PAIR - ROT // 2, 1),
        pltpu.roll(field, ROT // 2, 1),
    )
    return field * cosine + (direction * sine) * partner


def qkv_body(x_ref, gain_ref, shift_ref, w_ref, b_ref, cos_ref, sin_ref, *outs):
    a_ref, at_ref, q_ref, k_ref, v_ref = outs
    normal, _ = norm_parts(x_ref[...].astype(f32))
    a = (normal * gain_ref[...] + shift_ref[...]).astype(bf16)
    a_ref[...] = a
    at_ref[...] = a.T
    cosine, sine = cos_ref[...], sin_ref[...]
    for t, ref in enumerate((q_ref, k_ref, v_ref)):
        part = slice(t * HALF, (t + 1) * HALF)
        lin = dot(a, w_ref[:, part]) + b_ref[:, part]
        if t == 2:
            ref[...] = lin.astype(bf16)
            continue
        for j in range(HALF // PAIR):
            lanes = slice(j * PAIR, (j + 1) * PAIR)
            ref[:, lanes] = rotated(lin[:, lanes], cosine, sine, 1.0).astype(bf16)


def qkv_call(x, gain, shift, w, b, cosine, sine, step):
    rows = x.shape[0]
    tables = cosine.shape[0] // step
    vector = pl.BlockSpec((1, D), lambda i: (0, 0))
    table = pl.BlockSpec((step, PAIR), lambda i: (i % tables, 0))
    third = pl.BlockSpec((step, HALF), lambda i: (i, 0))
    return pl.pallas_call(
        qkv_body,
        grid=(rows // step,),
        in_specs=[
            pl.BlockSpec((step, D), lambda i: (i, 0)),
            vector,
            vector,
            pl.BlockSpec((D, 3 * HALF), lambda i: (0, 0)),
            pl.BlockSpec((1, 3 * HALF), lambda i: (0, 0)),
            table,
            table,
        ],
        out_specs=[
            pl.BlockSpec((step, D), lambda i: (i, 0)),
            pl.BlockSpec((D, step), lambda i: (0, i)),
            third,
            third,
            third,
        ],
        out_shape=[shape((rows, D), bf16), shape((D, rows), bf16)]
        + [shape((rows, HALF), bf16)] * 3,
        compiler_params=params(),
        cost_estimate=cost(2 * rows * D * 3 * HALF, rows * D * 9 + 3 * 2**20),
        name="qkv",
    )(x, gain, shift, w, b, cosine, sine)


def heads_beside(block_t):
    dim = lax.broadcasted_iota(jnp.int32, block_t.shape, 0)
    zero = jnp.zeros_like(block_t)
    return jnp.concatenate(
        [jnp.where(dim < HD, block_t, zero), jnp.where(dim < HD, zero, block_t)], axis=1
    )


def heads_below(block):
    dim = lax.broadcasted_iota(jnp.int32, block.shape, 1)
    zero = jnp.zeros_like(block)
    return jnp.concatenate(
        [jnp.where(dim < HD, block, zero), jnp.where(dim < HD, zero, block)], axis=0
    )


def heads_back(both):
    n = both.shape[1] // 2
    dim = lax.broadcasted_iota(jnp.int32, (PAIR, n), 0)
    return jnp.where(dim < HD, both[:, :n], both[:, n:])


def near_body(
    info,
    q_ref,
    k_ref,
    v_ref,
    dol_ref,
    kp_ref,
    vp_ref,
    kg_ref,
    vg_ref,
    glob_ref,
    cos_ref,
    sin_ref,
    cosp_ref,
    sinp_ref,
    cosg_ref,
    sing_ref,
    o_ref,
    dq_ref,
    dk_ref,
    dv_ref,
    dkp_ref,
    dvp_ref,
    dkg_ref,
    dvg_ref,
    dk_acc,
    dv_acc,
):
    scale = HD**-0.5
    base = info[0]
    absent = jnp.where(base == 0, f32(negative), f32(0.0))
    keys = jnp.concatenate([kp_ref[...], k_ref[...]], axis=0)
    values = jnp.concatenate([vp_ref[...], v_ref[...]], axis=0)
    keys_t = keys.T
    values_t = values.T
    gkeys, gvalues = kg_ref[...], vg_ref[...]
    glob_n = gkeys.shape[0]
    gkeys_t = gkeys.astype(f32).T.astype(bf16)
    gvalues_t = gvalues.astype(f32).T.astype(bf16)
    query = (q_ref[...].astype(f32) * scale).astype(bf16)
    query_t = query.T
    dol = dol_ref[...]
    dol_t = dol.T
    dk_acc[...] = jnp.zeros_like(dk_acc)
    dv_acc[...] = jnp.zeros_like(dv_acc)
    two = 2 * TILE
    window = WIN + TILE
    cosine, sine = cos_ref[...], sin_ref[...]
    row = lax.broadcasted_iota(jnp.int32, (TILE, two), 0)
    lane = lax.broadcasted_iota(jnp.int32, (TILE, two), 1) % TILE
    glane = lax.broadcasted_iota(jnp.int32, (glob_n, two), 1) % TILE
    gpos = jnp.concatenate([glob_ref[0], glob_ref[0]], axis=1)
    dkg = jnp.zeros((glob_n, PAIR), f32)
    dvg = jnp.zeros((glob_n, PAIR), f32)
    for t in range(ROW // TILE):
        rows = slice(t * TILE, (t + 1) * TILE)
        span = slice(t * TILE, t * TILE + window)
        cut = WIN - t * TILE
        q_beside = heads_beside(query_t[:, rows])
        d_beside = heads_beside(dol_t[:, rows])
        q_below = heads_below(query[rows])
        d_below = heads_below(dol[rows])
        score = dot(keys[span], q_beside)
        far = dot(gkeys, q_beside)
        parts = [
            jnp.where(row > lane, score[:TILE] + absent, negative),
        ]
        if cut > TILE:
            parts.append(score[TILE:cut] + absent)
        parts.append(score[cut:WIN])
        if t == 0:
            parts.pop()
        parts.append(jnp.where(row <= lane, score[WIN:], negative))
        score = jnp.concatenate(parts, axis=0)
        far = jnp.where(base + t * TILE + glane - gpos >= WIN, far, negative)
        top = jnp.maximum(
            jnp.max(score, axis=0, keepdims=True), jnp.max(far, axis=0, keepdims=True)
        )
        prob = jnp.exp(score - top)
        far_prob = jnp.exp(far - top)
        total = jnp.sum(prob, axis=0, keepdims=True) + jnp.sum(far_prob, axis=0, keepdims=True)
        inverse = 1.0 / total
        prob = prob * inverse
        far_prob = far_prob * inverse
        low, far_low = prob.astype(bf16), far_prob.astype(bf16)
        out_t = dot(values_t[:, span], low) + dot(gvalues_t, far_low)
        o_ref[rows, :] = heads_back(out_t).T.astype(bf16)
        d_prob = dot(values[span], d_beside)
        d_far = dot(gvalues, d_beside)
        delta = jnp.sum(prob * d_prob, axis=0, keepdims=True) + jnp.sum(
            far_prob * d_far, axis=0, keepdims=True
        )
        d_score = (prob * (d_prob - delta)).astype(bf16)
        d_far = (far_prob * (d_far - delta)).astype(bf16)
        dq_t = dot(keys_t[:, span], d_score) + dot(gkeys_t, d_far)
        dq = heads_back(dq_t).T * scale
        dq_ref[rows, :] = rotated(dq, cosine[rows], sine[rows], -1.0).astype(bf16)
        dk_acc[span, :] += dot(d_score, q_below)
        dv_acc[span, :] += dot(low, d_below)
        dkg = dkg + dot(d_far, q_below)
        dvg = dvg + dot(far_low, d_below)
    dk_ref[...] = dk_acc[ROW:, :]
    dv_ref[...] = dv_acc[ROW:, :]
    dkp_ref[...] = rotated(dk_acc[:ROW, :], cosp_ref[...], sinp_ref[...], -1.0).astype(bf16)
    dvp_ref[...] = dv_acc[:ROW, :].astype(bf16)
    dkg_ref[...] = rotated(dkg, cosg_ref[...], sing_ref[...], -1.0).astype(bf16)
    dvg_ref[...] = dvg.astype(bf16)


def near_call(info, q, k, v, dol, k2, v2, glob_wide, tables, tables2):
    glob_n = glob_wide.shape[1]
    own = pl.BlockSpec((ROW, PAIR), lambda j, h, info: (j, h))
    first = 2 * ROW // glob_n
    glob = pl.BlockSpec((glob_n, PAIR), lambda j, h, info: (first + j, h))
    glob_out = pl.BlockSpec((glob_n, PAIR), lambda j, h, info: (j, h))
    table = pl.BlockSpec((ROW, PAIR), lambda j, h, info: (0, 0))
    gtable = pl.BlockSpec((glob_n, PAIR), lambda j, h, info: (first + j, 0))
    rows = q.shape[0]
    own_low, own_high = shape((rows, HALF), bf16), shape((rows, HALF), f32)
    glob_low = shape((2 * glob_n, HALF), bf16)
    return pl.pallas_call(
        near_body,
        grid_spec=pltpu.PrefetchScalarGridSpec(
            num_scalar_prefetch=1,
            grid=(2, HALF // PAIR),
            in_specs=[own] * 6
            + [glob] * 2
            + [pl.BlockSpec((1, glob_n, PAIR), lambda j, h, info: (j, 0, 0))]
            + [table] * 4
            + [gtable] * 2,
            out_specs=[own] * 6 + [glob_out] * 2,
            scratch_shapes=[pltpu.VMEM((2 * ROW, PAIR), f32)] * 2,
        ),
        out_shape=[own_low, own_low, own_high, own_high, own_low, own_low, glob_low, glob_low],
        compiler_params=params(),
        cost_estimate=cost(8 * 4 * 6 * 2 * 704 * 256 * 256, 16 * 2**20),
        name="near",
    )(
        info,
        q,
        k,
        v,
        dol,
        k2,
        v2,
        k2,
        v2,
        glob_wide,
        tables[0],
        tables[1],
        tables2[0],
        tables2[1],
        tables2[0],
        tables2[1],
    )


def glob_first_body(info, qg_ref, k_ref, v_ref, glob_ref, out_ref):
    glob_n = qg_ref.shape[0]
    query = qg_ref[...].astype(f32) * HD**-0.5
    beside = heads_beside(query.T).astype(bf16)
    score = dot(k_ref[...], beside)
    key_pos = info[0] + lax.broadcasted_iota(jnp.int32, score.shape, 0)
    mask = key_pos <= glob_ref[0][0:1]
    masked = jnp.where(mask, score, negative)
    top = jnp.max(masked, axis=0, keepdims=True)
    prob = jnp.where(mask, jnp.exp(masked - top), 0.0)
    total = jnp.sum(prob, axis=0, keepdims=True)
    both = dot(v_ref[...].T, prob.astype(bf16))
    lane = lax.broadcasted_iota(jnp.int32, (HD, 2 * glob_n), 1)
    out_ref[0, 0:HD, :] = jnp.where(lane < glob_n, both[:HD], both[HD:])
    out_ref[0, HD : HD + 1, :] = top
    out_ref[0, HD + 1 : HD + 2, :] = total
    out_ref[0, HD + 2 : HD + 8, :] = jnp.zeros((6, 2 * glob_n), f32)


def glob_first_call(info, q2, k, v, glob_row):
    glob_n = glob_row.shape[2] // 2
    first = 2 * ROW // glob_n
    own = pl.BlockSpec((ROW, PAIR), lambda j, h, info: (j, h))
    pairs = HALF // PAIR
    return pl.pallas_call(
        glob_first_body,
        grid_spec=pltpu.PrefetchScalarGridSpec(
            num_scalar_prefetch=1,
            grid=(2, pairs),
            in_specs=[
                pl.BlockSpec((glob_n, PAIR), lambda j, h, info: (first + j, h)),
                own,
                own,
                pl.BlockSpec((1, 8, 2 * glob_n), lambda j, h, info: (j, 0, 0)),
            ],
            out_specs=pl.BlockSpec(
                (1, HD + 8, 2 * glob_n), lambda j, h, info: (j * pairs + h, 0, 0)
            ),
        ),
        out_shape=shape((2 * pairs, HD + 8, 2 * glob_n), f32),
        compiler_params=params(),
        cost_estimate=cost(8 * 2 * 2 * 512 * 128 * 256, 3 * 2**20),
        name="glob_first",
    )(info, q2, k, v, glob_row)


def merged(first, second):
    top_a, top_b = first[:, HD : HD + 1], second[:, HD : HD + 1]
    top = jnp.maximum(top_a, top_b)
    weight_a, weight_b = jnp.exp(top_a - top), jnp.exp(top_b - top)
    total = first[:, HD + 1 : HD + 2] * weight_a + second[:, HD + 1 : HD + 2] * weight_b
    out = first[:, :HD] * weight_a + second[:, :HD] * weight_b
    return jnp.concatenate([out, top, total, first[:, HD + 2 :]], axis=1)


def glob_second_body(
    info,
    qg_ref,
    dolg_ref,
    k_ref,
    v_ref,
    stat_ref,
    glob_ref,
    near_ref,
    dk_in,
    dv_in,
    cos_ref,
    sin_ref,
    cosg_ref,
    sing_ref,
    o_ref,
    ot_ref,
    dk_ref,
    dv_ref,
    dqg_ref,
):
    scale = HD**-0.5
    glob_n = qg_ref.shape[0]
    keys, values = k_ref[...], v_ref[...]
    query = qg_ref[...].astype(f32) * scale
    q_beside = heads_beside(query.T).astype(bf16)
    q_below = heads_below(query.astype(bf16))
    dol = dolg_ref[...]
    dol_t = dol.astype(f32).T
    d_beside = heads_beside(dol_t).astype(bf16)
    d_below = heads_below(dol)
    out_t = stat_ref[0, 0:HD, :]
    top = stat_ref[0, HD : HD + 1, :]
    total = stat_ref[0, HD + 1 : HD + 2, :]
    out_t = out_t * (1.0 / total)
    lse = top + jnp.log(total)
    delta = jnp.sum(
        out_t * jnp.concatenate([dol_t[:HD], dol_t[HD:]], axis=1), axis=0, keepdims=True
    )
    score = dot(keys, q_beside)
    key_pos = info[0] + lax.broadcasted_iota(jnp.int32, score.shape, 0)
    positions = glob_ref[0][0:1]
    mask = key_pos <= positions
    prob = jnp.where(mask, jnp.exp(jnp.where(mask, score, negative) - lse), 0.0)
    d_prob = dot(values, d_beside)
    d_score = (prob * (d_prob - delta)).astype(bf16)
    low = prob.astype(bf16)
    dk = dk_in[...] + dot(d_score, q_below)
    dv = dv_in[...] + dot(low, d_below)
    dk_ref[...] = rotated(dk, cos_ref[...], sin_ref[...], -1.0).astype(bf16)
    dv_ref[...] = dv.astype(bf16)
    dq_both = dot(keys.T, d_score)
    dq_t = jnp.concatenate([dq_both[:HD, :glob_n], dq_both[HD:, glob_n:]], axis=0)
    dqg_ref[...] = rotated(dq_t.T * scale, cosg_ref[...], sing_ref[...], -1.0).astype(bf16)
    rows = jnp.concatenate([out_t[:, :glob_n], out_t[:, glob_n:]], axis=0).T.astype(bf16)
    place = (key_pos[:, :glob_n] == positions[:, :glob_n]).astype(f32)
    hit = jnp.sum(place, axis=1, keepdims=True) > 0.0
    out = jnp.where(hit, dot(place.astype(bf16), rows).astype(bf16), near_ref[...])
    o_ref[...] = out
    ot_ref[...] = out.T


def glob_second_call(info, q2, dolg, k, v, stats, glob_row, near, dk, dv, tables, tables2):
    glob_n = glob_row.shape[2] // 2
    first = 2 * ROW // glob_n
    pairs = HALF // PAIR
    rows = k.shape[0]
    own = pl.BlockSpec((ROW, PAIR), lambda j, h, info: (j, h))
    glob = pl.BlockSpec((glob_n, PAIR), lambda j, h, info: (j, h))
    gtable = pl.BlockSpec((glob_n, PAIR), lambda j, h, info: (first + j, 0))
    table = pl.BlockSpec((ROW, PAIR), lambda j, h, info: (0, 0))
    return pl.pallas_call(
        glob_second_body,
        grid_spec=pltpu.PrefetchScalarGridSpec(
            num_scalar_prefetch=1,
            grid=(2, pairs),
            in_specs=[
                pl.BlockSpec((glob_n, PAIR), lambda j, h, info: (first + j, h)),
                glob,
                own,
                own,
                pl.BlockSpec((1, HD + 8, 2 * glob_n), lambda j, h, info: (j * pairs + h, 0, 0)),
                pl.BlockSpec((1, 8, 2 * glob_n), lambda j, h, info: (j, 0, 0)),
                own,
                own,
                own,
                table,
                table,
                gtable,
                gtable,
            ],
            out_specs=[
                own,
                pl.BlockSpec((PAIR, ROW), lambda j, h, info: (h, j)),
                own,
                own,
                glob,
            ],
        ),
        out_shape=[
            shape((rows, HALF), bf16),
            shape((HALF, rows), bf16),
            shape((rows, HALF), bf16),
            shape((rows, HALF), bf16),
            shape((2 * glob_n, HALF), bf16),
        ],
        compiler_params=params(),
        cost_estimate=cost(8 * 5 * 2 * 512 * 128 * 256, 10 * 2**20),
        name="glob_second",
    )(
        info,
        q2,
        dolg,
        k,
        v,
        stats,
        glob_row,
        near,
        dk,
        dv,
        tables[0],
        tables[1],
        tables2[0],
        tables2[1],
    )


def split_rows(idx, step, ref, wide, tile, core, two):
    for m in range(2):
        at = pl.ds(pl.multiple_of(jnp.where(core == m, TILE, 0), TILE), TILE)
        for r in range(2):
            begin = (2 * m + r) * TILE
            ref[jnp.where(two == r, 1, 0), tile, at, :] = wide[begin : begin + TILE]


def weights_body(sources, idx, *refs):
    core, two = idx[0], idx[2]
    step = pl.program_id(0)
    send_ref, keep_ref = refs[-2:]

    def run(ref):
        at = 0
        for tile, (kind, count) in enumerate(sources):
            total = None
            for _ in range(count):
                left = refs[at][...]
                if kind == "spread":
                    left = left.reshape(4 * TILE, left.shape[-1])
                term = dot(left, refs[at + 1][...])
                total = term if total is None else total + term
                at += 2
            total = total.astype(bf16)
            if kind == "spread":
                split_rows(idx, step, ref, total, tile, core, two)
            else:
                for r in range(2):
                    ref[jnp.where(two == r, 1, 0), tile, :, :] = total[
                        :, r * HALF : (r + 1) * HALF
                    ]

    @pl.when(step == 0)
    def _():
        run(send_ref)

    @pl.when(step == 1)
    def _():
        run(keep_ref)


def weights_call(idx, tiles):
    part = lambda s, idx: idx[1] ^ (1 - s)
    operands, specs, sources, flops = [], [], [], 0
    for kind, products in tiles:
        sources.append((kind, len(products)))
        for left, right in products:
            n = left.shape[1]
            if kind == "spread":
                left = left.reshape(2, 2, 2, TILE, n)
                specs.append(
                    pl.BlockSpec(
                        (2, 1, 2, TILE, n), lambda s, idx: (0, part(s, idx), 0, 0, 0)
                    )
                )
            else:
                specs.append(pl.BlockSpec((256, n), lambda s, idx: (part(s, idx), 0)))
            specs.append(pl.BlockSpec(right.shape, lambda s, idx: (0, 0)))
            operands += [left, right]
            flops += 2 * n * 512 * 1024
    out = pl.BlockSpec((2, 2, 256, 512), lambda s, idx: (0, 0, 0, 0))
    return pl.pallas_call(
        functools.partial(weights_body, tuple(sources)),
        grid_spec=pltpu.PrefetchScalarGridSpec(
            num_scalar_prefetch=1, grid=(2,), in_specs=specs, out_specs=[out, out]
        ),
        out_shape=[shape((2, 2, 256, 512), bf16)] * 2,
        compiler_params=params(),
        cost_estimate=cost(flops, 10 * 2**20),
        name="weight_grads",
    )(idx, *operands)


def input_body(thirds, with_more, *refs):
    refs = list(refs)
    x_ref, gain_ref, w_ref = refs[:3]
    parts = refs[3 : 3 + thirds]
    at = 3 + thirds
    more_ref = refs[at] if with_more else None
    g_ref, sums_ref, bias_ref = refs[-3:]

    @pl.when(pl.program_id(0) == 0)
    def _():
        sums_ref[...] = jnp.zeros_like(sums_ref)
        bias_ref[...] = jnp.zeros_like(bias_ref)

    grad = None
    width = parts[0].shape[1]
    first = 3 - thirds if thirds < 3 and width == HALF else 0
    for i, ref in enumerate(parts):
        part = ref[...]
        lanes = slice((first + i) * width, (first + i + 1) * width)
        term = dot_nt(part, w_ref[:, lanes])
        grad = term if grad is None else grad + term
        bias_ref[0:1, lanes] += jnp.sum(part.astype(f32), axis=0, keepdims=True)
    normal, _ = norm_parts(x_ref[...].astype(f32))
    sums_ref[0:1, :] += jnp.sum(grad * normal, axis=0, keepdims=True)
    sums_ref[1:2, :] += jnp.sum(grad, axis=0, keepdims=True)
    g = grad * gain_ref[...]
    if with_more:
        g = g + more_ref[...].astype(f32)
    g_ref[...] = g.astype(g_ref.dtype)


def input_call(x, at_block, rows, step, gain, w, parts, more, kind):
    width = parts[0].shape[1]
    vector = pl.BlockSpec((1, D), lambda i: (0, 0))
    specs = [
        pl.BlockSpec((step, D), lambda i: (at_block + i, 0)),
        vector,
        pl.BlockSpec(w.shape, lambda i: (0, 0)),
    ] + [pl.BlockSpec((step, width), lambda i: (i, 0))] * len(parts)
    operands = [x, gain, w, *parts]
    if more is not None:
        specs.append(pl.BlockSpec((step, D), lambda i: (i, 0)))
        operands.append(more)
    return pl.pallas_call(
        functools.partial(input_body, len(parts), more is not None),
        grid=(rows // step,),
        in_specs=specs,
        out_specs=[
            pl.BlockSpec((step, D), lambda i: (i, 0)),
            pl.BlockSpec((8, D), lambda i: (0, 0)),
            pl.BlockSpec((8, w.shape[1]), lambda i: (0, 0)),
        ],
        out_shape=[
            shape((rows, D), kind),
            shape((8, D), f32),
            shape((8, w.shape[1]), f32),
        ],
        compiler_params=params(),
        cost_estimate=cost(2 * rows * D * width * len(parts), rows * D * 8 + 4 * 2**20),
        name="input_grads",
    )(*operands)


def place_body(kinds, n_alias, idx, *refs):
    pieces = refs[:4]
    outs = refs[4 + n_alias :]
    half = pl.program_id(1)

    for g in range(4):

        @pl.when(pl.program_id(0) == g)
        def _(g=g):
            for tile, out in enumerate(outs):
                at = pl.ds(pl.multiple_of(tile * 256 + half * TILE, TILE), TILE)
                out[...] = pieces[g][at, :].astype(f32)


def place_call(idx, pieces, targets):
    def mapped(where):
        def index(g, h, idx):
            return where(idx[1] ^ (g // 2), idx[2] ^ (g % 2), h, idx[0])

        return index

    alias = [buf for buf, _, _ in targets if buf is not None]
    aliases, at = {}, 5
    for out, (buf, _, _) in enumerate(targets):
        if buf is not None:
            aliases[at] = out
            at += 1
    whole = pl.BlockSpec((512, 512), lambda g, h, idx: (0, 0))
    return pl.pallas_call(
        functools.partial(place_body, None, len(alias)),
        grid_spec=pltpu.PrefetchScalarGridSpec(
            num_scalar_prefetch=1,
            grid=(4, 2),
            in_specs=[whole] * 4 + [pl.BlockSpec(memory_space=pl.ANY)] * len(alias),
            out_specs=[pl.BlockSpec((TILE, 512), mapped(where)) for _, _, where in targets],
        ),
        out_shape=[shape(dims, f32) for _, dims, _ in targets],
        input_output_aliases=aliases,
        compiler_params=params(),
        cost_estimate=cost(0, 6 * 2**20),
        name="place",
    )(idx, *pieces, *alias)


def rotary_tables(positions):
    lane = jnp.arange(PAIR, dtype=jnp.int32) % HD
    half = ROT // 2
    freqs = rotary_base ** (-2.0 * (lane % half).astype(f32) / ROT)
    angles = positions.astype(f32)[:, None] * freqs[None, :]
    active = (lane < ROT)[None, :]
    sign = jnp.where(lane < half, -1.0, 1.0)[None, :]
    return jnp.where(active, jnp.cos(angles), 1.0), jnp.where(active, jnp.sin(angles) * sign, 0.0)


def per_device(
    tokens,
    cotangent,
    global_pos,
    attn_gain,
    attn_shift,
    mlp_gain,
    mlp_shift,
    qkv_weight,
    qkv_bias,
    proj_weight,
    proj_bias,
    up_weight,
    up_bias,
    down_weight,
    down_bias,
):
    n_ctx = lax.axis_size("ctx")
    core = lax.axis_index("fsdp")
    seq = lax.axis_index("seq")
    ctx = lax.axis_index("ctx")
    x_bit, y_bit = seq & 1, seq >> 1
    base = ctx * ROW
    own_x = tokens[0]
    own_dy = cotangent[0]
    glob_n = global_pos.shape[1]
    share = glob_n // n_ctx
    info = jnp.stack([base]).astype(jnp.int32)
    index = {
        "xy": jnp.stack([core, x_bit, y_bit]).astype(jnp.int32),
        "yx": jnp.stack([core, y_bit, x_bit]).astype(jnp.int32),
    }

    other_x = pair(own_x)
    up_halves = up_weight.reshape(HALF, 2, FF // 2)
    up_recv = pair(lax.dynamic_index_in_dim(up_halves, 1 - core, 1, False))
    other_dy = pair(own_dy)
    vectors = jnp.concatenate(
        [
            v.reshape(-1, 512)
            for v in (attn_gain, attn_shift, mlp_gain, mlp_shift, proj_bias, down_bias, qkv_bias)
        ],
        axis=0,
    )
    vectors_recv = pair(vectors)
    prev_x = shifted(own_x, 1)
    own_glob = lax.dynamic_slice_in_dim(global_pos[0], ctx * share, share, 0)
    pick = (own_glob[:, None] - base == jnp.arange(ROW, dtype=jnp.int32)[None, :]).astype(bf16)
    picked = jnp.stack([dot(pick, own_x), dot(pick, own_dy)]).astype(bf16)[None]
    qkv_halves = qkv_weight.reshape(HALF, 3, 2, HALF)
    qkv_recv = pair(lax.dynamic_index_in_dim(qkv_halves, 1 - core, 2, False))
    pos_pair = jnp.stack([global_pos[0], pair(global_pos[0])])
    other_prev = pair(prev_x)
    for distance in doubling("ctx"):
        beside = exchange(picked, "ctx", distance)
        picked = jnp.concatenate([picked, beside], axis=0)
    picked = jnp.take(picked, jnp.arange(n_ctx, dtype=jnp.int32) ^ ctx, axis=0)
    picked = jnp.transpose(picked, (1, 0, 2, 3)).reshape(2, glob_n, D)
    other_picked = pair(picked)

    low_first = core == 0

    def whole(mine, recv):
        return jnp.where(
            low_first,
            jnp.concatenate([mine, recv], axis=0),
            jnp.concatenate([recv, mine], axis=0),
        )

    both = jnp.where(
        low_first,
        jnp.stack([vectors, vectors_recv], axis=1),
        jnp.stack([vectors_recv, vectors], axis=1),
    ).astype(f32)
    gain_a, shift_a, gain_m, shift_m, bias_p, bias_d = (
        both[i].reshape(1, D) for i in range(6)
    )
    bias_qkv = jnp.swapaxes(both[6:9], 0, 1).reshape(3, 2, HALF)
    bias_qkv = lax.dynamic_index_in_dim(bias_qkv, core, 1, False).reshape(1, 3 * HALF)
    bias_up = up_bias.astype(f32).reshape(1, FF // 2)

    x = jnp.concatenate([own_x, other_x], axis=0)
    dy = jnp.concatenate([own_dy, other_dy], axis=0)
    w_up = whole(lax.dynamic_index_in_dim(up_halves, core, 1, False), up_recv)
    a_mlp, a_mlp_t = norm_call(x, gain_m, shift_m)
    kinds = ("xy", "yx", "xy", "yx", "xy", "yx")
    act = dup = None
    grads, up_sums = [], []
    for f in range(4):
        send, keep, act, dup, sums = unit_call(
            index[kinds[f]], f, a_mlp, a_mlp_t, dy, w_up, down_weight, bias_up, act, dup
        )
        grads.append((send, keep))
        up_sums.append(sums)

    tables = rotary_tables(base + jnp.arange(ROW, dtype=jnp.int32))
    before = base - ROW + jnp.arange(ROW, dtype=jnp.int32)
    tables2 = rotary_tables(jnp.concatenate([before, before, pos_pair.reshape(-1)]))
    w_qkv = whole(
        lax.dynamic_index_in_dim(qkv_halves, core, 2, False).reshape(HALF, 3 * HALF),
        qkv_recv.reshape(HALF, 3 * HALF),
    )
    a1, a1_t, q1, k1, v1 = qkv_call(x, gain_a, shift_a, w_qkv, bias_qkv, *tables, 256)
    x2 = jnp.concatenate([prev_x, other_prev, picked[0], other_picked[0]], axis=0)
    a2, a2_t, q2, k2, v2 = qkv_call(x2, gain_a, shift_a, w_qkv, bias_qkv, *tables2, 384)
    row_pos = base + jnp.arange(ROW, dtype=jnp.int32)
    is_glob = jnp.any(row_pos[None, :, None] == pos_pair[:, None, :], axis=2).reshape(2 * ROW, 1)
    dol = jnp.where(is_glob, 0.0, dot_nt(dy, proj_weight)).astype(bf16)
    dolg = dot_nt(
        jnp.concatenate([picked[1], other_picked[1]], axis=0), proj_weight
    ).astype(bf16)
    glob_row = jnp.broadcast_to(
        jnp.concatenate([pos_pair, pos_pair], axis=1)[:, None, :], (2, 8, 2 * glob_n)
    )
    glob_wide = jnp.broadcast_to(pos_pair[:, :, None], (2, glob_n, PAIR))
    stats = glob_first_call(info, q2, k1, v1, glob_row)
    for distance in doubling("ctx"):
        stats = merged(stats, exchange(stats, "ctx", distance))
    near, dq1, dk1, dv1, dkp, dvp, dkg, dvg = near_call(
        info, q1, k1, v1, dol, k2, v2, glob_wide, tables, tables2
    )
    ol, ol_t, dk1, dv1, dqg = glob_second_call(
        info, q2, dolg, k1, v1, stats, glob_row, near, dk1, dv1, tables, tables2
    )
    a2p_t, a2g_t = a2_t[:, : 2 * ROW], a2_t[:, 2 * ROW :]
    grads.append(
        weights_call(
            index[kinds[4]],
            [
                ("spread", [(a1_t, dv1), (a2p_t, dvp), (a2g_t, dvg)]),
                ("rows", [(ol_t, dy)]),
            ],
        )
    )
    grads.append(
        weights_call(
            index[kinds[5]],
            [
                ("spread", [(a1_t, dq1), (a2g_t, dqg)]),
                ("spread", [(a1_t, dk1), (a2p_t, dkp), (a2g_t, dkg)]),
            ],
        )
    )

    up_out = down_out = qkv_out = proj_out = None
    up_dims, down_dims = (HALF, FF), (FF // 2, D)
    qkv_dims, proj_dims = (HALF, 3 * D), (HALF, D)
    last = None
    for u, (send, keep) in enumerate(grads):
        kind = kinds[u]
        quarter = reduced(send, keep, kind)
        tiles = []
        for tile in range(2):
            if (tile == 0) or u == 5:
                tiles += [quarter[tile, TILE:], pair(quarter[tile, :TILE])]
            else:
                tiles.append(quarter[tile])
        piece = jnp.concatenate(tiles, axis=0)
        if last is not None:
            piece, _ = lax.optimization_barrier((piece, last))
        piece = lax.psum(piece, "ctx")
        last = piece
        pieces = spread(piece, kind)
        if u < 4:
            up_out, down_out = place_call(
                index[kind],
                pieces,
                [
                    (up_out, up_dims, lambda p, r, h, c, u=u: (p * 2 + r, (c ^ h) * 4 + u)),
                    (down_out, down_dims, lambda p, r, h, c, u=u: (u * 4 + p * 2 + h, r)),
                ],
            )
        elif u == 4:
            qkv_out, proj_out = place_call(
                index[kind],
                pieces,
                [
                    (None, qkv_dims, lambda p, r, h, c: (p * 2 + r, 4 + (c ^ h))),
                    (None, proj_dims, lambda p, r, h, c: (p * 2 + h, r)),
                ],
            )
        else:
            for t in range(2):
                rows = [jnp.concatenate([v[t * 256 : (t + 1) * 256]] * 2, axis=0) for v in pieces]
                (qkv_out,) = place_call(
                    index[kind],
                    rows,
                    [(qkv_out, qkv_dims, lambda p, r, h, c, t=t: (p * 2 + r, 2 * t + (c ^ h)))],
                )

    part = (dot(act, down_weight) + dot(ol, proj_weight)).astype(bf16)
    result = own_x.astype(f32) + part[:ROW].astype(f32) + pair(part[ROW:]).astype(f32)
    layer_out = (result + bias_p + bias_d).astype(bf16)[None]

    g_mlp, sums_m, _ = input_call(x, 0, 2 * ROW, 256, gain_m, w_up, [dup], None, f32)
    g_own, sums_1, bias_1 = input_call(
        x, 0, 2 * ROW, 256, gain_a, w_qkv, [dq1, dk1, dv1], g_mlp, bf16
    )
    g_prev, sums_2, bias_2 = input_call(x2, 0, 2 * ROW, 256, gain_a, w_qkv, [dkp, dvp], None, bf16)
    g_glob, sums_3, bias_3 = input_call(
        x2, 2 * ROW // 128, 2 * glob_n, 128, gain_a, w_qkv, [dqg, dkg, dvg], None, bf16
    )
    from_prev = shifted(added(g_prev[:ROW], pair(g_prev[ROW:])), -1)
    glob_sum = added(g_glob[:glob_n], pair(g_glob[glob_n:]))
    for distance in doubling("ctx"):
        glob_sum = added(glob_sum, exchange(glob_sum, "ctx", distance))
    place = (row_pos[:, None] == global_pos[0][None, :]).astype(bf16)
    g = (
        g_own[:ROW].astype(f32)
        + pair(g_own[ROW:]).astype(f32)
        + from_prev.astype(f32)
        + dot(place, glob_sum)
    )
    normal, inverse = norm_parts(own_x.astype(f32))
    lower = inverse * (
        g
        - jnp.mean(g, axis=-1, keepdims=True)
        - normal * jnp.mean(g * normal, axis=-1, keepdims=True)
    )
    tokens_grad = (own_dy.astype(f32) + lower)[None]

    sums_a = sums_1[:2] + sums_2[:2] + sums_3[:2]
    dy_sum = jnp.sum(own_dy.astype(f32), axis=0)
    qkv_sum = (bias_1[0] + bias_2[0] + bias_3[0]).reshape(3, 1, HALF)
    mine = jnp.arange(2, dtype=jnp.int32)[None, :, None] == core
    qkv_sum = jnp.where(mine, qkv_sum, 0.0).reshape(2, 3, 512)
    split = jnp.concatenate(
        [
            sums_a.reshape(2, 2, 512).swapaxes(0, 1),
            sums_m[:2].reshape(2, 2, 512).swapaxes(0, 1),
            dy_sum.reshape(2, 1, 512),
            qkv_sum,
        ],
        axis=1,
    )
    kept = lax.dynamic_index_in_dim(split, core, 0, False)
    given = lax.dynamic_index_in_dim(split, 1 - core, 0, False)
    total = jnp.concatenate([kept + pair(given)] + up_sums, axis=0)
    for axis in ("seq", "ctx"):
        for distance in doubling(axis):
            total = total + exchange(total, axis, distance)
    return (
        layer_out,
        tokens_grad,
        total[0],
        total[1],
        total[2],
        total[3],
        qkv_out,
        total[5:8].reshape(-1),
        proj_out,
        total[4],
        up_out,
        total[8:12].reshape(-1),
        down_out,
        total[4],
    )


def solution(mesh):
    rows = P(("seq", "fsdp"), "ctx", None)
    vector, matrix = P("fsdp"), P("fsdp", None)
    return jax.shard_map(
        per_device,
        mesh=mesh,
        in_specs=(
            rows,
            rows,
            P(("seq", "fsdp"), None),
            vector,
            vector,
            vector,
            vector,
            matrix,
            vector,
            matrix,
            vector,
            matrix,
            vector,
            matrix,
            vector,
        ),
        out_specs=(
            rows,
            rows,
            vector,
            vector,
            vector,
            vector,
            matrix,
            vector,
            matrix,
            vector,
            matrix,
            vector,
            matrix,
            vector,
        ),
        check_vma=False,
    )
```

```python
import functools
import math

import jax
import jax.numpy as jnp
from jax import lax
from jax.experimental import pallas as pl
from jax.experimental.pallas import tpu as pltpu
from jax.sharding import PartitionSpec as P

D = 1024
H = 16
HD = 64
ROT = 16
WIN = 512
FF = 4096
HALF = D // 2
PAIR = 2 * HD
ROW = 512
TILE = 128

epsilon = 1e-05
negative = -1e30
rotary_base = 10000.0
f32 = jnp.float32
bf16 = jnp.bfloat16
VMEM = 60 * 2**20
KINDS = ("xy", "yx")
COST = 1000


def shape(dims, dtype):
    return jax.ShapeDtypeStruct(dims, dtype)


def params():
    return pltpu.CompilerParams(vmem_limit_bytes=VMEM)


def cost(flops, moved):
    return pl.CostEstimate(flops=int(flops) // COST, bytes_accessed=int(moved) // COST, transcendentals=0)


def dot(left, right):
    return jnp.dot(left, right, preferred_element_type=f32)


def dot_nt(left, right):
    return lax.dot_general(left, right, (((1,), (1,)), ((), ())), preferred_element_type=f32)


def dot_tn(left, right):
    return lax.dot_general(left, right, (((0,), (0,)), ((), ())), preferred_element_type=f32)


def lanes_of(block, width):
    return pl.ds(pl.multiple_of(block * width, width), width)


def pair(block):
    return lax.ppermute(block, "fsdp", [(0, 1), (1, 0)])


def exchange(block, axis, distance):
    return lax.ppermute(block, axis, [(i, i ^ distance) for i in range(lax.axis_size(axis))])


def shifted(block, distance):
    devices = range(lax.axis_size("ctx"))
    return lax.ppermute(
        block, "ctx", [(i - distance, i) for i in devices if i - distance in devices]
    )


def doubling(axis):
    distance, out = 1, []
    while distance < lax.axis_size(axis):
        out.append(distance)
        distance *= 2
    return out


def first_axis(kind):
    distance = 1 if kind == "xy" else 2
    return lambda block: exchange(block, "seq", distance)


def second_axis(kind):
    distance = 2 if kind == "xy" else 1
    return lambda block: exchange(block, "seq", distance)


def added(*parts):
    total = parts[0].astype(f32)
    for part in parts[1:]:
        total = total + part.astype(f32)
    return total.astype(bf16)


class Order:
    def __init__(self):
        self.token = None

    def gate(self, *arrays):
        if self.token is None:
            return arrays if len(arrays) > 1 else arrays[0]
        out = lax.optimization_barrier((*arrays, self.token))[:-1]
        return out if len(out) > 1 else out[0]

    def mark(self, array):
        self.token = array
        return array


class Reduction:
    def __init__(self, order, idx, parts):
        self.order, self.idx = order, idx
        self.tiles = parts[0][0].shape[1]
        self.keeps = [keep for _, keep in parts]
        self.recv = [first_axis(kind)(send) for kind, (send, _) in zip(KINDS, parts)]

    def second(self):
        gated = self.order.gate(*self.keeps, *self.recv)
        self.keeps, self.recv = gated[:2], gated[2:]
        sums = halves_call(*self.keeps, *self.recv)
        self.order.mark(sums[0])
        self.other = [second_axis(kind)(part) for kind, part in zip(KINDS, sums)]

    def over_ctx(self):
        gated = self.order.gate(*self.keeps, *self.recv, *self.other)
        outs = quarters_call(self.idx, *gated)
        self.order.mark(outs[0])
        if len(outs) == 2:
            self.total = lax.psum(tuple(outs), "ctx")
            return
        self.own = outs[0]
        self.recv = [exchange(part, "ctx", k + 1) for k, part in enumerate(outs[1:])]

    def ctx_sum(self):
        if lax.axis_size("ctx") != 4:
            return
        self.own = self.order.mark(added(*self.order.gate(self.own, *self.recv)))
        self.recv = [exchange(self.own, "ctx", k) for k in (1, 2, 3)]

    def gather(self):
        if lax.axis_size("ctx") != 4:
            total = self.order.gate(*self.total)
        else:
            total = regroup_call(self.idx, *self.order.gate(self.own, *self.recv))
            self.order.mark(total[0])
        self.total = [part.reshape(self.tiles, 256, 512) for part in total]
        self.beside = [second_axis(k)(part) for k, part in zip(KINDS, self.total)]
        self.across = [first_axis(k)(part) for k, part in zip(KINDS, self.total)]

    def gather_rest(self):
        self.beside = self.order.gate(*self.beside)
        self.order.mark(self.beside[0])
        self.both = [first_axis(k)(beside) for k, beside in zip(KINDS, self.beside)]

    def swap(self, tiles):
        pieces = [
            [self.total[u], self.beside[u], self.across[u], self.both[u]] for u in range(2)
        ]
        flat = self.order.gate(*pieces[0], *pieces[1])
        self.pieces = [flat[:4], flat[4:]]
        given = swap_call([(self.pieces[u][k], t) for u, t in tiles for k in range(4)])
        self.swapped = pair(self.order.mark(given))


def halves_body(keep_a, keep_b, recv_a, recv_b, out_a, out_b):
    for keep, recv, out in ((keep_a, recv_a, out_a), (keep_b, recv_b, out_b)):
        out[...] = (keep[0].astype(f32) + recv[0].astype(f32)).astype(bf16)


def halves_call(keep_a, keep_b, recv_a, recv_b):
    tiles = keep_a.shape[1]
    block = pl.BlockSpec((1, 1, 256, 512), lambda t: (0, t, 0, 0))
    out = pl.BlockSpec((1, 256, 512), lambda t: (t, 0, 0))
    return pl.pallas_call(
        halves_body,
        grid=(tiles,),
        in_specs=[block] * 4,
        out_specs=[out] * 2,
        out_shape=[shape((tiles, 256, 512), bf16)] * 2,
        compiler_params=params(),
        cost_estimate=cost(10**6, 3 * 2**20),
        name="halves",
    )(keep_a, keep_b, recv_a, recv_b)


def quarters_body(idx, keep_a, keep_b, recv_a, recv_b, other_a, other_b, *outs):
    for u, refs in enumerate(((keep_a, recv_a, other_a), (keep_b, recv_b, other_b))):
        keep, recv, other = refs
        total = keep[0, 0].astype(f32) + recv[0, 0].astype(f32) + other[0].astype(f32)
        total = total.astype(bf16)
        if len(outs) == 2:
            outs[u][0] = total
            continue
        for k, out in enumerate(outs):

            @pl.when(pl.program_id(0) == k)
            def _(out=out, total=total):
                out[u] = total


def quarters_call(idx, keep_a, keep_b, recv_a, recv_b, other_a, other_b):
    split = lax.axis_size("ctx") == 4
    rows = keep_a.shape[1] * 256 // 4
    order = (lambda k, idx: idx[3] ^ k) if split else (lambda k, idx: k)
    block = pl.BlockSpec((1, 1, rows, 512), lambda k, idx: (1, order(k, idx), 0, 0))
    other = pl.BlockSpec((1, rows, 512), lambda k, idx: (order(k, idx), 0, 0))
    if split:
        out_specs = [pl.BlockSpec((2, rows, 512), lambda k, idx: (0, 0, 0))] * 4
        out_shape = [shape((2, rows, 512), bf16)] * 4
    else:
        out_specs, out_shape = [other] * 2, [shape((4, rows, 512), bf16)] * 2
    views = [v.reshape(2, 4, rows, 512) for v in (keep_a, keep_b, recv_a, recv_b)]
    views += [v.reshape(4, rows, 512) for v in (other_a, other_b)]
    return pl.pallas_call(
        quarters_body,
        grid_spec=pltpu.PrefetchScalarGridSpec(
            num_scalar_prefetch=1,
            grid=(4,),
            in_specs=[block] * 4 + [other] * 2,
            out_specs=out_specs,
        ),
        out_shape=out_shape,
        compiler_params=params(),
        cost_estimate=cost(10**6, 4 * 2**20),
        name="quarters",
    )(idx, *views)


def regroup_body(idx, *refs):
    for k in range(4):

        @pl.when(pl.program_id(0) == k)
        def _(k=k):
            for u in range(2):
                refs[4 + u][0] = refs[k][u]


def regroup_call(idx, *parts):
    rows = parts[0].shape[1]
    return pl.pallas_call(
        regroup_body,
        grid_spec=pltpu.PrefetchScalarGridSpec(
            num_scalar_prefetch=1,
            grid=(4,),
            in_specs=[pl.BlockSpec((2, rows, 512), lambda k, idx: (0, 0, 0))] * 4,
            out_specs=[pl.BlockSpec((1, rows, 512), lambda k, idx: (idx[3] ^ k, 0, 0))] * 2,
        ),
        out_shape=[shape((4, rows, 512), bf16)] * 2,
        compiler_params=params(),
        cost_estimate=cost(10**6, 2 * 2**20),
        name="regroup",
    )(idx, *parts)


def swap_body(*refs):
    for k, ref in enumerate(refs[:-1]):
        refs[-1][k] = ref[0]


def swap_call(blocks):
    return pl.pallas_call(
        swap_body,
        grid=(1,),
        in_specs=[
            pl.BlockSpec((1, TILE, 512), lambda i, t=t: (t, 0, 0)) for _, t in blocks
        ],
        out_specs=pl.BlockSpec((len(blocks), TILE, 512), lambda i: (0, 0, 0)),
        out_shape=shape((len(blocks), TILE, 512), bf16),
        compiler_params=params(),
        cost_estimate=cost(10**6, 2 * 2**20),
        name="swap",
    )(*[piece for piece, _ in blocks])


def norm_parts(x):
    center = x - jnp.mean(x, axis=-1, keepdims=True)
    inverse = lax.rsqrt(jnp.mean(center * center, axis=-1, keepdims=True) + epsilon)
    return center * inverse, inverse


def vector(ref, i):
    part = slice(i * HALF, (i + 1) * HALF)
    return jnp.concatenate([ref[0:1, part], ref[1:2, part]], axis=1)


def norm_body(x_ref, other_ref, dy_ref, dy_other_ref, vec_ref, *outs):
    a_ref, x_out, dy_out = outs

    def run(x_in, dy_in):
        block = x_in[...]
        normal, _ = norm_parts(block.astype(f32))
        a = (normal * vector(vec_ref, 2) + vector(vec_ref, 3)).astype(bf16)
        a_ref[...] = a
        x_out[...] = block
        dy_out[...] = dy_in[...]

    half = pl.num_programs(0) // 2

    @pl.when(pl.program_id(0) < half)
    def _():
        run(x_ref, dy_ref)

    @pl.when(pl.program_id(0) >= half)
    def _():
        run(other_ref, dy_other_ref)


def norm_call(x, other, dy, dy_other, vectors):
    rows, step = 2 * x.shape[0], 256
    half = x.shape[0] // step
    mine = pl.BlockSpec((step, D), lambda i: (jnp.minimum(i, half - 1), 0))
    theirs = pl.BlockSpec((step, D), lambda i: (jnp.maximum(i - half, 0), 0))
    block = pl.BlockSpec((step, D), lambda i: (i, 0))
    return pl.pallas_call(
        norm_body,
        grid=(rows // step,),
        in_specs=[mine, theirs, mine, theirs, pl.BlockSpec(vectors.shape, lambda i: (0, 0))],
        out_specs=[block] * 3,
        out_shape=[shape((rows, D), bf16)] * 3,
        compiler_params=params(),
        cost_estimate=cost(rows * D * 10, rows * D * 12),
        name="norm",
    )(x, other, dy, dy_other, vectors)


def rows_of(core):
    return pl.ds(pl.multiple_of(core * HALF, HALF), HALF)


def place_of(bit, value):
    return jnp.where(bit == value, 1, 0)


def spread_rows(ref, tile, grad, m, core, two, lanes):
    at = pl.ds(pl.multiple_of(jnp.where(core == m, TILE, 0), TILE), TILE)
    for r in range(2):
        ref[place_of(two, r), tile, at, lanes] = grad[r * TILE : (r + 1) * TILE]


def unit_body(n_alias, idx, a_ref, dy_ref, wu_mine, wu_recv, wd_ref, bu_ref, *rest):
    sends, keeps = rest[n_alias : n_alias + 4 : 2], rest[n_alias + 1 : n_alias + 4 : 2]
    act_ref, dup_ref, bias_ref, wu_ref = rest[n_alias + 4 :]
    core = idx[0]
    wu_ref[rows_of(core), :] = wu_mine[...]
    wu_ref[rows_of(1 - core), :] = wu_recv[...]
    rows = a_ref.shape[0]
    chunk = 256
    bias = jnp.zeros((1, chunk), f32)
    for i in range(rows // chunk):
        at = slice(i * chunk, (i + 1) * chunk)
        up = dot(a_ref[at, :], wu_ref[...]) + bu_ref[...]
        grad = dot_nt(dy_ref[at, :], wd_ref[...])
        cdf = 0.5 * (1.0 + lax.erf(up * (0.5**0.5)))
        density = jnp.exp(-0.5 * up * up) * (1.0 / math.sqrt(2.0 * math.pi))
        act_ref[at, :] = (up * cdf).astype(bf16)
        dup = (grad * (cdf + up * density)).astype(bf16)
        dup_ref[at, :] = dup
        bias = bias + jnp.sum(dup.astype(f32), axis=0, keepdims=True)
    bias_ref[...] = bias
    down = dot_tn(act_ref[...], dy_ref[...]).astype(bf16)

    for u in range(2):
        one, two = idx[1 + u], idx[2 - u]

        @pl.when(pl.program_id(0) // 2 == u)
        def _(u=u, one=one, two=two):
            step = pl.program_id(0) % 2
            for half, ref in ((0, sends[u]), (1, keeps[u])):

                @pl.when(step == half)
                def _(ref=ref):
                    for r in range(2):
                        ref[place_of(two, r), 1, :, :] = down[:, r * HALF : (r + 1) * HALF]

                p = one ^ (1 - half)
                for m in range(2):
                    left = a_ref[:, lanes_of(2 * m + p, chunk)]
                    grad = dot_tn(left, dup_ref[...]).astype(bf16)
                    spread_rows(ref, 0, grad, m, core, two, lanes_of(one ^ (1 - step), chunk))


def unit_call(idx, first, a, dy, up_mine, up_recv, w_down, b_up, act_all, dup_all):
    rows = a.shape[0]

    def sub(s, idx):
        u = s // 2
        return 2 * (first + u) + (idx[1 + u] ^ (1 - s % 2))

    whole = lambda s, idx: (0, 0)
    column = pl.BlockSpec((rows, 256), lambda s, idx: (0, sub(s, idx)))
    grads = pl.BlockSpec((2, 2, 256, 512), lambda s, idx: (0, 0, 0, 0))
    alias = [] if act_all is None else [act_all, dup_all]
    return pl.pallas_call(
        functools.partial(unit_body, len(alias)),
        grid_spec=pltpu.PrefetchScalarGridSpec(
            num_scalar_prefetch=1,
            grid=(4,),
            in_specs=[
                pl.BlockSpec((rows, D), whole),
                pl.BlockSpec((rows, D), whole),
                pl.BlockSpec((HALF, 256), lambda s, idx: (0, idx[0] * 8 + sub(s, idx))),
                pl.BlockSpec((HALF, 256), lambda s, idx: (0, sub(s, idx))),
                pl.BlockSpec((256, D), lambda s, idx: (sub(s, idx), 0)),
                pl.BlockSpec((1, 256), lambda s, idx: (0, sub(s, idx))),
            ]
            + [pl.BlockSpec(memory_space=pl.ANY)] * len(alias),
            out_specs=[grads] * 4
            + [
                column,
                column,
                pl.BlockSpec((1, 256), lambda s, idx: (0, sub(s, idx) - 2 * first)),
            ],
            scratch_shapes=[pltpu.VMEM((D, 256), bf16)],
        ),
        out_shape=[shape((2, 2, 256, 512), bf16)] * 4
        + [
            shape((rows, FF // 2), bf16),
            shape((rows, FF // 2), bf16),
            shape((1, 1024), f32),
        ],
        input_output_aliases={7: 4, 8: 5} if alias else {},
        compiler_params=params(),
        cost_estimate=cost(16 * rows * D * 512, 14 * 2**20),
        name="feed_forward",
    )(idx, a, dy, up_mine, up_recv, w_down, b_up, *alias)


def rotated(field, cosine, sine, direction):
    lane = lax.broadcasted_iota(jnp.int32, field.shape, 1) % HD
    partner = jnp.where(
        lane < ROT // 2,
        pltpu.roll(field, PAIR - ROT // 2, 1),
        pltpu.roll(field, ROT // 2, 1),
    )
    return field * cosine + (direction * sine) * partner


def whole_qkv(core, mine, recv_ref, w_ref):
    for t in range(3):
        w_ref[rows_of(core), t * HALF : (t + 1) * HALF] = mine[t][...]
    w_ref[rows_of(1 - core), :] = recv_ref[...]


def qkv_specs():
    return [
        pl.BlockSpec((HALF, HALF), lambda i, idx, t=t: (0, 2 * t + idx[0])) for t in range(3)
    ] + [pl.BlockSpec((HALF, 3 * HALF), lambda i, idx: (0, 0))]


def qkv_body(
    idx,
    x_ref,
    prev_ref,
    other_prev_ref,
    glob_ref,
    vec_ref,
    wq,
    wk,
    wv,
    recv_ref,
    cos_ref,
    sin_ref,
    cosp_ref,
    sinp_ref,
    cosg_ref,
    sing_ref,
    *outs,
):
    a1, q1, k1, v1, a2, k2, v2, a3, q3, k3, v3, w_ref = outs
    step = pl.program_id(0)
    first = idx[0] == 0

    def bias(t):
        at = [((2 * t + core) // 3, 6 + (2 * t + core) % 3) for core in range(2)]
        low, high = (vec_ref[h : h + 1, i * HALF : (i + 1) * HALF] for h, i in at)
        return jnp.where(first, low, high)

    @pl.when(step == 0)
    def _():
        whole_qkv(idx[0], (wq, wk, wv), recv_ref, w_ref)

    def run(x, cosine, sine, a_ref, refs):
        normal, _ = norm_parts(x.astype(f32))
        a = (normal * vector(vec_ref, 0) + vector(vec_ref, 1)).astype(bf16)
        a_ref[...] = a
        cosine, sine = cosine[...], sine[...]
        for t, ref in enumerate(refs):
            if ref is None:
                continue
            part = slice(t * HALF, (t + 1) * HALF)
            lin = dot(a, w_ref[:, part]) + bias(t)
            if t == 2:
                ref[...] = lin.astype(bf16)
                continue
            for j in range(HALF // PAIR):
                lanes = slice(j * PAIR, (j + 1) * PAIR)
                ref[:, lanes] = rotated(lin[:, lanes], cosine, sine, 1.0).astype(bf16)

    @pl.when(step < 4)
    def _():
        run(x_ref[...], cos_ref, sin_ref, a1, (q1, k1, v1))

    @pl.when((step >= 4) & (step < 6))
    def _():
        run(prev_ref[...], cosp_ref, sinp_ref, a2, (None, k2, v2))

    @pl.when((step >= 6) & (step < 8))
    def _():
        run(other_prev_ref[...], cosp_ref, sinp_ref, a2, (None, k2, v2))

    @pl.when(step == 8)
    def _():
        run(glob_ref[...], cosg_ref, sing_ref, a3, (q3, k3, v3))


def clamped(i, low, count):
    return jnp.clip(i - low, 0, count - 1)


def qkv_call(idx, x, prev, other_prev, glob, vectors, mine, recv, tables, before, far):
    step, rows = 256, x.shape[0]
    glob_n = glob.shape[0]

    def block(low, count, width, period=None):
        at = lambda i: clamped(i, low, count)
        if period:
            return pl.BlockSpec((step, width), lambda i, idx: (at(i) % period, 0))
        return pl.BlockSpec((step, width), lambda i, idx: (at(i), 0))

    whole = lambda width: pl.BlockSpec((glob_n, width), lambda i, idx: (0, 0))
    own, third = block(0, 4, D), block(0, 4, HALF)
    return pl.pallas_call(
        qkv_body,
        grid_spec=pltpu.PrefetchScalarGridSpec(
            num_scalar_prefetch=1,
            grid=(9,),
            in_specs=[own, block(4, 2, D), block(6, 2, D), whole(D)]
            + [pl.BlockSpec(vectors.shape, lambda i, idx: (0, 0))]
            + qkv_specs()
            + [block(0, 4, PAIR, 2)] * 2
            + [block(4, 4, PAIR, 2)] * 2
            + [whole(PAIR)] * 2,
            out_specs=[own, third, third, third, block(4, 4, D)]
            + [block(4, 4, HALF)] * 2
            + [whole(D)]
            + [whole(HALF)] * 3,
            scratch_shapes=[pltpu.VMEM((D, 3 * HALF), bf16)],
        ),
        out_shape=[shape((rows, D), bf16)]
        + [shape((rows, HALF), bf16)] * 3
        + [shape((rows, D), bf16)]
        + [shape((rows, HALF), bf16)] * 2
        + [shape((glob_n, D), bf16)]
        + [shape((glob_n, HALF), bf16)] * 3,
        compiler_params=params(),
        cost_estimate=cost(2 * rows * D * 5 * HALF, 22 * 2**20),
        name="qkv",
    )(idx, x, prev, other_prev, glob, vectors, mine, mine, mine, recv, *tables, *before, *far)


def heads_beside(block_t):
    dim = lax.broadcasted_iota(jnp.int32, block_t.shape, 0)
    zero = jnp.zeros_like(block_t)
    return jnp.concatenate(
        [jnp.where(dim < HD, block_t, zero), jnp.where(dim < HD, zero, block_t)], axis=1
    )


def heads_below(block):
    dim = lax.broadcasted_iota(jnp.int32, block.shape, 1)
    zero = jnp.zeros_like(block)
    return jnp.concatenate(
        [jnp.where(dim < HD, block, zero), jnp.where(dim < HD, zero, block)], axis=0
    )


def heads_back(both):
    n = both.shape[1] // 2
    dim = lax.broadcasted_iota(jnp.int32, (PAIR, n), 0)
    return jnp.where(dim < HD, both[:, :n], both[:, n:])


def near_body(
    info,
    q_ref,
    k_ref,
    v_ref,
    dol_ref,
    kp_ref,
    vp_ref,
    kg_ref,
    vg_ref,
    glob_ref,
    cos_ref,
    sin_ref,
    cosp_ref,
    sinp_ref,
    cosg_ref,
    sing_ref,
    *rest,
):
    o_ref, dq_ref, dk_ref, dv_ref, dkp_ref, dvp_ref, dkg_ref, dvg_ref, dk_acc, dv_acc = rest
    scale = HD**-0.5
    base = info[0]
    absent = jnp.where(base == 0, f32(negative), f32(0.0))
    keys = jnp.concatenate([kp_ref[...], k_ref[...]], axis=0)
    values = jnp.concatenate([vp_ref[...], v_ref[...]], axis=0)
    keys_t = keys.T
    values_t = values.T
    gkeys, gvalues = kg_ref[...], vg_ref[...]
    glob_n = gkeys.shape[0]
    gkeys_t = gkeys.astype(f32).T.astype(bf16)
    gvalues_t = gvalues.astype(f32).T.astype(bf16)
    keys_values = jnp.concatenate([keys, values], axis=1)
    gkeys_values = jnp.concatenate([gkeys, gvalues], axis=1)
    query = (q_ref[...].astype(f32) * scale).astype(bf16)
    query_t = query.T
    dol = dol_ref[...]
    dol_t = dol.T
    two = 2 * TILE
    window = WIN + TILE
    cosine, sine = cos_ref[...], sin_ref[...]
    row = lax.broadcasted_iota(jnp.int32, (TILE, two), 0)
    lane = lax.broadcasted_iota(jnp.int32, (TILE, two), 1) % TILE
    glane = lax.broadcasted_iota(jnp.int32, (glob_n, two), 1) % TILE
    gpos = jnp.concatenate([glob_ref[0], glob_ref[0]], axis=1)
    dkg = jnp.zeros((glob_n, PAIR), f32)
    dvg = jnp.zeros((glob_n, PAIR), f32)
    kk, vv = [None] * 8, [None] * 8
    for t in range(ROW // TILE):
        rows = slice(t * TILE, (t + 1) * TILE)
        span = slice(t * TILE, t * TILE + window)
        cut = WIN - t * TILE
        q_beside = heads_beside(query_t[:, rows])
        d_beside = heads_beside(dol_t[:, rows])
        q_below = heads_below(query[rows])
        d_below = heads_below(dol[rows])
        blank = jnp.zeros_like(q_beside)
        right = jnp.concatenate(
            [
                jnp.concatenate([q_beside, blank], axis=1),
                jnp.concatenate([blank, d_beside], axis=1),
            ],
            axis=0,
        )
        both = dot(keys_values[span], right)
        far_both = dot(gkeys_values, right)
        score, d_prob = both[:, :two], both[:, two:]
        far, d_far = far_both[:, :two], far_both[:, two:]
        parts = [
            jnp.where(row > lane, score[:TILE] + absent, negative),
        ]
        if cut > TILE:
            parts.append(score[TILE:cut] + absent)
        parts.append(score[cut:WIN])
        if t == 0:
            parts.pop()
        parts.append(jnp.where(row <= lane, score[WIN:], negative))
        score = jnp.concatenate(parts, axis=0)
        far = jnp.where(base + t * TILE + glane - gpos >= WIN, far, negative)
        top = jnp.maximum(
            jnp.max(score, axis=0, keepdims=True), jnp.max(far, axis=0, keepdims=True)
        )
        prob = jnp.exp(score - top)
        far_prob = jnp.exp(far - top)
        total = jnp.sum(prob, axis=0, keepdims=True) + jnp.sum(far_prob, axis=0, keepdims=True)
        delta = jnp.sum(prob * d_prob, axis=0, keepdims=True) + jnp.sum(
            far_prob * d_far, axis=0, keepdims=True
        )
        inverse = 1.0 / total
        delta = delta * inverse
        prob = prob * inverse
        far_prob = far_prob * inverse
        low, far_low = prob.astype(bf16), far_prob.astype(bf16)
        d_score = (prob * (d_prob - delta)).astype(bf16)
        d_far = (far_prob * (d_far - delta)).astype(bf16)
        out_t = dot(values_t[:, span], low) + dot(gvalues_t, far_low)
        o_ref[rows, :] = heads_back(out_t).T.astype(bf16)
        dq_t = dot(keys_t[:, span], d_score) + dot(gkeys_t, d_far)
        dq = heads_back(dq_t).T * scale
        dq_ref[rows, :] = rotated(dq, cosine[rows], sine[rows], -1.0).astype(bf16)
        tk, tv = dot(d_score, q_below), dot(low, d_below)
        for b in range(5):
            bk, bv = tk[b * TILE : (b + 1) * TILE], tv[b * TILE : (b + 1) * TILE]
            kk[t + b] = bk if kk[t + b] is None else kk[t + b] + bk
            vv[t + b] = bv if vv[t + b] is None else vv[t + b] + bv
        dkg = dkg + dot(d_far, q_below)
        dvg = dvg + dot(far_low, d_below)
    for b in range(8):
        dk_acc[b * TILE : (b + 1) * TILE, :] = kk[b]
        dv_acc[b * TILE : (b + 1) * TILE, :] = vv[b]
    dk_ref[...] = dk_acc[ROW:, :]
    dv_ref[...] = dv_acc[ROW:, :]
    dkp_ref[...] = rotated(dk_acc[:ROW, :], cosp_ref[...], sinp_ref[...], -1.0).astype(bf16)
    dvp_ref[...] = dv_acc[:ROW, :].astype(bf16)
    dkg_ref[...] = rotated(dkg, cosg_ref[...], sing_ref[...], -1.0).astype(bf16)
    dvg_ref[...] = dvg.astype(bf16)


def near_call(info, q, k, v, dol, k2, v2, kg, vg, glob_wide, tables, before, far):
    glob_n = glob_wide.shape[1]
    own = pl.BlockSpec((ROW, PAIR), lambda j, h, info: (j, h))
    glob = pl.BlockSpec((glob_n, PAIR), lambda j, h, info: (j, h))
    table = pl.BlockSpec((ROW, PAIR), lambda j, h, info: (0, 0))
    gtable = pl.BlockSpec((glob_n, PAIR), lambda j, h, info: (j, 0))
    rows = q.shape[0]
    own_low, own_high = shape((rows, HALF), bf16), shape((rows, HALF), f32)
    glob_low = shape((2 * glob_n, HALF), bf16)
    return pl.pallas_call(
        near_body,
        grid_spec=pltpu.PrefetchScalarGridSpec(
            num_scalar_prefetch=1,
            grid=(2, HALF // PAIR),
            in_specs=[own] * 6
            + [glob] * 2
            + [pl.BlockSpec((1, glob_n, PAIR), lambda j, h, info: (j, 0, 0))]
            + [table] * 4
            + [gtable] * 2,
            out_specs=[own] * 6 + [glob] * 2,
            scratch_shapes=[pltpu.VMEM((2 * ROW, PAIR), f32)] * 2,
        ),
        out_shape=[own_low, own_low, own_high, own_high, own_low, own_low, glob_low, glob_low],
        compiler_params=params(),
        cost_estimate=cost(8 * 4 * 6 * 2 * 704 * 256 * 256, 16 * 2**20),
        name="near",
    )(info, q, k, v, dol, k2, v2, kg, vg, glob_wide, *tables, *before, *far)


def glob_first_body(info, qg_ref, k_ref, v_ref, glob_ref, out_ref):
    glob_n = qg_ref.shape[0]
    query = qg_ref[...].astype(f32) * HD**-0.5
    beside = heads_beside(query.T).astype(bf16)
    score = dot(k_ref[...], beside)
    key_pos = info[0] + lax.broadcasted_iota(jnp.int32, score.shape, 0)
    mask = key_pos <= glob_ref[0][0:1]
    masked = jnp.where(mask, score, negative)
    top = jnp.max(masked, axis=0, keepdims=True)
    prob = jnp.where(mask, jnp.exp(masked - top), 0.0)
    total = jnp.sum(prob, axis=0, keepdims=True)
    both = dot(v_ref[...].T, prob.astype(bf16))
    lane = lax.broadcasted_iota(jnp.int32, (HD, 2 * glob_n), 1)
    out_ref[0, 0:HD, :] = jnp.where(lane < glob_n, both[:HD], both[HD:])
    out_ref[0, HD : HD + 1, :] = top
    out_ref[0, HD + 1 : HD + 2, :] = total
    out_ref[0, HD + 2 : HD + 8, :] = jnp.zeros((6, 2 * glob_n), f32)


def glob_first_call(info, qg, k, v, glob_row):
    glob_n = glob_row.shape[2] // 2
    own = pl.BlockSpec((ROW, PAIR), lambda j, h, info: (j, h))
    pairs = HALF // PAIR
    return pl.pallas_call(
        glob_first_body,
        grid_spec=pltpu.PrefetchScalarGridSpec(
            num_scalar_prefetch=1,
            grid=(2, pairs),
            in_specs=[
                pl.BlockSpec((glob_n, PAIR), lambda j, h, info: (j, h)),
                own,
                own,
                pl.BlockSpec((1, 8, 2 * glob_n), lambda j, h, info: (j, 0, 0)),
            ],
            out_specs=pl.BlockSpec(
                (1, HD + 8, 2 * glob_n), lambda j, h, info: (j * pairs + h, 0, 0)
            ),
        ),
        out_shape=shape((2 * pairs, HD + 8, 2 * glob_n), f32),
        compiler_params=params(),
        cost_estimate=cost(8 * 2 * 2 * 512 * 128 * 256, 3 * 2**20),
        name="glob_first",
    )(info, qg, k, v, glob_row)


def merged(first, second):
    top_a, top_b = first[:, HD : HD + 1], second[:, HD : HD + 1]
    top = jnp.maximum(top_a, top_b)
    weight_a, weight_b = jnp.exp(top_a - top), jnp.exp(top_b - top)
    total = first[:, HD + 1 : HD + 2] * weight_a + second[:, HD + 1 : HD + 2] * weight_b
    out = first[:, :HD] * weight_a + second[:, :HD] * weight_b
    return jnp.concatenate([out, top, total, first[:, HD + 2 :]], axis=1)


def glob_second_body(
    info,
    qg_ref,
    dolg_ref,
    k_ref,
    v_ref,
    stat_ref,
    glob_ref,
    near_ref,
    dk_in,
    dv_in,
    cos_ref,
    sin_ref,
    cosg_ref,
    sing_ref,
    o_ref,
    dk_ref,
    dv_ref,
    dqg_ref,
):
    scale = HD**-0.5
    glob_n = qg_ref.shape[0]
    keys, values = k_ref[...], v_ref[...]
    query = qg_ref[...].astype(f32) * scale
    q_beside = heads_beside(query.T).astype(bf16)
    q_below = heads_below(query.astype(bf16))
    dol = dolg_ref[...]
    dol_t = dol.astype(f32).T
    d_beside = heads_beside(dol_t).astype(bf16)
    d_below = heads_below(dol)
    out_t = stat_ref[0, 0:HD, :]
    top = stat_ref[0, HD : HD + 1, :]
    total = stat_ref[0, HD + 1 : HD + 2, :]
    out_t = out_t * (1.0 / total)
    lse = top + jnp.log(total)
    delta = jnp.sum(
        out_t * jnp.concatenate([dol_t[:HD], dol_t[HD:]], axis=1), axis=0, keepdims=True
    )
    score = dot(keys, q_beside)
    key_pos = info[0] + lax.broadcasted_iota(jnp.int32, score.shape, 0)
    positions = glob_ref[0][0:1]
    mask = key_pos <= positions
    prob = jnp.where(mask, jnp.exp(jnp.where(mask, score, negative) - lse), 0.0)
    d_prob = dot(values, d_beside)
    d_score = (prob * (d_prob - delta)).astype(bf16)
    low = prob.astype(bf16)
    dk = dk_in[...] + dot(d_score, q_below)
    dv = dv_in[...] + dot(low, d_below)
    dk_ref[...] = rotated(dk, cos_ref[...], sin_ref[...], -1.0).astype(bf16)
    dv_ref[...] = dv.astype(bf16)
    dq_both = dot(keys.T, d_score)
    dq_t = jnp.concatenate([dq_both[:HD, :glob_n], dq_both[HD:, glob_n:]], axis=0)
    dqg_ref[...] = rotated(dq_t.T * scale, cosg_ref[...], sing_ref[...], -1.0).astype(bf16)
    rows = jnp.concatenate([out_t[:, :glob_n], out_t[:, glob_n:]], axis=0).T.astype(bf16)
    place = (key_pos[:, :glob_n] == positions[:, :glob_n]).astype(f32)
    hit = jnp.sum(place, axis=1, keepdims=True) > 0.0
    o_ref[...] = jnp.where(hit, dot(place.astype(bf16), rows).astype(bf16), near_ref[...])


def glob_second_call(info, qg, dolg, k, v, stats, glob_row, near, dk, dv, tables, far):
    glob_n = glob_row.shape[2] // 2
    pairs = HALF // PAIR
    rows = k.shape[0]
    own = pl.BlockSpec((ROW, PAIR), lambda j, h, info: (j, h))
    glob = pl.BlockSpec((glob_n, PAIR), lambda j, h, info: (j, h))
    gtable = pl.BlockSpec((glob_n, PAIR), lambda j, h, info: (j, 0))
    table = pl.BlockSpec((ROW, PAIR), lambda j, h, info: (0, 0))
    return pl.pallas_call(
        glob_second_body,
        grid_spec=pltpu.PrefetchScalarGridSpec(
            num_scalar_prefetch=1,
            grid=(2, pairs),
            in_specs=[
                pl.BlockSpec((glob_n, PAIR), lambda j, h, info: (j, h)),
                glob,
                own,
                own,
                pl.BlockSpec((1, HD + 8, 2 * glob_n), lambda j, h, info: (j * pairs + h, 0, 0)),
                pl.BlockSpec((1, 8, 2 * glob_n), lambda j, h, info: (j, 0, 0)),
                own,
                own,
                own,
                table,
                table,
                gtable,
                gtable,
            ],
            out_specs=[
                own,
                own,
                own,
                glob,
            ],
        ),
        out_shape=[
            shape((rows, HALF), bf16),
            shape((rows, HALF), bf16),
            shape((rows, HALF), bf16),
            shape((2 * glob_n, HALF), bf16),
        ],
        compiler_params=params(),
        cost_estimate=cost(8 * 5 * 2 * 512 * 128 * 256, 10 * 2**20),
        name="glob_second",
    )(info, qg, dolg, k, v, stats, glob_row, near, dk, dv, *tables, *far)


def weights_body(units, idx, *refs):
    sends, keeps = refs[-4::2], refs[-3::2]
    core = idx[0]

    def run(u, ref):
        two = idx[2 - u]
        kind, *operands = units[u]
        if kind == "rows":
            left, right = operands
            total = dot_tn(refs[left][...], refs[right][...]).astype(bf16)
            for r in range(2):
                ref[place_of(two, r), 0, :, :] = total[:, r * HALF : (r + 1) * HALF]
            return
        for m in range(2):
            total = None
            for left, right in operands[0]:
                term = dot_tn(refs[left + m][...], refs[right][...])
                total = term if total is None else total + term
            spread_rows(ref, 0, total.astype(bf16), m, core, two, slice(None))

    for u in range(2):
        for half, ref in ((0, sends[u]), (1, keeps[u])):

            @pl.when(pl.program_id(0) == 2 * u + half)
            def _(u=u, ref=ref):
                run(u, ref)


def weights_call(idx, units):
    specs, operands, table, lefts = [], [], [], {}

    def add(array, spec):
        specs.append(spec)
        operands.append(array)
        return len(operands) - 1

    def whole(array):
        return add(array, pl.BlockSpec(array.shape, lambda s, idx: (0, 0)))

    def part(s, idx):
        return idx[1 + s // 2] ^ (1 - s % 2)

    def left_of(array):
        if id(array) not in lefts:
            lefts[id(array)] = [
                add(
                    array,
                    pl.BlockSpec(
                        (array.shape[0], 256), lambda s, idx, m=m: (0, 2 * m + part(s, idx))
                    ),
                )
                for m in range(2)
            ][0]
        return lefts[id(array)]

    for kind, products in units:
        if kind == "rows":
            left, right = products
            spec = pl.BlockSpec((left.shape[0], 256), lambda s, idx: (0, part(s, idx)))
            table.append((kind, add(left, spec), whole(right)))
        else:
            table.append((kind, tuple((left_of(left), whole(right)) for left, right in products)))
    out = pl.BlockSpec((2, 1, 256, 512), lambda s, idx: (0, 0, 0, 0))
    return pl.pallas_call(
        functools.partial(weights_body, tuple(table)),
        grid_spec=pltpu.PrefetchScalarGridSpec(
            num_scalar_prefetch=1, grid=(4,), in_specs=specs, out_specs=[out] * 4
        ),
        out_shape=[shape((2, 1, 256, 512), bf16)] * 4,
        compiler_params=params(),
        cost_estimate=cost(4 * 10**9, 12 * 2**20),
        name="weight_grads",
    )(idx, *operands)


def input_body(idx, *refs):
    x_ref, xp_ref, xop_ref, xg_ref, vec_ref = refs[:5]
    weights, up_mine, up_recv = refs[5:9], refs[9], refs[10]
    dq1, dk1, dv1, dkp, dvp, dqg, dkg, dvg, dup_ref = refs[11:20]
    own, own_other, prev, prev_other, glob, sums_a, sums_m, bias_ref, w_ref, wu_ref = refs[20:]
    step = pl.program_id(0)

    @pl.when(step == 0)
    def _():
        sums_a[...] = jnp.zeros_like(sums_a)
        sums_m[...] = jnp.zeros_like(sums_m)
        bias_ref[...] = jnp.zeros_like(bias_ref)
        whole_qkv(idx[0], weights[:3], weights[3], w_ref)
        wu_ref[rows_of(idx[0]), :] = up_mine[...]
        wu_ref[rows_of(1 - idx[0]), :] = up_recv[...]

    def gather(sums, grad, normal):
        sums[0:1, :] += jnp.sum(grad * normal, axis=0, keepdims=True)
        sums[1:2, :] += jnp.sum(grad, axis=0, keepdims=True)

    def attn(x, parts):
        grad = None
        for t, ref in enumerate(parts):
            if ref is None:
                continue
            part = ref[...]
            lanes = slice(t * HALF, (t + 1) * HALF)
            term = dot_nt(part, w_ref[:, lanes])
            grad = term if grad is None else grad + term
            bias_ref[0:1, lanes] += jnp.sum(part.astype(f32), axis=0, keepdims=True)
        normal, _ = norm_parts(x[...].astype(f32))
        gather(sums_a, grad, normal)
        return grad * vector(vec_ref, 0), normal

    def own_rows(out):
        g, normal = attn(x_ref, (dq1, dk1, dv1))
        grad = dot_nt(dup_ref[...], wu_ref[...])
        gather(sums_m, grad, normal)
        out[...] = (g + grad * vector(vec_ref, 2)).astype(bf16)

    @pl.when(step < 2)
    def _():
        own_rows(own)

    @pl.when((step >= 2) & (step < 4))
    def _():
        own_rows(own_other)

    @pl.when((step >= 4) & (step < 6))
    def _():
        prev[...] = attn(xp_ref, (None, dkp, dvp))[0].astype(bf16)

    @pl.when((step >= 6) & (step < 8))
    def _():
        prev_other[...] = attn(xop_ref, (None, dkp, dvp))[0].astype(bf16)

    @pl.when(step == 8)
    def _():
        glob[...] = attn(xg_ref, (dqg, dkg, dvg))[0].astype(bf16)


def input_call(idx, x, prev, other_prev, glob, vectors, mine, recv, up_mine, up_recv, grads):
    step, rows, glob_n = 256, x.shape[0], glob.shape[0]

    def block(low, count, width):
        return pl.BlockSpec((step, width), lambda i, idx: (clamped(i, low, count), 0))

    whole = lambda rows, width: pl.BlockSpec((rows, width), lambda i, idx: (0, 0))
    return pl.pallas_call(
        input_body,
        grid_spec=pltpu.PrefetchScalarGridSpec(
            num_scalar_prefetch=1,
            grid=(9,),
            in_specs=[block(0, 4, D), block(4, 2, D), block(6, 2, D), whole(glob_n, D)]
            + [whole(*vectors.shape)]
            + qkv_specs()
            + [
                pl.BlockSpec((HALF, FF // 2), lambda i, idx: (0, idx[0])),
                whole(HALF, FF // 2),
            ]
            + [block(0, 4, HALF)] * 3
            + [block(4, 4, HALF)] * 2
            + [whole(glob_n, HALF)] * 3
            + [block(0, 4, FF // 2)],
            out_specs=[
                block(0, 2, D),
                block(2, 2, D),
                block(4, 2, D),
                block(6, 2, D),
                whole(glob_n, D),
                whole(8, D),
                whole(8, D),
                whole(8, 3 * HALF),
            ],
            scratch_shapes=[pltpu.VMEM((D, 3 * HALF), bf16), pltpu.VMEM((D, FF // 2), bf16)],
        ),
        out_shape=[shape((rows // 2, D), bf16)] * 4
        + [
            shape((glob_n, D), bf16),
            shape((8, D), f32),
            shape((8, D), f32),
            shape((8, 3 * HALF), f32),
        ],
        compiler_params=params(),
        cost_estimate=cost(2 * rows * D * (5 * HALF + FF // 2), 30 * 2**20),
        name="input_grads",
    )(
        idx,
        x,
        prev,
        other_prev,
        glob,
        vectors,
        mine,
        mine,
        mine,
        recv,
        up_mine,
        up_recv,
        *grads,
    )


def result_body(act_ref, wd_ref, ol_ref, wp_ref, mine_ref, other_ref):
    part = (dot(act_ref[...], wd_ref[...]) + dot(ol_ref[...], wp_ref[...])).astype(bf16)
    half = pl.num_programs(0) // 2

    @pl.when(pl.program_id(0) < half)
    def _():
        mine_ref[...] = part

    @pl.when(pl.program_id(0) >= half)
    def _():
        other_ref[...] = part


def result_call(act, w_down, ol, w_proj):
    rows, step = act.shape[0], 256
    half = rows // step // 2
    return pl.pallas_call(
        result_body,
        grid=(rows // step,),
        in_specs=[
            pl.BlockSpec((step, act.shape[1]), lambda i: (i, 0)),
            pl.BlockSpec(w_down.shape, lambda i: (0, 0)),
            pl.BlockSpec((step, HALF), lambda i: (i, 0)),
            pl.BlockSpec(w_proj.shape, lambda i: (0, 0)),
        ],
        out_specs=[
            pl.BlockSpec((step, D), lambda i: (jnp.minimum(i, half - 1), 0)),
            pl.BlockSpec((step, D), lambda i: (jnp.maximum(i - half, 0), 0)),
        ],
        out_shape=[shape((rows // 2, D), bf16)] * 2,
        compiler_params=params(),
        cost_estimate=cost(2 * rows * D * (FF // 2 + HALF), 14 * 2**20),
        name="result",
    )(act, w_down, ol, w_proj)


def place_body(spreads, rows, n_alias, idx, *refs):
    pieces, swapped = (refs[:4], refs[4:8]), refs[8]
    outs = list(refs[9 + n_alias :])
    spread_out = outs.pop(0) if spreads else None
    rows_out = outs.pop(0) if rows else None
    half = pl.program_id(2)

    for i in range(max(len(spreads), len(rows))):
        for g in range(2):

            @pl.when((pl.program_id(0) == i) & (pl.program_id(1) == g))
            def _(i=i, g=g):
                for beside in range(2):
                    if i < len(spreads):
                        u, tile = spreads[i]
                        r = idx[2 - u] ^ beside
                        at = pl.ds(pl.multiple_of(r * TILE, TILE), TILE)
                        piece = pieces[u][2 * g + beside]

                        @pl.when(half == 0)
                        def _():
                            spread_out[at, :] = piece[tile, TILE:, :].astype(f32)

                        @pl.when(half == 1)
                        def _():
                            spread_out[at, :] = swapped[4 * i + 2 * g + beside].astype(f32)

                    if i < len(rows):
                        u, tile = rows[i]
                        r = idx[2 - u] ^ beside
                        at = pl.ds(pl.multiple_of(half * TILE, TILE), TILE)
                        part = pieces[u][2 * g + beside][tile, at, :]
                        rows_out[:, lanes_of(r, HALF)] = part.astype(f32)


def place_call(idx, work, spreads, rows, spread_target, rows_target):
    targets = [target for target in (spread_target, rows_target) if target is not None]
    alias = [buf for buf, _, _ in targets if buf is not None]
    aliases, at = {}, 10
    for out, (buf, _, _) in enumerate(targets):
        if buf is not None:
            aliases[at] = out
            at += 1

    def index(tiles, where):
        def block(i, g, h, idx):
            last = len(tiles) - 1
            over = i > last
            i, g, h = jnp.where(over, last, i), jnp.where(over, 1, g), jnp.where(over, 1, h)
            unit = tiles[0][0]
            for k, (u, _) in enumerate(tiles):
                unit = jnp.where(i == k, u, unit)
            return where(i, jnp.where(unit == 0, idx[1], idx[2]) ^ g, h, idx[0])

        return block

    out_specs = []
    if spreads:
        out_specs.append(pl.BlockSpec((2 * TILE, HALF), index(spreads, spread_target[2])))
    if rows:
        out_specs.append(pl.BlockSpec((TILE, D), index(rows, rows_target[2])))
    whole = lambda array: pl.BlockSpec(array.shape, lambda i, g, h, idx: (0, 0, 0))
    operands = [*work.pieces[0], *work.pieces[1], work.swapped]
    return pl.pallas_call(
        functools.partial(place_body, spreads, rows, len(alias)),
        grid_spec=pltpu.PrefetchScalarGridSpec(
            num_scalar_prefetch=1,
            grid=(max(len(spreads), len(rows)), 2, 2),
            in_specs=[whole(array) for array in operands]
            + [pl.BlockSpec(memory_space=pl.ANY)] * len(alias),
            out_specs=out_specs,
        ),
        out_shape=[shape(dims, f32) for _, dims, _ in targets],
        input_output_aliases=aliases,
        compiler_params=params(),
        cost_estimate=cost(0, 14 * 2**20),
        name="place",
    )(idx, *operands, *alias)


def rotary_tables(positions):
    lane = jnp.arange(PAIR, dtype=jnp.int32) % HD
    half = ROT // 2
    freqs = rotary_base ** (-2.0 * (lane % half).astype(f32) / ROT)
    angles = positions.astype(f32)[:, None] * freqs[None, :]
    active = (lane < ROT)[None, :]
    sign = jnp.where(lane < half, -1.0, 1.0)[None, :]
    return jnp.where(active, jnp.cos(angles), 1.0), jnp.where(active, jnp.sin(angles) * sign, 0.0)


def per_device(
    tokens,
    cotangent,
    global_pos,
    attn_gain,
    attn_shift,
    mlp_gain,
    mlp_shift,
    qkv_weight,
    qkv_bias,
    proj_weight,
    proj_bias,
    up_weight,
    up_bias,
    down_weight,
    down_bias,
):
    n_ctx = lax.axis_size("ctx")
    core = lax.axis_index("fsdp")
    seq = lax.axis_index("seq")
    ctx = lax.axis_index("ctx")
    x_bit, y_bit = seq & 1, seq >> 1
    base = ctx * ROW
    own_x = tokens[0]
    own_dy = cotangent[0]
    glob_n = global_pos.shape[1]
    share = glob_n // n_ctx
    info = jnp.stack([base]).astype(jnp.int32)
    idx = jnp.stack([core, x_bit, y_bit, ctx]).astype(jnp.int32)
    order = Order()

    other_x = pair(own_x)
    mine = jnp.concatenate(
        [attn_gain, attn_shift, mlp_gain, mlp_shift, proj_bias, down_bias, qkv_bias]
    )
    theirs = pair(mine)
    up_recv = pair(lax.dynamic_slice_in_dim(up_weight, (1 - core) * (FF // 2), FF // 2, 1))
    other_dy = pair(own_dy)
    halves = jnp.stack([mine, theirs])
    vectors = jnp.where(core == 0, halves, halves[::-1]).astype(f32)
    bias_up = up_bias.astype(f32).reshape(1, FF // 2)

    a_mlp, x, dy = norm_call(own_x, other_x, own_dy, other_dy, vectors)
    order.mark(a_mlp)
    prev_x = shifted(order.gate(own_x), 1)
    positions, w_in, x_in, dy_in = order.gate(global_pos[0], qkv_weight, own_x, own_dy)
    own_glob = lax.dynamic_slice_in_dim(positions, ctx * share, share, 0)
    pick = (own_glob[:, None] - base == jnp.arange(ROW, dtype=jnp.int32)[None, :]).astype(bf16)
    picked = jnp.stack([dot(pick, x_in), dot(pick, dy_in)]).astype(bf16)
    picked = order.mark(picked)[None]
    pos_pair = jnp.stack([positions, pair(positions)])
    if n_ctx == 4:
        picked_parts = [picked] + [exchange(picked, "ctx", k) for k in (1, 2, 3)]
    act = dup = None
    up_sums = []

    def units(first, act, dup):
        a = order.gate(a_mlp)
        *four, act, dup, sums = unit_call(
            idx, first, a, dy, up_weight, up_recv, down_weight, bias_up, act, dup
        )
        order.mark(sums)
        up_sums.append(sums.reshape(2, 512))
        return Reduction(order, idx, [four[:2], four[2:]]), act, dup

    work0, act, dup = units(0, act, dup)
    qkv_recv = pair(
        jnp.concatenate(
            [
                lax.dynamic_slice_in_dim(w_in, (2 * t + 1 - core) * HALF, HALF, 1)
                for t in range(3)
            ],
            axis=1,
        )
    )
    other_prev = pair(order.gate(prev_x))
    if n_ctx == 4:
        picked = jnp.concatenate(order.gate(*picked_parts), axis=0)
    else:
        for distance in doubling("ctx"):
            picked = jnp.concatenate([picked, exchange(picked, "ctx", distance)], axis=0)
    picked = jnp.take(picked, jnp.arange(n_ctx, dtype=jnp.int32) ^ ctx, axis=0)
    picked = order.mark(jnp.transpose(picked, (1, 0, 2, 3)).reshape(2, glob_n, D))
    other_picked = pair(picked)
    row_pos = base + jnp.arange(ROW, dtype=jnp.int32)
    work1, act, dup = units(2, act, dup)
    work0.second()

    tables = rotary_tables(order.gate(row_pos))
    before = rotary_tables(order.gate(row_pos) - ROW)
    far = rotary_tables(order.gate(pos_pair).reshape(-1))
    x_glob = jnp.concatenate([picked[0], other_picked[0]], axis=0)
    a1, q1, k1, v1, a2, k2, v2, a3, q3, k3, v3 = qkv_call(
        idx,
        order.gate(x),
        prev_x,
        other_prev,
        x_glob,
        vectors,
        qkv_weight,
        qkv_recv,
        tables,
        before,
        far,
    )
    order.mark(q3)
    is_glob = jnp.any(row_pos[None, :, None] == pos_pair[:, None, :], axis=2).reshape(2 * ROW, 1)
    glob_row = jnp.broadcast_to(
        jnp.concatenate([pos_pair, pos_pair], axis=1)[:, None, :], (2, 8, 2 * glob_n)
    )
    glob_wide = jnp.broadcast_to(pos_pair[:, :, None], (2, glob_n, PAIR))
    stats = order.mark(glob_first_call(info, order.gate(q3), k1, v1, glob_row))
    stats_beside = exchange(stats, "ctx", 1)
    dol = order.mark(
        jnp.where(is_glob, 0.0, dot_nt(order.gate(dy), proj_weight)).astype(bf16)
    )
    dolg = order.mark(
        dot_nt(
            jnp.concatenate([order.gate(picked)[1], other_picked[1]], axis=0), proj_weight
        ).astype(bf16)
    )
    work0.over_ctx()
    stats, stats_beside = order.gate(stats, stats_beside)
    stats = order.mark(merged(stats, stats_beside))
    for distance in doubling("ctx")[1:]:
        stats_beside = exchange(stats, "ctx", distance)
        if distance > 2:
            stats = merged(stats, stats_beside)
    work1.second()
    outs = near_call(
        info, order.gate(q1), k1, v1, dol, k2, v2, k3, v3, glob_wide, tables, before, far
    )
    near, dq1, dk1, dv1, dkp, dvp, dkg, dvg = outs
    order.mark(dkg)
    work0.ctx_sum()
    work1.over_ctx()
    if n_ctx <= 4:
        stats = order.mark(merged(*order.gate(stats, stats_beside)))
    ol, dk1, dv1, dqg = glob_second_call(
        info, q3, dolg, k1, v1, order.gate(stats), glob_row, near, dk1, dv1, tables, far
    )
    order.mark(dqg)
    lin_grads = (dq1, dk1, dv1, dkp, dvp, dqg, dkg, dvg)
    four = weights_call(
        idx,
        [
            ("spread", ((a1, order.gate(dv1)), (a2, dvp), (a3, dvg))),
            ("spread", ((a1, dq1), (a3, dqg))),
        ],
    )
    order.mark(four[0])
    work2 = Reduction(order, idx, [four[:2], four[2:]])
    four = weights_call(
        idx,
        [
            ("rows", (order.gate(ol), dy)),
            ("spread", ((a1, dk1), (a2, dkp), (a3, dkg))),
        ],
    )
    order.mark(four[0])
    work3 = Reduction(order, idx, [four[:2], four[2:]])
    work0.gather()
    work1.ctx_sum()
    work2.second()

    g_own, g_own_other, g_prev, g_prev_other, g_globs, sums_a, sums_m, bias = input_call(
        idx,
        order.gate(x),
        prev_x,
        other_prev,
        x_glob,
        vectors,
        qkv_weight,
        qkv_recv,
        up_weight,
        up_recv,
        (*lin_grads, dup),
    )
    order.mark(bias)
    prev_beside = pair(g_prev_other)
    own_beside = pair(g_own_other)
    glob_sum = added(g_globs[:glob_n], pair(g_globs[glob_n:]))
    work2.over_ctx()
    work3.second()
    work0.gather_rest()
    work1.gather()
    from_prev = shifted(order.mark(added(*order.gate(g_prev, prev_beside))), -1)

    part, part_other = result_call(order.gate(act), down_weight, ol, proj_weight)
    order.mark(part)
    part_beside = pair(part_other)
    work2.ctx_sum()
    work3.over_ctx()

    up_dims, down_dims = (HALF, FF), (FF // 2, D)

    def place_units(work, first, up_out, down_out):
        up_out, down_out = place_call(
            idx,
            work,
            ((0, 0), (1, 0)),
            ((0, 1), (1, 1)),
            (up_out, up_dims, lambda i, p, h, c: (p, (c ^ h) * 4 + first + i)),
            (down_out, down_dims, lambda i, p, h, c: ((first + i) * 4 + p * 2 + h, 0)),
        )
        order.mark(up_out[:8, :128])
        return up_out, down_out

    work0.swap([(0, 0), (1, 0)])
    work1.gather_rest()
    own, part, part_beside = order.gate(own_x, part, part_beside)
    result = own.astype(f32) + part.astype(f32) + part_beside.astype(f32)
    biases = [vectors[:, i * HALF : (i + 1) * HALF].reshape(1, D) for i in (4, 5)]
    layer_out = order.mark((result + biases[0] + biases[1]).astype(bf16))[None]
    work2.gather()
    work3.ctx_sum()
    up_out, down_out = place_units(work0, 0, None, None)

    for distance in doubling("ctx"):
        beside = exchange(glob_sum, "ctx", distance)
        glob_sum, beside = order.gate(glob_sum, beside)
        glob_sum = order.mark(added(glob_sum, beside))
    place = (row_pos[:, None] == global_pos[0][None, :]).astype(bf16)
    own, g_own, own_beside, from_prev = order.gate(own_x, g_own, own_beside, from_prev)
    g = (
        g_own.astype(f32)
        + own_beside.astype(f32)
        + from_prev.astype(f32)
        + dot(place, glob_sum)
    )
    normal, inverse = norm_parts(own.astype(f32))
    lower = inverse * (
        g
        - jnp.mean(g, axis=-1, keepdims=True)
        - normal * jnp.mean(g * normal, axis=-1, keepdims=True)
    )
    tokens_grad = order.mark(own_dy.astype(f32) + lower)[None]
    work2.gather_rest()
    work3.gather()
    work1.swap([(0, 0), (1, 0)])

    dy_sum = jnp.sum(order.gate(own_dy).astype(f32), axis=0)
    qkv_sum = bias[0].reshape(3, 1, HALF)
    mine = jnp.arange(2, dtype=jnp.int32)[None, :, None] == core
    qkv_sum = jnp.where(mine, qkv_sum, 0.0).reshape(2, 3, 512)
    split = jnp.concatenate(
        [
            sums_a[:2].reshape(2, 2, 512).swapaxes(0, 1),
            sums_m[:2].reshape(2, 2, 512).swapaxes(0, 1),
            dy_sum.reshape(2, 1, 512),
            qkv_sum,
        ],
        axis=1,
    )
    kept = lax.dynamic_index_in_dim(split, core, 0, False)
    given = lax.dynamic_index_in_dim(split, 1 - core, 0, False)
    total = jnp.concatenate([kept + pair(given)] + up_sums, axis=0)
    for axis in ("seq", "ctx"):
        for distance in doubling(axis):
            total = total + exchange(total, axis, distance)

    work3.gather_rest()
    up_out, down_out = place_units(work1, 2, up_out, down_out)
    work2.swap([(0, 0), (1, 0)])
    qkv_dims = (HALF, 3 * D)
    (qkv_out,) = place_call(
        idx,
        work2,
        ((0, 0), (1, 0)),
        (),
        (None, qkv_dims, lambda i, p, h, c: (p, jnp.where(i == 0, 4, 0) + (c ^ h))),
        None,
    )
    order.mark(qkv_out[:8, :128])
    work3.swap([(1, 0)])
    qkv_out, proj_out = place_call(
        idx,
        work3,
        ((1, 0),),
        ((0, 0),),
        (qkv_out, qkv_dims, lambda i, p, h, c: (p, 2 + (c ^ h))),
        (None, (HALF, D), lambda i, p, h, c: (p * 2 + h, 0)),
    )
    return (
        layer_out,
        tokens_grad,
        total[0],
        total[1],
        total[2],
        total[3],
        qkv_out,
        total[5:8].reshape(-1),
        proj_out,
        total[4],
        up_out,
        total[8:12].reshape(-1),
        down_out,
        total[4],
    )


def solution(mesh):
    rows = P(("seq", "fsdp"), "ctx", None)
    vector, matrix = P("fsdp"), P("fsdp", None)
    return jax.shard_map(
        per_device,
        mesh=mesh,
        in_specs=(
            rows,
            rows,
            P(("seq", "fsdp"), None),
            vector,
            vector,
            vector,
            vector,
            matrix,
            vector,
            matrix,
            vector,
            matrix,
            vector,
            matrix,
            vector,
        ),
        out_specs=(
            rows,
            rows,
            vector,
            vector,
            vector,
            vector,
            matrix,
            vector,
            matrix,
            vector,
            matrix,
            vector,
            matrix,
            vector,
        ),
        check_vma=False,
    )
```

```python
import functools
import math

import jax
import jax.numpy as jnp
from jax import lax
from jax.experimental import pallas as pl
from jax.experimental.pallas import tpu as pltpu
from jax.sharding import PartitionSpec as P

D = 1024
H = 16
HD = 64
ROT = 16
WIN = 512
FF = 4096
HALF = D // 2
PAIR = 2 * HD
ROW = 512
TILE = 128

epsilon = 1e-05
negative = -1e30
rotary_base = 10000.0
f32 = jnp.float32
bf16 = jnp.bfloat16
VMEM = 60 * 2**20
RATE = 3.6e6
FLOPS = 4.6e9
PAIRS = HALF // PAIR


def shape(dims, dtype):
    return jax.ShapeDtypeStruct(dims, dtype)


def params():
    return pltpu.CompilerParams(vmem_limit_bytes=VMEM)


def cost(microseconds):
    return pl.CostEstimate(flops=int(microseconds * FLOPS), bytes_accessed=int(microseconds * RATE), transcendentals=int(microseconds * 1e7))


def dot(left, right):
    return jnp.dot(left, right, preferred_element_type=f32)


def dot_nt(left, right):
    return lax.dot_general(left, right, (((1,), (1,)), ((), ())), preferred_element_type=f32)


def dot_tn(left, right):
    return lax.dot_general(left, right, (((0,), (0,)), ((), ())), preferred_element_type=f32)


def lanes_of(block, width):
    return pl.ds(pl.multiple_of(block * width, width), width)


def pair(block):
    return lax.ppermute(block, "fsdp", [(0, 1), (1, 0)])


def exchange(block, axis, distance):
    return lax.ppermute(block, axis, [(i, i ^ distance) for i in range(lax.axis_size(axis))])


def shifted(block, distance):
    devices = range(lax.axis_size("ctx"))
    return lax.ppermute(
        block, "ctx", [(i - distance, i) for i in devices if i - distance in devices]
    )


def doubling(axis):
    distance, out = 1, []
    while distance < lax.axis_size(axis):
        out.append(distance)
        distance *= 2
    return out


def crossed(block, turn, axis="seq"):
    route = []
    for at in range(lax.axis_size(axis)):
        for core in range(2):
            route.append((2 * at + core, 2 * (at ^ (1 + (core ^ turn))) + core))
    return lax.ppermute(block, (axis, "fsdp"), route)


def added(*parts):
    total = parts[0].astype(f32)
    for part in parts[1:]:
        total = total + part.astype(f32)
    return total.astype(bf16)


class Order:
    def __init__(self):
        self.token = None

    def gate(self, *arrays):
        if self.token is None:
            return arrays if len(arrays) > 1 else arrays[0]
        out = lax.optimization_barrier((*arrays, self.token))[:-1]
        return out if len(out) > 1 else out[0]

    def mark(self, array):
        self.token = array
        return array

    def land(self, *arrays):
        arrays = self.gate(*arrays)
        self.mark(arrays[0] if isinstance(arrays, (tuple, list)) else arrays)
        return arrays


class Reduction:
    def __init__(self, order, idx, send, keep, direct):
        self.order, self.idx, self.keep, self.direct = order, idx, keep, direct
        self.tiles = keep.shape[1]
        self.split = lax.axis_size("ctx") == 4
        self.recv = crossed(send, 0)

    def second(self):
        self.keep, self.recv = self.order.gate(self.keep, self.recv)
        self.other = crossed(self.order.mark(halves_call(self.keep, self.recv)), 1)

    def over_ctx(self):
        parts = self.order.gate(self.keep, self.recv, self.other)
        outs = quarters_call(self.idx, *parts, self.direct)
        if not self.split:
            self.total = lax.psum(self.order.mark(outs), "ctx")
        elif self.direct:
            self.own = self.order.mark(outs[0])
            self.recv = [exchange(part, "ctx", k + 1) for k, part in enumerate(outs[1:])]
        else:
            send, self.half = outs
            self.recv = crossed(self.order.mark(send), 0, "ctx")

    def ctx_half(self):
        if self.split and not self.direct:
            self.half, self.recv = self.order.gate(self.half, self.recv)
            far = self.order.mark(added(self.half[0], self.recv[0]))
            self.other = crossed(far, 1, "ctx")

    def ctx_sum(self):
        if not self.split:
            return
        if self.direct:
            self.own = self.order.mark(added(*self.order.gate(self.own, *self.recv)))
            self.recv = [exchange(self.own, "ctx", k) for k in (1, 2, 3)]
        else:
            half, recv, other = self.order.gate(self.half, self.recv, self.other)
            self.own = self.order.mark(added(half[1], recv[1], other))
            self.recv = [crossed(self.own, 1, "ctx"), crossed(self.own, 0, "ctx")]

    def ctx_rest(self):
        if self.split and not self.direct:
            self.recv[0] = self.order.land(self.recv[0])
            self.recv.append(crossed(self.recv[0], 0, "ctx"))

    def regroup(self):
        if self.split:
            parts = self.order.gate(self.own, *self.recv)
            self.total = self.order.mark(regroup_call(self.idx, *parts, direct=self.direct))
        self.total = self.total.reshape(self.tiles, 256, 512)

    def to_beside(self):
        self.beside = crossed(self.order.gate(self.total), 1)

    def to_across(self):
        self.across = crossed(self.order.gate(self.total), 0)

    def to_both(self):
        self.beside = self.order.land(self.beside)
        self.both = crossed(self.beside, 0)

    def swap(self, tiles):
        self.pieces = self.order.gate(self.total, self.beside, self.across, self.both)
        self.swapped = pair(self.order.mark(swap_call(self.pieces, tiles)))


def halves_body(keep, recv, out):
    out[...] = (keep[0].astype(f32) + recv[0].astype(f32)).astype(bf16)


def halves_call(keep, recv):
    tiles = keep.shape[1]
    step = tiles // 2
    block = pl.BlockSpec((1, step, 256, 512), lambda t: (0, t, 0, 0))
    return pl.pallas_call(
        halves_body,
        grid=(2,),
        in_specs=[block] * 2,
        out_specs=pl.BlockSpec((step, 256, 512), lambda t: (t, 0, 0)),
        out_shape=shape((tiles, 256, 512), bf16),
        compiler_params=params(),
        cost_estimate=cost(2.5),
        name="halves",
    )(keep, recv)


def quarters_body(split, direct, idx, keep, recv, other, *outs):
    def block(at):
        total = keep[0, at].astype(f32) + recv[0, at].astype(f32) + other[at].astype(f32)
        return total.astype(bf16)

    ctx, one = idx[3], 1 + idx[0]
    for k in range(4):
        if not split:
            outs[0][k] = block(k)
        elif direct:
            outs[k][...] = block(ctx ^ k)
        else:
            outs[k // 2][k % 2] = block(ctx ^ (3, one, 3 - one, 0)[k])


def quarters_call(idx, keep, recv, other, direct):
    split = lax.axis_size("ctx") == 4
    rows = keep.shape[1] * 256 // 4
    block = pl.BlockSpec((1, 4, rows, 512), lambda i, idx: (1, 0, 0, 0))
    quarter = pl.BlockSpec((4, rows, 512), lambda i, idx: (0, 0, 0))
    if not split:
        out_specs, out_shape = quarter, shape((4, rows, 512), bf16)
    elif direct:
        out_specs = [pl.BlockSpec((rows, 512), lambda i, idx: (0, 0))] * 4
        out_shape = [shape((rows, 512), bf16)] * 4
    else:
        out_specs = [pl.BlockSpec((2, rows, 512), lambda i, idx: (0, 0, 0))] * 2
        out_shape = [shape((2, rows, 512), bf16)] * 2
    return pl.pallas_call(
        functools.partial(quarters_body, split, direct),
        grid_spec=pltpu.PrefetchScalarGridSpec(
            num_scalar_prefetch=1,
            grid=(1,),
            in_specs=[block] * 2 + [quarter],
            out_specs=out_specs,
        ),
        out_shape=out_shape,
        compiler_params=params(),
        cost_estimate=cost(3.8),
        name="quarters",
    )(
        idx,
        keep.reshape(2, 4, rows, 512),
        recv.reshape(2, 4, rows, 512),
        other.reshape(4, rows, 512),
    )


def regroup_body(direct, idx, *refs):
    one = 1 + idx[0]
    for k in range(4):
        refs[4][idx[3] ^ (k if direct else (0, 3 - one, one, 3)[k])] = refs[k][...]


def regroup_call(idx, *parts, direct):
    rows = parts[0].shape[0]
    return pl.pallas_call(
        functools.partial(regroup_body, direct),
        grid_spec=pltpu.PrefetchScalarGridSpec(
            num_scalar_prefetch=1,
            grid=(1,),
            in_specs=[pl.BlockSpec((rows, 512), lambda i, idx: (0, 0))] * 4,
            out_specs=pl.BlockSpec((4, rows, 512), lambda i, idx: (0, 0, 0)),
        ),
        out_shape=shape((4, rows, 512), bf16),
        compiler_params=params(),
        cost_estimate=cost(3.0),
        name="regroup",
    )(idx, *parts)


def swap_body(*refs):
    for k, ref in enumerate(refs[:-1]):
        refs[-1][k] = ref[0]


def swap_call(pieces, tiles):
    operands = [(piece, t) for t in tiles for piece in pieces]
    return pl.pallas_call(
        swap_body,
        grid=(1,),
        in_specs=[
            pl.BlockSpec((1, TILE, 512), lambda i, t=t: (t, 0, 0)) for _, t in operands
        ],
        out_specs=pl.BlockSpec((len(operands), TILE, 512), lambda i: (0, 0, 0)),
        out_shape=shape((len(operands), TILE, 512), bf16),
        compiler_params=params(),
        cost_estimate=cost(2.5),
        name="swap",
    )(*[piece for piece, _ in operands])


def norm_parts(x):
    center = x - jnp.mean(x, axis=-1, keepdims=True)
    inverse = lax.rsqrt(jnp.mean(center * center, axis=-1, keepdims=True) + epsilon)
    return center * inverse, inverse


def vectors_body(pos_ref, *refs):
    at = 0
    for ref in refs[:-1]:
        value = ref[...].astype(f32)
        count = value.shape[0] // HALF
        refs[-1][at : at + count, :] = value.reshape(count, HALF)
        at += count
    refs[-1][at : at + 1, : pos_ref.shape[1]] = pos_ref[...].astype(f32)


def vectors_call(positions, *vectors):
    count = sum(v.shape[0] // HALF for v in vectors) + 1
    return pl.pallas_call(
        vectors_body,
        out_shape=shape((count, HALF), f32),
        compiler_params=params(),
        cost_estimate=cost(1.4),
        name="vectors",
    )(positions, *vectors)


def vector(refs, core, i):
    mine, theirs = refs[0][i : i + 1, :], refs[1][i : i + 1, :]
    first = core == 0
    return jnp.concatenate(
        [jnp.where(first, mine, theirs), jnp.where(first, theirs, mine)], axis=1
    )


def slice_body(idx, in_ref, out_ref):
    out_ref[...] = in_ref[...]


def slice_call(idx, w, width):
    step = width // 2
    return pl.pallas_call(
        slice_body,
        grid_spec=pltpu.PrefetchScalarGridSpec(
            num_scalar_prefetch=1,
            grid=(2,),
            in_specs=[pl.BlockSpec((w.shape[0], step), lambda i, idx: (0, 2 * (1 - idx[0]) + i))],
            out_specs=pl.BlockSpec((w.shape[0], step), lambda i, idx: (0, i)),
        ),
        out_shape=shape((w.shape[0], width), w.dtype),
        compiler_params=params(),
        cost_estimate=cost(3.4),
        name="slice",
    )(idx, w)


def collect_body(idx, *refs):
    share = refs[0].shape[-2]
    parts = [ref[k] for ref in refs[:-1] for k in range(ref.shape[0])]
    for k, part in enumerate(parts):
        at = pl.ds(pl.multiple_of((idx[3] ^ k) * share, share), share)
        refs[-1][:, :, at, :] = part


def collect_call(idx, *parts):
    share = parts[0].shape[-2]
    count = sum(part.shape[0] for part in parts)
    whole = lambda dims: pl.BlockSpec(dims, lambda i, idx: (0,) * len(dims))
    return pl.pallas_call(
        collect_body,
        grid_spec=pltpu.PrefetchScalarGridSpec(
            num_scalar_prefetch=1,
            grid=(1,),
            in_specs=[whole(part.shape) for part in parts],
            out_specs=whole((2, 2, share * count, D)),
        ),
        out_shape=shape((2, 2, share * count, D), bf16),
        compiler_params=params(),
        cost_estimate=cost(2.3),
        name="collect",
    )(idx, *parts)


def rows_of(core):
    return pl.ds(pl.multiple_of(core * HALF, HALF), HALF)


def place_of(bit, value):
    return jnp.where(bit == value, 1, 0)


def spread_rows(ref, tile, grad, m, core, two, lanes):
    at = pl.ds(pl.multiple_of(jnp.where(core == m, TILE, 0), TILE), TILE)
    for r in range(2):
        ref[place_of(two, r), tile, at, lanes] = grad[r * TILE : (r + 1) * TILE]


def unit_body(fresh, idx, *refs):
    refs = list(refs)
    if fresh:
        x_refs, vecs = refs[:2], refs[2:4]
        refs = refs[4:]
    else:
        a_ref, refs = refs[0], refs[3:]
    dy_refs, wu_mine, wu_recv, wd_ref, bu_ref, *refs = refs[:2], *refs[2:]
    if fresh:
        a_ref, *refs = refs
    send_ref, keep_ref, act_ref, dup_ref, bias_ref, wu_ref = refs
    core, one, two = idx[0], idx[1], idx[2]
    chunk = 256
    unit, half = pl.program_id(0) // 2, pl.program_id(0) % 2

    if fresh:

        @pl.when(pl.program_id(0) == 0)
        def _():
            gain, shift = vector(vecs, core, 2), vector(vecs, core, 3)
            for i in range(2 * ROW // chunk):
                at = slice(i % 2 * chunk, (i % 2 + 1) * chunk)
                normal, _ = norm_parts(x_refs[i // 2][at, :].astype(f32))
                a_ref[i * chunk : (i + 1) * chunk, :] = (normal * gain + shift).astype(bf16)
    wu_ref[rows_of(core), :] = wu_mine[...]
    wu_ref[rows_of(1 - core), :] = wu_recv[...]
    bias = jnp.zeros((1, chunk), f32)
    for i in range(2 * ROW // chunk):
        at, at_dy = slice(i * chunk, (i + 1) * chunk), slice(i % 2 * chunk, (i % 2 + 1) * chunk)
        up = dot(a_ref[at, :], wu_ref[...]) + bu_ref[...]
        grad = dot_nt(dy_refs[i // 2][at_dy, :], wd_ref[...])
        cdf = 0.5 * (1.0 + lax.erf(up * (0.5**0.5)))
        density = jnp.exp(-0.5 * up * up) * (1.0 / math.sqrt(2.0 * math.pi))
        act_ref[at, :] = (up * cdf).astype(bf16)
        dup = (grad * (cdf + up * density)).astype(bf16)
        dup_ref[at, :] = dup
        bias = bias + jnp.sum(dup.astype(f32), axis=0, keepdims=True)
    bias_ref[...] = bias
    lanes = lanes_of(one ^ (1 - half), chunk)
    for out, p in ((send_ref, 1 - one), (keep_ref, one)):
        for m in range(2):
            left = a_ref[:, lanes_of(2 * m + p, chunk)]
            grad = dot_tn(left, dup_ref[...]).astype(bf16)
            spread_rows(out, 2 * unit, grad, m, core, two, lanes)
    down = dot_tn(act_ref[:ROW, :], dy_refs[0][...]) + dot_tn(act_ref[ROW:, :], dy_refs[1][...])
    down = down.astype(bf16)
    for step, out in ((0, send_ref), (1, keep_ref)):

        @pl.when(half == step)
        def _(out=out):
            for r in range(2):
                out[place_of(two, r), 2 * unit + 1, :, :] = down[:, r * HALF : (r + 1) * HALF]


def unit_call(idx, first, source, dys, up_mine, up_recv, w_down, b_up, olds):
    fresh = isinstance(source, tuple)
    rows = 2 * ROW

    def sub(s, idx):
        return 2 * (first + s // 2) + (idx[1] ^ (1 - s % 2))

    def whole(dims):
        return pl.BlockSpec(dims, lambda s, idx: (0,) * len(dims))

    column = pl.BlockSpec((rows, 256), lambda s, idx: (0, sub(s, idx)))
    grads = whole((2, 4, 256, 512))
    if fresh:
        own, other, vectors = source
        operands = [own, other, *vectors]
        in_specs = [whole(v.shape) for v in operands]
        out_specs, out_shape = [whole((rows, D))], [shape((rows, D), bf16)]
        aliases = {}
    else:
        operands = [source, *olds]
        in_specs = [whole((rows, D))] + [pl.BlockSpec(memory_space=pl.ANY)] * 2
        out_specs, out_shape = [], []
        aliases = {2: 2, 3: 3}
    return pl.pallas_call(
        functools.partial(unit_body, fresh),
        grid_spec=pltpu.PrefetchScalarGridSpec(
            num_scalar_prefetch=1,
            grid=(4,),
            in_specs=in_specs
            + [
                whole((ROW, D)),
                whole((ROW, D)),
                pl.BlockSpec((HALF, 256), lambda s, idx: (0, idx[0] * 8 + sub(s, idx))),
                pl.BlockSpec((HALF, 256), lambda s, idx: (0, sub(s, idx))),
                pl.BlockSpec((256, D), lambda s, idx: (sub(s, idx), 0)),
                pl.BlockSpec((1, 256), lambda s, idx: (0, sub(s, idx))),
            ],
            out_specs=out_specs
            + [
                grads,
                grads,
                column,
                column,
                pl.BlockSpec((1, 256), lambda s, idx: (0, sub(s, idx) - 2 * first)),
            ],
            scratch_shapes=[pltpu.VMEM((D, 256), bf16)],
        ),
        out_shape=out_shape
        + [
            shape((2, 4, 256, 512), bf16),
            shape((2, 4, 256, 512), bf16),
            shape((rows, FF // 2), bf16),
            shape((rows, FF // 2), bf16),
            shape((1, 1024), f32),
        ],
        input_output_aliases=aliases,
        compiler_params=params(),
        cost_estimate=cost(18),
        name="feed_forward",
    )(idx, *operands, *dys, up_mine, up_recv, w_down, b_up)


def rotated(field, cosine, sine, direction):
    lane = lax.broadcasted_iota(jnp.int32, field.shape, 1) % HD
    partner = jnp.where(
        lane < ROT // 2,
        pltpu.roll(field, PAIR - ROT // 2, 1),
        pltpu.roll(field, ROT // 2, 1),
    )
    return field * cosine + (direction * sine) * partner


def whole_qkv(core, mine, recv_ref, w_ref):
    for t in range(3):
        w_ref[rows_of(core), t * HALF : (t + 1) * HALF] = mine[t][...]
    w_ref[rows_of(1 - core), :] = recv_ref[...]


def qkv_specs():
    return [
        pl.BlockSpec((HALF, HALF), lambda i, idx, t=t: (0, 2 * t + idx[0])) for t in range(3)
    ] + [pl.BlockSpec((HALF, 3 * HALF), lambda i, idx: (0, 0))]


def qkv_bias(vecs, core, t):
    def of(c):
        owner, row = (2 * t + c) // 3, 6 + (2 * t + c) % 3
        return vecs[0 if owner == c else 1][row : row + 1, :]

    return jnp.where(core == 0, of(0), of(1))


def qkv_rows(x, core, vecs, w_ref, table, a_ref, outs):
    normal, _ = norm_parts(x.astype(f32))
    a = (normal * vector(vecs, core, 0) + vector(vecs, core, 1)).astype(bf16)
    a_ref[...] = a
    cosine, sine = table[0][...], table[1][...]
    for t, ref in enumerate(outs):
        if ref is None:
            continue
        part = slice(t * HALF, (t + 1) * HALF)
        lin = dot(a, w_ref[:, part]) + qkv_bias(vecs, core, t)
        if t == 2:
            ref[...] = lin.astype(bf16)
            continue
        for j in range(PAIRS):
            lanes = slice(j * PAIR, (j + 1) * PAIR)
            ref[:, lanes] = rotated(lin[:, lanes], cosine, sine, 1.0).astype(bf16)


def qkv_own_body(idx, *refs):
    xs, dys, vecs, weights, recv_ref = refs[0:2], refs[2:4], refs[4:6], refs[6:9], refs[9]
    wp_ref, pos_ref, tables = refs[10], refs[11], refs[12:14]
    a1, q1, k1, v1, d1, w_out, w_ref = refs[14:]
    step, core = pl.program_id(0), idx[0]

    @pl.when(step == 0)
    def _():
        whole_qkv(core, weights, recv_ref, w_ref)
        w_out[...] = w_ref[...]

    for j in range(2):

        @pl.when(step // 2 == j)
        def _(j=j):
            qkv_rows(xs[j][...], core, vecs, w_ref, tables, a1, (q1, k1, v1))
            dol = dot_nt(dys[j][...], wp_ref[...])
            glob_n, rows = pos_ref.shape[1], dol.shape[0]
            row = lax.broadcasted_iota(jnp.int32, (rows, glob_n), 0)
            row = row + idx[3] * ROW + step % 2 * rows
            hits = jnp.sum((row == pos_ref[j : j + 1, :]).astype(f32), axis=1, keepdims=True)
            d1[...] = jnp.where(hits > 0.0, 0.0, dol).astype(bf16)


def qkv_more_body(idx, *refs):
    prevs, globs, vecs, w_ref, wp_ref = refs[0:2], refs[2], refs[3:5], refs[5], refs[6]
    before, far = refs[7:9], refs[9:11]
    a2, k2, v2, a3, q3, k3, v3, d3 = refs[11:]
    step, core = pl.program_id(0), idx[0]
    for j in range(2):

        @pl.when(step // 2 == j)
        def _(j=j):
            qkv_rows(prevs[j][...], core, vecs, w_ref, before, a2, (None, k2, v2))

    @pl.when(step == 4)
    def _():
        x = jnp.concatenate([globs[0, 0], globs[1, 0]], axis=0)
        qkv_rows(x, core, vecs, w_ref, far, a3, (q3, k3, v3))
        dy = jnp.concatenate([globs[0, 1], globs[1, 1]], axis=0)
        d3[...] = dot_nt(dy, wp_ref[...]).astype(bf16)


def clamped(i, low, count):
    return jnp.clip(i - low, 0, count - 1)


def qkv_block(low, count, width, period=None):
    def at(i, idx):
        block = clamped(i, low, count)
        return (block % period if period else block, 0)

    return pl.BlockSpec((256, width), at)


def whole_block(dims):
    return pl.BlockSpec(dims, lambda i, idx: (0,) * len(dims))


def qkv_own_call(idx, xs, dys, vectors, mine, recv, w_proj, positions, tables):
    rows = 2 * ROW
    third = qkv_block(0, 4, HALF)
    return pl.pallas_call(
        qkv_own_body,
        grid_spec=pltpu.PrefetchScalarGridSpec(
            num_scalar_prefetch=1,
            grid=(4,),
            in_specs=[qkv_block(0, 2, D), qkv_block(2, 2, D)] * 2
            + [whole_block(v.shape) for v in vectors]
            + qkv_specs()
            + [whole_block(w_proj.shape), whole_block(positions.shape)]
            + [qkv_block(0, 4, PAIR, 2)] * 2,
            out_specs=[qkv_block(0, 4, D)] + [third] * 4 + [whole_block((D, 3 * HALF))],
            scratch_shapes=[pltpu.VMEM((D, 3 * HALF), bf16)],
        ),
        out_shape=[shape((rows, D), bf16)]
        + [shape((rows, HALF), bf16)] * 4
        + [shape((D, 3 * HALF), bf16)],
        compiler_params=params(),
        cost_estimate=cost(11),
        name="qkv_own",
    )(idx, *xs, *dys, *vectors, mine, mine, mine, recv, w_proj, positions, *tables)


def qkv_more_call(idx, prevs, globs, vectors, w, w_proj, before, far):
    rows, glob_n = 2 * ROW, 2 * globs.shape[2]
    third, glob = qkv_block(0, 4, HALF), whole_block((glob_n, HALF))
    return pl.pallas_call(
        qkv_more_body,
        grid_spec=pltpu.PrefetchScalarGridSpec(
            num_scalar_prefetch=1,
            grid=(5,),
            in_specs=[qkv_block(0, 2, D), qkv_block(2, 2, D)]
            + [whole_block(v.shape) for v in (globs, *vectors, w, w_proj)]
            + [qkv_block(0, 4, PAIR, 2)] * 2
            + [whole_block((glob_n, PAIR))] * 2,
            out_specs=[qkv_block(0, 4, D), third, third, whole_block((glob_n, D))] + [glob] * 4,
        ),
        out_shape=[shape((rows, D), bf16)]
        + [shape((rows, HALF), bf16)] * 2
        + [shape((glob_n, D), bf16)]
        + [shape((glob_n, HALF), bf16)] * 4,
        compiler_params=params(),
        cost_estimate=cost(10),
        name="qkv_more",
    )(idx, *prevs, globs, *vectors, w, w_proj, *before, *far)


def heads_beside(block_t):
    dim = lax.broadcasted_iota(jnp.int32, block_t.shape, 0)
    zero = jnp.zeros_like(block_t)
    return jnp.concatenate(
        [jnp.where(dim < HD, block_t, zero), jnp.where(dim < HD, zero, block_t)], axis=1
    )


def heads_below(block):
    dim = lax.broadcasted_iota(jnp.int32, block.shape, 1)
    zero = jnp.zeros_like(block)
    return jnp.concatenate(
        [jnp.where(dim < HD, block, zero), jnp.where(dim < HD, zero, block)], axis=0
    )


def heads_back(both):
    n = both.shape[1] // 2
    dim = lax.broadcasted_iota(jnp.int32, (PAIR, n), 0)
    return jnp.where(dim < HD, both[:, :n], both[:, n:])


def near_body(
    info,
    q_ref,
    k_ref,
    v_ref,
    dol_ref,
    kp_ref,
    vp_ref,
    kg_ref,
    vg_ref,
    glob_ref,
    cos_ref,
    sin_ref,
    cosp_ref,
    sinp_ref,
    cosg_ref,
    sing_ref,
    *rest,
):
    o_ref, dq_ref, dk_ref, dv_ref, dkp_ref, dvp_ref, dkg_ref, dvg_ref, dk_acc, dv_acc = rest
    scale = HD**-0.5
    base = info[0]
    absent = jnp.where(base == 0, f32(negative), f32(0.0))
    keys = jnp.concatenate([kp_ref[...], k_ref[...]], axis=0)
    values = jnp.concatenate([vp_ref[...], v_ref[...]], axis=0)
    keys_t = keys.T
    values_t = values.T
    gkeys, gvalues = kg_ref[...], vg_ref[...]
    glob_n = gkeys.shape[0]
    gkeys_t = gkeys.astype(f32).T.astype(bf16)
    gvalues_t = gvalues.astype(f32).T.astype(bf16)
    keys_values = jnp.concatenate([keys, values], axis=1)
    gkeys_values = jnp.concatenate([gkeys, gvalues], axis=1)
    query = (q_ref[...].astype(f32) * scale).astype(bf16)
    query_t = query.T
    dol = dol_ref[...]
    dol_t = dol.T
    two = 2 * TILE
    window = WIN + TILE
    cosine, sine = cos_ref[...], sin_ref[...]
    row = lax.broadcasted_iota(jnp.int32, (TILE, two), 0)
    lane = lax.broadcasted_iota(jnp.int32, (TILE, two), 1) % TILE
    glane = lax.broadcasted_iota(jnp.int32, (glob_n, two), 1) % TILE
    gpos = jnp.concatenate([glob_ref[0], glob_ref[0]], axis=1)
    dkg = jnp.zeros((glob_n, PAIR), f32)
    dvg = jnp.zeros((glob_n, PAIR), f32)
    kk, vv = [None] * 8, [None] * 8
    for t in range(ROW // TILE):
        rows = slice(t * TILE, (t + 1) * TILE)
        span = slice(t * TILE, t * TILE + window)
        cut = WIN - t * TILE
        q_beside = heads_beside(query_t[:, rows])
        d_beside = heads_beside(dol_t[:, rows])
        q_below = heads_below(query[rows])
        d_below = heads_below(dol[rows])
        blank = jnp.zeros_like(q_beside)
        right = jnp.concatenate(
            [
                jnp.concatenate([q_beside, blank], axis=1),
                jnp.concatenate([blank, d_beside], axis=1),
            ],
            axis=0,
        )
        both = dot(keys_values[span], right)
        far_both = dot(gkeys_values, right)
        score, d_prob = both[:, :two], both[:, two:]
        far, d_far = far_both[:, :two], far_both[:, two:]
        parts = [
            jnp.where(row > lane, score[:TILE] + absent, negative),
        ]
        if cut > TILE:
            parts.append(score[TILE:cut] + absent)
        parts.append(score[cut:WIN])
        if t == 0:
            parts.pop()
        parts.append(jnp.where(row <= lane, score[WIN:], negative))
        score = jnp.concatenate(parts, axis=0)
        far = jnp.where(base + t * TILE + glane - gpos >= WIN, far, negative)
        top = jnp.maximum(
            jnp.max(score, axis=0, keepdims=True), jnp.max(far, axis=0, keepdims=True)
        )
        prob = jnp.exp(score - top)
        far_prob = jnp.exp(far - top)
        total = jnp.sum(prob, axis=0, keepdims=True) + jnp.sum(far_prob, axis=0, keepdims=True)
        delta = jnp.sum(prob * d_prob, axis=0, keepdims=True) + jnp.sum(
            far_prob * d_far, axis=0, keepdims=True
        )
        inverse = 1.0 / total
        delta = delta * inverse
        prob = prob * inverse
        far_prob = far_prob * inverse
        low, far_low = prob.astype(bf16), far_prob.astype(bf16)
        d_score = (prob * (d_prob - delta)).astype(bf16)
        d_far = (far_prob * (d_far - delta)).astype(bf16)
        out_t = dot(values_t[:, span], low) + dot(gvalues_t, far_low)
        o_ref[rows, :] = heads_back(out_t).T.astype(bf16)
        dq_t = dot(keys_t[:, span], d_score) + dot(gkeys_t, d_far)
        dq = heads_back(dq_t).T * scale
        dq_ref[rows, :] = rotated(dq, cosine[rows], sine[rows], -1.0).astype(bf16)
        tk, tv = dot(d_score, q_below), dot(low, d_below)
        for b in range(5):
            bk, bv = tk[b * TILE : (b + 1) * TILE], tv[b * TILE : (b + 1) * TILE]
            kk[t + b] = bk if kk[t + b] is None else kk[t + b] + bk
            vv[t + b] = bv if vv[t + b] is None else vv[t + b] + bv
        dkg = dkg + dot(d_far, q_below)
        dvg = dvg + dot(far_low, d_below)
    for b in range(8):
        dk_acc[b * TILE : (b + 1) * TILE, :] = kk[b]
        dv_acc[b * TILE : (b + 1) * TILE, :] = vv[b]
    dk_ref[...] = dk_acc[ROW:, :]
    dv_ref[...] = dv_acc[ROW:, :]
    dkp_ref[...] = rotated(dk_acc[:ROW, :], cosp_ref[...], sinp_ref[...], -1.0).astype(bf16)
    dvp_ref[...] = dv_acc[:ROW, :].astype(bf16)
    dkg_ref[...] = rotated(dkg, cosg_ref[...], sing_ref[...], -1.0).astype(bf16)
    dvg_ref[...] = dvg.astype(bf16)


def near_call(info, j, q, k, v, dol, k2, v2, kg, vg, glob_wide, tables, before, far):
    glob_n = glob_wide.shape[1]
    own = pl.BlockSpec((ROW, PAIR), lambda h, info: (j, h))
    glob = pl.BlockSpec((glob_n, PAIR), lambda h, info: (j, h))
    table = pl.BlockSpec((ROW, PAIR), lambda h, info: (0, 0))
    gtable = pl.BlockSpec((glob_n, PAIR), lambda h, info: (j, 0))
    own_out = pl.BlockSpec((ROW, PAIR), lambda h, info: (0, h))
    glob_out = pl.BlockSpec((glob_n, PAIR), lambda h, info: (0, h))
    own_low, own_high = shape((ROW, HALF), bf16), shape((ROW, HALF), f32)
    glob_low = shape((glob_n, HALF), bf16)
    return pl.pallas_call(
        near_body,
        grid_spec=pltpu.PrefetchScalarGridSpec(
            num_scalar_prefetch=1,
            grid=(PAIRS,),
            in_specs=[own] * 6
            + [glob] * 2
            + [pl.BlockSpec((1, glob_n, PAIR), lambda h, info: (j, 0, 0))]
            + [table] * 4
            + [gtable] * 2,
            out_specs=[own_out] * 6 + [glob_out] * 2,
            scratch_shapes=[pltpu.VMEM((2 * ROW, PAIR), f32)] * 2,
        ),
        out_shape=[own_low, own_low, own_high, own_high, own_low, own_low, glob_low, glob_low],
        compiler_params=params(),
        cost_estimate=cost(17.5),
        name="near",
    )(info, q, k, v, dol, k2, v2, kg, vg, glob_wide, *tables, *before, *far)


def glob_first_body(info, qg_ref, k_ref, v_ref, glob_ref, out_ref):
    glob_n = qg_ref.shape[0]
    key_pos = info[0] + lax.broadcasted_iota(jnp.int32, (ROW, 2 * glob_n), 0)
    mask = key_pos <= glob_ref[0][0:1]
    lane = lax.broadcasted_iota(jnp.int32, (HD, 2 * glob_n), 1)
    for h in range(HALF // PAIR):
        lanes = slice(h * PAIR, (h + 1) * PAIR)
        query = qg_ref[:, lanes].astype(f32) * HD**-0.5
        beside = heads_beside(query.T).astype(bf16)
        masked = jnp.where(mask, dot(k_ref[:, lanes], beside), negative)
        top = jnp.max(masked, axis=0, keepdims=True)
        prob = jnp.where(mask, jnp.exp(masked - top), 0.0)
        total = jnp.sum(prob, axis=0, keepdims=True)
        both = dot(v_ref[:, lanes].T, prob.astype(bf16))
        out_ref[h, 0:HD, :] = jnp.where(lane < glob_n, both[:HD], both[HD:])
        out_ref[h, HD : HD + 1, :] = top
        out_ref[h, HD + 1 : HD + 2, :] = total
        out_ref[h, HD + 2 : HD + 8, :] = jnp.zeros((6, 2 * glob_n), f32)


def glob_first_call(info, qg, k, v, glob_row):
    glob_n = glob_row.shape[2] // 2
    own = pl.BlockSpec((ROW, HALF), lambda j, info: (j, 0))
    pairs = HALF // PAIR
    return pl.pallas_call(
        glob_first_body,
        grid_spec=pltpu.PrefetchScalarGridSpec(
            num_scalar_prefetch=1,
            grid=(2,),
            in_specs=[
                pl.BlockSpec((glob_n, HALF), lambda j, info: (j, 0)),
                own,
                own,
                pl.BlockSpec((1, 8, 2 * glob_n), lambda j, info: (j, 0, 0)),
            ],
            out_specs=pl.BlockSpec((pairs, HD + 8, 2 * glob_n), lambda j, info: (j, 0, 0)),
        ),
        out_shape=shape((2 * pairs, HD + 8, 2 * glob_n), f32),
        compiler_params=params(),
        cost_estimate=cost(4),
        name="glob_first",
    )(info, qg, k, v, glob_row)


def merged(first, second):
    top_a, top_b = first[:, HD : HD + 1], second[:, HD : HD + 1]
    top = jnp.maximum(top_a, top_b)
    weight_a, weight_b = jnp.exp(top_a - top), jnp.exp(top_b - top)
    total = first[:, HD + 1 : HD + 2] * weight_a + second[:, HD + 1 : HD + 2] * weight_b
    out = first[:, :HD] * weight_a + second[:, :HD] * weight_b
    return jnp.concatenate([out, top, total, first[:, HD + 2 :]], axis=1)


def glob_second_body(
    info,
    qg_ref,
    dolg_ref,
    k_ref,
    v_ref,
    glob_ref,
    cos_ref,
    sin_ref,
    cosg_ref,
    sing_ref,
    *rest,
):
    near, rest = rest[:6], rest[6:]
    stat_refs, (o_ref, dk_ref, dv_ref, dqg_ref) = rest[:-4], rest[-4:]
    first = pl.program_id(0) == 0
    scale = HD**-0.5
    glob_n = qg_ref.shape[0]
    key_pos = info[0] + lax.broadcasted_iota(jnp.int32, (ROW, 2 * glob_n), 0)
    positions = glob_ref[0][0:1]
    mask = key_pos <= positions
    place = (key_pos[:, :glob_n] == positions[:, :glob_n]).astype(f32)
    hit = jnp.sum(place, axis=1, keepdims=True) > 0.0
    place = place.astype(bf16)
    cosine, sine = cos_ref[...], sin_ref[...]
    cosine_g, sine_g = cosg_ref[...], sing_ref[...]
    for h in range(HALF // PAIR):
        lanes = slice(h * PAIR, (h + 1) * PAIR)
        keys, values = k_ref[:, lanes], v_ref[:, lanes]
        query = qg_ref[:, lanes].astype(f32) * scale
        q_beside = heads_beside(query.T).astype(bf16)
        q_below = heads_below(query.astype(bf16))
        dol = dolg_ref[:, lanes]
        dol_t = dol.astype(f32).T
        d_beside = heads_beside(dol_t).astype(bf16)
        d_below = heads_below(dol)
        tops = [ref[h, HD : HD + 1, :] for ref in stat_refs]
        top = functools.reduce(jnp.maximum, tops)
        weights = [jnp.exp(part - top) for part in tops]
        total = sum(w * ref[h, HD + 1 : HD + 2, :] for w, ref in zip(weights, stat_refs))
        out_t = sum(w * ref[h, 0:HD, :] for w, ref in zip(weights, stat_refs)) * (1.0 / total)
        lse = top + jnp.log(total)
        delta = jnp.sum(
            out_t * jnp.concatenate([dol_t[:HD], dol_t[HD:]], axis=1), axis=0, keepdims=True
        )
        score = jnp.where(mask, dot(keys, q_beside), negative)
        prob = jnp.where(mask, jnp.exp(score - lse), 0.0)
        d_score = (prob * (dot(values, d_beside) - delta)).astype(bf16)
        near_o, near_dk, near_dv = (
            jnp.where(first, near[i][:, lanes], near[i + 1][:, lanes]) for i in (0, 2, 4)
        )
        dk = near_dk + dot(d_score, q_below)
        dv = near_dv + dot(prob.astype(bf16), d_below)
        dk_ref[:, lanes] = rotated(dk, cosine, sine, -1.0).astype(bf16)
        dv_ref[:, lanes] = dv.astype(bf16)
        dq_both = dot(keys.T, d_score)
        dq_t = jnp.concatenate([dq_both[:HD, :glob_n], dq_both[HD:, glob_n:]], axis=0)
        dqg_ref[:, lanes] = rotated(dq_t.T * scale, cosine_g, sine_g, -1.0).astype(bf16)
        rows = jnp.concatenate([out_t[:, :glob_n], out_t[:, glob_n:]], axis=0).T.astype(bf16)
        o_ref[:, lanes] = jnp.where(hit, dot(place, rows).astype(bf16), near_o)


def glob_second_call(info, qg, dolg, k, v, stats, glob_row, near, tables, far):
    glob_n = glob_row.shape[2] // 2
    pairs = HALF // PAIR
    rows = k.shape[0]
    own = pl.BlockSpec((ROW, HALF), lambda j, info: (j, 0))
    glob = pl.BlockSpec((glob_n, HALF), lambda j, info: (j, 0))
    table = pl.BlockSpec((ROW, PAIR), lambda j, info: (0, 0))
    gtable = pl.BlockSpec((glob_n, PAIR), lambda j, info: (j, 0))
    return pl.pallas_call(
        glob_second_body,
        grid_spec=pltpu.PrefetchScalarGridSpec(
            num_scalar_prefetch=1,
            grid=(2,),
            in_specs=[
                glob,
                glob,
                own,
                own,
                pl.BlockSpec((1, 8, 2 * glob_n), lambda j, info: (j, 0, 0)),
                table,
                table,
                gtable,
                gtable,
            ]
            + [pl.BlockSpec((ROW, HALF), lambda j, info: (0, 0))] * 6
            + [pl.BlockSpec((pairs, HD + 8, 2 * glob_n), lambda j, info: (j, 0, 0))] * len(stats),
            out_specs=[own, own, own, glob],
        ),
        out_shape=[shape((rows, HALF), bf16)] * 3 + [shape((2 * glob_n, HALF), bf16)],
        compiler_params=params(),
        cost_estimate=cost(8),
        name="glob_second",
    )(info, qg, dolg, k, v, glob_row, *tables, *far, *near, *stats)


def weights_body(tiles, idx, *refs):
    core, two = idx[0], idx[2]

    def run(at, ref):
        for tile in (at, at + 1):
            kind, operands = tiles[tile]
            if kind == "rows":
                total = sum(dot_tn(refs[left][...], refs[right][...]) for left, right in operands)
                total = total.astype(bf16)
                for r in range(2):
                    ref[place_of(two, r), tile, :, :] = total[:, r * HALF : (r + 1) * HALF]
                continue
            for m in range(2):
                total = None
                for left, right in operands:
                    term = dot_tn(refs[left + m][...], refs[right][...])
                    total = term if total is None else total + term
                spread_rows(ref, tile, total.astype(bf16), m, core, two, slice(None))

    for at in range(0, len(tiles), 2):
        for half in range(2):

            @pl.when(pl.program_id(0) == at + half)
            def _(at=at, half=half):
                run(at, refs[len(refs) - 2 + half])


def weights_call(idx, tiles):
    specs, operands, table, lefts = [], [], [], {}

    def add(array, spec):
        specs.append(spec)
        operands.append(array)
        return len(operands) - 1

    def whole(array):
        return add(array, pl.BlockSpec(array.shape, lambda s, idx: (0, 0)))

    def part(s, idx):
        return idx[1] ^ (1 - s % 2)

    def left_of(array, rows, j):
        if (id(array), rows, j) not in lefts:
            specs = [
                pl.BlockSpec((rows, 256), lambda s, idx, m=m: (j, 2 * m + part(s, idx)))
                for m in range(2)
            ]
            lefts[id(array), rows, j] = [add(array, spec) for spec in specs][0]
        return lefts[id(array), rows, j]

    for kind, products in tiles:
        if kind == "rows":
            pairs = []
            for j, (left, right) in enumerate(products):
                spec = pl.BlockSpec((right.shape[0], 256), lambda s, idx, j=j: (j, part(s, idx)))
                pairs.append((add(left, spec), whole(right)))
        else:
            pairs = []
            for left, *rights in products:
                for j, right in enumerate(rights):
                    pairs.append((left_of(left, right.shape[0], j), whole(right)))
        table.append((kind, tuple(pairs)))
    count = len(tiles)
    out = pl.BlockSpec((2, count, 256, 512), lambda s, idx: (0, 0, 0, 0))
    return pl.pallas_call(
        functools.partial(weights_body, tuple(table)),
        grid_spec=pltpu.PrefetchScalarGridSpec(
            num_scalar_prefetch=1, grid=(count,), in_specs=specs, out_specs=[out] * 2
        ),
        out_shape=[shape((2, count, 256, 512), bf16)] * 2,
        compiler_params=params(),
        cost_estimate=cost(16),
        name="weight_grads",
    )(idx, *operands)


def input_body(idx, *refs):
    x_ref, xo_ref, xp_ref, xop_ref, glob_ref = refs[:5]
    vecs, core = refs[5:7], idx[0]
    w_ref, up_mine, up_recv = refs[7:10]
    dqs, dk1, dv1, dkps, dvps, dqg = refs[10:12], refs[12], refs[13], refs[14:16], refs[16:18], refs[18]
    dkgs, dvgs, dup_ref = refs[19:21], refs[21:23], refs[23]
    mine, other, sums_a, sums_m, bias_ref, wu_ref = refs[24:]
    step = pl.program_id(0)

    @pl.when(step == 0)
    def _():
        sums_a[...] = jnp.zeros_like(sums_a)
        sums_m[...] = jnp.zeros_like(sums_m)
        bias_ref[...] = jnp.zeros_like(bias_ref)
        wu_ref[rows_of(idx[0]), :] = up_mine[...]
        wu_ref[rows_of(1 - idx[0]), :] = up_recv[...]

    def gather(sums, grad, normal):
        sums[0:1, :] += jnp.sum(grad * normal, axis=0, keepdims=True)
        sums[1:2, :] += jnp.sum(grad, axis=0, keepdims=True)

    def attn(x, parts):
        grad = None
        for t, part in enumerate(parts):
            if part is None:
                continue
            lanes = slice(t * HALF, (t + 1) * HALF)
            term = dot_nt(part, w_ref[:, lanes])
            grad = term if grad is None else grad + term
            bias_ref[0:1, lanes] += jnp.sum(part.astype(f32), axis=0, keepdims=True)
        normal, _ = norm_parts(x.astype(f32))
        gather(sums_a, grad, normal)
        return grad * vector(vecs, core, 0), normal

    def own_rows(x, dq, out):
        g, normal = attn(x[...], (dq[...], dk1[...], dv1[...]))
        grad = dot_nt(dup_ref[...], wu_ref[...])
        gather(sums_m, grad, normal)
        out[...] = (g + grad * vector(vecs, core, 2)).astype(bf16)

    @pl.when(step < 2)
    def _():
        own_rows(x_ref, dqs[0], mine)

    @pl.when((step >= 2) & (step < 4))
    def _():
        own_rows(xo_ref, dqs[1], other)

    @pl.when((step >= 4) & (step < 6))
    def _():
        mine[...] = attn(xp_ref[...], (None, dkps[0][...], dvps[0][...]))[0].astype(bf16)

    @pl.when((step >= 6) & (step < 8))
    def _():
        other[...] = attn(xop_ref[...], (None, dkps[1][...], dvps[1][...]))[0].astype(bf16)

    @pl.when(step == 8)
    def _():
        rows = jnp.concatenate([glob_ref[0, 0], glob_ref[1, 0]], axis=0)
        dkg, dvg = (jnp.concatenate([v[0][...], v[1][...]], axis=0) for v in (dkgs, dvgs))
        grad = attn(rows, (dqg[...], dkg, dvg))[0].astype(bf16)
        glob_n = glob_ref.shape[2]
        mine[:glob_n, :] = grad[:glob_n]
        other[:glob_n, :] = grad[glob_n:]


def input_call(idx, xs, prevs, globs, vectors, w_qkv, up_mine, up_recv, grads):
    step, rows, glob_n = 256, 2 * ROW, 2 * globs.shape[2]
    part = pl.BlockSpec((2, 1, *globs.shape[2:]), lambda i, idx: (0, 0, 0, 0))

    def mine_at(i):
        return jnp.where(i < 4, jnp.minimum(i, 1), jnp.where(i < 8, jnp.minimum(i - 2, 3), 4))

    def other_at(i):
        return jnp.where(i < 6, clamped(i, 2, 2), jnp.where(i < 8, i - 4, 4))


    def block(low, count, width):
        return pl.BlockSpec((step, width), lambda i, idx: (clamped(i, low, count), 0))

    whole = lambda rows, width: pl.BlockSpec((rows, width), lambda i, idx: (0, 0))
    return pl.pallas_call(
        input_body,
        grid_spec=pltpu.PrefetchScalarGridSpec(
            num_scalar_prefetch=1,
            grid=(9,),
            in_specs=[block(2 * j, 2, D) for j in range(4)]
            + [part]
            + [whole(*v.shape) for v in vectors]
            + [whole(*w_qkv.shape)]
            + [
                pl.BlockSpec((HALF, FF // 2), lambda i, idx: (0, idx[0])),
                whole(HALF, FF // 2),
            ]
            + [block(0, 2, HALF), block(2, 2, HALF)]
            + [block(0, 4, HALF)] * 2
            + [block(4, 2, HALF), block(6, 2, HALF)] * 2
            + [whole(glob_n, HALF)]
            + [whole(glob_n // 2, HALF)] * 4
            + [block(0, 4, FF // 2)],
            out_specs=[
                pl.BlockSpec((step, D), lambda i, idx: (mine_at(i), 0)),
                pl.BlockSpec((step, D), lambda i, idx: (other_at(i), 0)),
                whole(8, D),
                whole(8, D),
                whole(8, 3 * HALF),
            ],
            scratch_shapes=[pltpu.VMEM((D, FF // 2), bf16)],
        ),
        out_shape=[shape((rows + step, D), bf16)] * 2
        + [
            shape((8, D), f32),
            shape((8, D), f32),
            shape((8, 3 * HALF), f32),
        ],
        compiler_params=params(),
        cost_estimate=cost(24),
        name="input_grads",
    )(
        idx,
        *xs,
        *prevs,
        globs,
        *vectors,
        w_qkv,
        up_mine,
        up_recv,
        *grads,
    )


def result_body(act_ref, wd_ref, ol_ref, wp_ref, mine_ref, other_ref):
    part = (dot(act_ref[...], wd_ref[...]) + dot(ol_ref[...], wp_ref[...])).astype(bf16)
    half = pl.num_programs(0) // 2

    @pl.when(pl.program_id(0) < half)
    def _():
        mine_ref[...] = part

    @pl.when(pl.program_id(0) >= half)
    def _():
        other_ref[...] = part


def result_call(act, w_down, ol, w_proj):
    rows, step = act.shape[0], 256
    half = rows // step // 2
    return pl.pallas_call(
        result_body,
        grid=(rows // step,),
        in_specs=[
            pl.BlockSpec((step, act.shape[1]), lambda i: (i, 0)),
            pl.BlockSpec(w_down.shape, lambda i: (0, 0)),
            pl.BlockSpec((step, HALF), lambda i: (i, 0)),
            pl.BlockSpec(w_proj.shape, lambda i: (0, 0)),
        ],
        out_specs=[
            pl.BlockSpec((step, D), lambda i: (jnp.minimum(i, half - 1), 0)),
            pl.BlockSpec((step, D), lambda i: (jnp.maximum(i - half, 0), 0)),
        ],
        out_shape=[shape((rows // 2, D), bf16)] * 2,
        compiler_params=params(),
        cost_estimate=cost(10.3),
        name="result",
    )(act, w_down, ol, w_proj)


def place_body(spreads, rows, n_alias, idx, *refs):
    pieces, swapped = refs[:4], refs[4]
    outs = list(refs[5 + n_alias :])
    spread_out, rows_out = outs[0], outs[1]
    one, two = idx[1], idx[2]
    for i in range(max(len(spreads), len(rows))):
        for h in range(2):

            @pl.when((pl.program_id(0) == i) & (pl.program_id(1) == h))
            def _(i=i, h=h):
                if i < len(spreads):
                    for k in range(4):
                        if h:
                            block = 2 * (two ^ (k // 2)) + (one ^ (k % 2))
                            part = swapped[4 * i + k]
                        else:
                            block = 2 * (one ^ (k // 2)) + (two ^ (k % 2))
                            part = pieces[k][spreads[i], TILE:, :]
                        spread_out[pl.ds(pl.multiple_of(block * TILE, TILE), TILE), :] = (
                            part.astype(f32)
                        )
                if i < len(rows):
                    for beside in range(2):
                        part = pieces[2 * h + beside][rows[i]]
                        rows_out[:, lanes_of(two ^ beside, HALF)] = part.astype(f32)


def place_call(idx, work, spreads, rows, spread_target, rows_target):
    targets = [spread_target, rows_target]
    alias = [buf for buf, _, _ in targets if buf is not None]
    aliases, at = {}, 6
    for out, (buf, _, _) in enumerate(targets):
        if buf is not None:
            aliases[at] = out
            at += 1

    def spread_index(i, h, idx):
        return 0, spread_target[2](i, idx[0] ^ h)

    def rows_index(i, h, idx):
        last = len(rows) - 1
        i, h = jnp.where(i > last, last, i), jnp.where(i > last, 1, h)
        return rows_target[2](i, idx[1] ^ h), 0

    whole = lambda array: pl.BlockSpec(array.shape, lambda i, h, idx: (0, 0, 0))
    operands = [*work.pieces, work.swapped]
    return pl.pallas_call(
        functools.partial(place_body, spreads, rows, len(alias)),
        grid_spec=pltpu.PrefetchScalarGridSpec(
            num_scalar_prefetch=1,
            grid=(len(spreads), 2),
            in_specs=[whole(array) for array in operands]
            + [pl.BlockSpec(memory_space=pl.ANY)] * len(alias),
            out_specs=[pl.BlockSpec((HALF, 512), spread_index), pl.BlockSpec((256, D), rows_index)],
        ),
        out_shape=[shape(dims, f32) for _, dims, _ in targets],
        input_output_aliases=aliases,
        compiler_params=params(),
        cost_estimate=cost(7.0),
        name="place",
    )(idx, *operands, *alias)


def rotary_tables(positions):
    lane = jnp.arange(PAIR, dtype=jnp.int32) % HD
    half = ROT // 2
    freqs = rotary_base ** (-2.0 * (lane % half).astype(f32) / ROT)
    angles = positions.astype(f32)[:, None] * freqs[None, :]
    active = (lane < ROT)[None, :]
    sign = jnp.where(lane < half, -1.0, 1.0)[None, :]
    return jnp.where(active, jnp.cos(angles), 1.0), jnp.where(active, jnp.sin(angles) * sign, 0.0)


def per_device(
    tokens,
    cotangent,
    global_pos,
    attn_gain,
    attn_shift,
    mlp_gain,
    mlp_shift,
    qkv_weight,
    qkv_bias,
    proj_weight,
    proj_bias,
    up_weight,
    up_bias,
    down_weight,
    down_bias,
):
    n_ctx = lax.axis_size("ctx")
    core = lax.axis_index("fsdp")
    seq = lax.axis_index("seq")
    ctx = lax.axis_index("ctx")
    x_bit, y_bit = seq & 1, seq >> 1
    base = ctx * ROW
    own_x = tokens[0]
    own_dy = cotangent[0]
    glob_n = global_pos.shape[1]
    share = glob_n // n_ctx
    info = jnp.stack([base]).astype(jnp.int32)
    one, two = jnp.where(core == 0, x_bit, y_bit), jnp.where(core == 0, y_bit, x_bit)
    idx = jnp.stack([core, one, two, ctx]).astype(jnp.int32)
    order = Order()

    other_x = pair(own_x)
    up_recv = pair(slice_call(idx, up_weight, FF // 2))
    other_dy = pair(own_dy)
    mine = vectors_call(
        global_pos, attn_gain, attn_shift, mlp_gain, mlp_shift, proj_bias, down_bias, qkv_bias
    )
    vectors = (mine, pair(mine))
    row_pos = base + jnp.arange(ROW, dtype=jnp.int32)
    own_glob = lax.dynamic_slice_in_dim(global_pos[0], ctx * share, share, 0)
    pick = (own_glob[:, None] == row_pos[None, :]).astype(bf16)
    picked = jnp.stack([dot(pick, own_x), dot(pick, own_dy)]).astype(bf16)
    picked = jnp.stack([picked, pair(picked)])[None]
    pos_pair = jnp.concatenate([v[9:10, :glob_n] for v in vectors]).astype(jnp.int32)
    bias_up = up_bias.astype(f32).reshape(1, FF // 2)
    tables = rotary_tables(row_pos)
    before = rotary_tables(row_pos - ROW)
    far = rotary_tables(pos_pair.reshape(-1))
    glob_row = jnp.broadcast_to(
        jnp.concatenate([pos_pair, pos_pair], axis=1)[:, None, :], (2, 8, 2 * glob_n)
    )
    glob_wide = jnp.broadcast_to(pos_pair[:, :, None], (2, glob_n, PAIR))
    tables, before, far, glob_row, glob_wide, picked, first_x = lax.optimization_barrier(
        (tables, before, far, glob_row, glob_wide, picked, own_x)
    )
    prev_x = shifted(first_x, 1)
    picks, distances = [picked], doubling("ctx")
    beside = exchange(picked, "ctx", distances[0])

    xs, dys = (own_x, other_x), (own_dy, other_dy)
    a_mlp, send, keep, act, dup, sums = unit_call(
        idx,
        0,
        (first_x, other_x, vectors),
        dys,
        up_weight,
        up_recv,
        down_weight,
        bias_up,
        None,
    )
    order.mark(sums)
    up_sums = [sums.reshape(2, 512)]
    work0 = Reduction(order, idx, send, keep, True)
    prev_x, beside = order.land(prev_x, beside)
    other_prev = pair(prev_x)
    picks.append(beside)
    for distance in distances[1:]:
        picked = order.mark(jnp.concatenate(picks, axis=0))
        picks.append(exchange(picked, "ctx", distance))
    w_in = order.gate(qkv_weight)
    w_in = order.mark(
        jnp.concatenate(
            [
                lax.dynamic_slice_in_dim(w_in, (2 * t + 1 - core) * HALF, HALF, 1)
                for t in range(3)
            ],
            axis=1,
        )
    )
    qkv_recv = pair(w_in)
    send, keep, act, dup, sums = unit_call(
        idx,
        2,
        order.gate(a_mlp),
        dys,
        up_weight,
        up_recv,
        down_weight,
        bias_up,
        (act, dup),
    )
    order.mark(sums)
    up_sums.append(sums.reshape(2, 512))
    qkv_recv, other_prev = order.land(qkv_recv, other_prev)
    prevs = (prev_x, other_prev)
    if n_ctx == 4:
        globs = collect_call(idx, *order.gate(*picks))
    else:
        picked = jnp.concatenate(picks, axis=0)
        picked = jnp.take(picked, jnp.arange(n_ctx, dtype=jnp.int32) ^ ctx, axis=0)
        globs = jnp.transpose(picked, (1, 2, 0, 3, 4)).reshape(2, 2, glob_n, D)
    order.mark(globs)
    work0.second()

    a1, q1, k1, v1, dol, w_qkv = qkv_own_call(
        idx,
        (order.gate(own_x), other_x),
        dys,
        vectors,
        qkv_weight,
        qkv_recv,
        proj_weight,
        pos_pair,
        tables,
    )
    order.mark(dol)
    work0.over_ctx()
    work1 = Reduction(order, idx, order.gate(send), keep, True)
    a2, k2, v2, a3, q3, k3, v3, dolg = qkv_more_call(
        idx, (order.gate(prev_x), other_prev), globs, vectors, w_qkv, proj_weight, before, far
    )
    order.mark(q3)
    stats = order.mark(glob_first_call(info, q3, k1, v1, glob_row))
    beside = exchange(stats, "ctx", 1)
    work1.second()

    def near_of(j):
        outs = near_call(
            info, j, order.gate(q1), k1, v1, dol, k2, v2, k3, v3, glob_wide, tables, before, far
        )
        order.mark(outs[-1])
        return outs

    near0 = near_of(0)
    for distance in distances[1:]:
        stats = order.mark(merged(*order.gate(stats, beside)))
        beside = exchange(stats, "ctx", distance)
    work0.ctx_sum()
    near1 = near_of(1)
    stats = order.land(stats, beside)
    work0.regroup()
    work1.over_ctx()
    work0.to_beside()
    work0.to_across()
    near, dqs, dks, dvs, dkps, dvps, dkgs, dvgs = zip(near0, near1)
    ol, dk1, dv1, dqg = glob_second_call(
        info,
        order.gate(q3),
        dolg,
        k1,
        v1,
        stats,
        glob_row,
        (*near, *dks, *dvs),
        tables,
        far,
    )
    order.mark(dqg)
    send, keep = weights_call(
        idx,
        (
            ("spread", ((a1, order.gate(dv1)), (a2, *dvps), (a3, *dvgs))),
            ("rows", ((ol, own_dy), (ol, other_dy))),
            ("spread", ((a1, *dqs), (a3, dqg))),
            ("spread", ((a1, dk1), (a2, *dkps), (a3, *dkgs))),
        ),
    )
    order.mark(send)
    work2 = Reduction(order, idx, send, keep, False)
    work0.beside, work0.across = order.land(work0.beside, work0.across)
    work1.ctx_sum()

    g_mine, g_other, sums_a, sums_m, bias = input_call(
        idx,
        (order.gate(own_x), other_x),
        prevs,
        globs,
        vectors,
        w_qkv,
        up_weight,
        up_recv,
        (*dqs, dk1, dv1, *dkps, *dvps, dqg, *dkgs, *dvgs, dup),
    )
    order.mark(bias)
    work2.second()
    work1.regroup()
    work0.to_both()
    part, part_other = result_call(order.gate(act), down_weight, ol, proj_weight)
    order.mark(part)
    work2.over_ctx()
    work1.to_beside()
    g_beside = pair(order.gate(g_other))
    work2.ctx_half()
    prev_mine, glob_mine, g_beside = order.gate(
        g_mine[ROW : 2 * ROW], g_mine[2 * ROW : 2 * ROW + glob_n], g_beside
    )
    glob_sum = order.mark(added(glob_mine, g_beside[2 * ROW : 2 * ROW + glob_n]))
    prev_sum = order.mark(added(prev_mine, g_beside[ROW : 2 * ROW]))
    part_beside = pair(order.gate(part_other))
    work0.swap([0, 2])
    work2.ctx_sum()

    def place_units(work, first, up_out, down_out):
        up_out, down_out = place_call(
            idx,
            work,
            (0, 2),
            (1, 3),
            (up_out, (HALF, FF), lambda i, c: c * 4 + first + i),
            (down_out, (FF // 2, D), lambda i, p: (first + i) * 2 + p),
        )
        order.mark(up_out[:8, :128])
        return up_out, down_out

    own, part, part_beside = order.gate(own_x, part, part_beside)
    result = own.astype(f32) + part.astype(f32) + part_beside.astype(f32)
    first = core == 0
    for i in (4, 5):
        rows = [v[i : i + 1] for v in vectors]
        result = result + jnp.concatenate(
            [jnp.where(first, rows[0], rows[1]), jnp.where(first, rows[1], rows[0])], axis=1
        )
    layer_out = order.mark(result.astype(bf16))[None]
    beside = exchange(order.gate(glob_sum), "ctx", 1)
    up_out, down_out = place_units(work0, 0, None, None)
    work1.beside = order.land(work1.beside)
    work1.to_across()
    work2.ctx_rest()
    for distance in doubling("ctx")[1:]:
        glob_sum = order.mark(added(*order.gate(glob_sum, beside)))
        beside = exchange(glob_sum, "ctx", distance)

    dy_sum = jnp.sum(order.gate(own_dy).astype(f32), axis=0)
    qkv_sum = bias[0].reshape(3, 1, HALF)
    mine = jnp.arange(2, dtype=jnp.int32)[None, :, None] == core
    qkv_sum = jnp.where(mine, qkv_sum, 0.0).reshape(2, 3, 512)
    split = jnp.concatenate(
        [
            sums_a[:2].reshape(2, 2, 512).swapaxes(0, 1),
            sums_m[:2].reshape(2, 2, 512).swapaxes(0, 1),
            dy_sum.reshape(2, 1, 512),
            qkv_sum,
        ],
        axis=1,
    )
    kept = lax.dynamic_index_in_dim(split, core, 0, False)
    given = pair(order.mark(lax.dynamic_index_in_dim(split, 1 - core, 0, False)))
    work1.to_both()
    work2.regroup()
    work2.to_beside()
    work2.to_across()
    kept, given = order.gate(kept, given)
    total = order.mark(jnp.concatenate([kept + given] + up_sums, axis=0))
    steps = [(axis, distance) for axis in ("seq", "ctx") for distance in doubling(axis)]
    glob_sum, beside = order.gate(glob_sum, beside)
    glob_sum = order.mark(added(glob_sum, beside))
    from_prev = shifted(order.gate(prev_sum), -1)
    work1.swap([0, 2])
    work2.to_both()
    up_out, down_out = place_units(work1, 2, up_out, down_out)
    for step in steps[:-2]:
        total = order.mark(total + order.gate(exchange(total, *step)))
    place = (row_pos[:, None] == global_pos[0][None, :]).astype(bf16)
    own, mine, g_beside, from_prev, glob_sum = order.gate(
        own_x, g_mine, g_beside, from_prev, glob_sum
    )
    g = (
        mine[:ROW].astype(f32)
        + g_beside[:ROW].astype(f32)
        + from_prev.astype(f32)
        + dot(place, glob_sum)
    )
    normal, inverse = norm_parts(own.astype(f32))
    lower = inverse * (
        g
        - jnp.mean(g, axis=-1, keepdims=True)
        - normal * jnp.mean(g * normal, axis=-1, keepdims=True)
    )
    tokens_grad = order.mark(own_dy.astype(f32) + lower)[None]
    for step in steps[-2:]:
        total = order.mark(total + order.gate(exchange(total, *step)))
    work2.swap([0, 2, 3])
    qkv_out, proj_out = place_call(
        idx,
        work2,
        (0, 2, 3),
        (1,),
        (None, (HALF, 3 * D), lambda i, c: 2 * ((i + 2) % 3) + c),
        (None, (HALF, D), lambda i, p: p),
    )
    return (
        layer_out,
        tokens_grad,
        total[0],
        total[1],
        total[2],
        total[3],
        qkv_out,
        total[5:8].reshape(-1),
        proj_out,
        total[4],
        up_out,
        total[8:12].reshape(-1),
        down_out,
        total[4],
    )


def solution(mesh):
    rows = P(("seq", "fsdp"), "ctx", None)
    vector, matrix = P("fsdp"), P("fsdp", None)
    return jax.shard_map(
        per_device,
        mesh=mesh,
        in_specs=(
            rows,
            rows,
            P(("seq", "fsdp"), None),
            vector,
            vector,
            vector,
            vector,
            matrix,
            vector,
            matrix,
            vector,
            matrix,
            vector,
            matrix,
            vector,
        ),
        out_specs=(
            rows,
            rows,
            vector,
            vector,
            vector,
            vector,
            matrix,
            vector,
            matrix,
            vector,
            matrix,
            vector,
            matrix,
            vector,
        ),
        check_vma=False,
    )
```

```python
import functools
import math

import jax
import jax.numpy as jnp
from jax import lax
from jax.experimental import pallas as pl
from jax.experimental.pallas import tpu as pltpu
from jax.sharding import PartitionSpec as P

D = 1024
H = 16
HD = 64
ROT = 16
WIN = 512
FF = 4096
HALF = D // 2
PAIR = 2 * HD
ROW = 512
TILE = 128

epsilon = 1e-05
negative = -1e30
rotary_base = 10000.0
f32 = jnp.float32
bf16 = jnp.bfloat16
VMEM = 60 * 2**20
RATE = 3.6e6
FLOPS = 4.6e9
PAIRS = HALF // PAIR


def shape(dims, dtype):
    return jax.ShapeDtypeStruct(dims, dtype)


def params():
    return pltpu.CompilerParams(vmem_limit_bytes=VMEM)


def cost(microseconds):
    return pl.CostEstimate(flops=int(microseconds * FLOPS), bytes_accessed=int(microseconds * RATE), transcendentals=int(microseconds * 1e7))


def dot(left, right):
    return jnp.dot(left, right, preferred_element_type=f32)


def dot_nt(left, right):
    return lax.dot_general(left, right, (((1,), (1,)), ((), ())), preferred_element_type=f32)


def dot_tn(left, right):
    return lax.dot_general(left, right, (((0,), (0,)), ((), ())), preferred_element_type=f32)


def lanes_of(block, width):
    return pl.ds(pl.multiple_of(block * width, width), width)


def pair(block):
    return lax.ppermute(block, "fsdp", [(0, 1), (1, 0)])


def exchange(block, axis, distance):
    return lax.ppermute(block, axis, [(i, i ^ distance) for i in range(lax.axis_size(axis))])


def shifted(block, distance):
    devices = range(lax.axis_size("ctx"))
    return lax.ppermute(
        block, "ctx", [(i - distance, i) for i in devices if i - distance in devices]
    )


def doubling(axis):
    distance, out = 1, []
    while distance < lax.axis_size(axis):
        out.append(distance)
        distance *= 2
    return out


def crossed(block, turn, axis="seq"):
    route = []
    for at in range(lax.axis_size(axis)):
        for core in range(2):
            route.append((2 * at + core, 2 * (at ^ (1 + (core ^ turn))) + core))
    return lax.ppermute(block, (axis, "fsdp"), route)


def added(*parts):
    total = parts[0].astype(f32)
    for part in parts[1:]:
        total = total + part.astype(f32)
    return total.astype(bf16)


class Order:
    def __init__(self):
        self.token = None

    def gate(self, *arrays):
        if self.token is None:
            return arrays if len(arrays) > 1 else arrays[0]
        out = lax.optimization_barrier((*arrays, self.token))[:-1]
        return out if len(out) > 1 else out[0]

    def mark(self, array):
        self.token = array
        return array

    def land(self, *arrays):
        arrays = self.gate(*arrays)
        self.mark(arrays[0] if isinstance(arrays, (tuple, list)) else arrays)
        return arrays


class Reduction:
    def __init__(self, order, idx, send, keep, direct):
        self.order, self.idx, self.keep, self.direct = order, idx, keep, direct
        self.tiles = keep.shape[1]
        self.split = lax.axis_size("ctx") == 4
        self.recv = crossed(send, 0)

    def second(self):
        self.keep, self.recv = self.order.gate(self.keep, self.recv)
        self.other = crossed(self.order.mark(halves_call(self.keep, self.recv)), 1)

    def over_ctx(self):
        parts = self.order.gate(self.keep, self.recv, self.other)
        outs = quarters_call(self.idx, *parts, self.direct)
        if not self.split:
            self.total = lax.psum(self.order.mark(outs), "ctx")
        elif self.direct:
            self.own = self.order.mark(outs[0])
            self.recv = [exchange(part, "ctx", k + 1) for k, part in enumerate(outs[1:])]
        else:
            send, self.half = outs
            self.recv = crossed(self.order.mark(send), 0, "ctx")

    def ctx_half(self):
        if self.split and not self.direct:
            self.half, self.recv = self.order.gate(self.half, self.recv)
            far = self.order.mark(added(self.half[0], self.recv[0]))
            self.other = crossed(far, 1, "ctx")

    def ctx_sum(self):
        if not self.split:
            return
        if self.direct:
            self.own = self.order.mark(added(*self.order.gate(self.own, *self.recv)))
            self.recv = [exchange(self.own, "ctx", k) for k in (1, 2, 3)]
        else:
            half, recv, other = self.order.gate(self.half, self.recv, self.other)
            self.own = self.order.mark(added(half[1], recv[1], other))
            self.recv = [crossed(self.own, 1, "ctx"), crossed(self.own, 0, "ctx")]

    def ctx_rest(self):
        if self.split and not self.direct:
            self.recv[0] = self.order.land(self.recv[0])
            self.recv.append(crossed(self.recv[0], 0, "ctx"))

    def regroup(self):
        if self.split:
            parts = self.order.gate(self.own, *self.recv)
            self.total = self.order.mark(regroup_call(self.idx, *parts, direct=self.direct))
        self.total = self.total.reshape(self.tiles, 256, 512)

    def to_beside(self):
        self.beside = crossed(self.order.gate(self.total), 1)

    def to_across(self):
        self.across = crossed(self.order.gate(self.total), 0)

    def to_both(self):
        self.beside = self.order.land(self.beside)
        self.both = crossed(self.beside, 0)

    def swap(self, tiles):
        self.pieces = self.order.gate(self.total, self.beside, self.across, self.both)
        self.swapped = pair(self.order.mark(swap_call(self.pieces, tiles)))


def halves_body(keep, recv, out):
    out[...] = (keep[0].astype(f32) + recv[0].astype(f32)).astype(bf16)


def halves_call(keep, recv):
    tiles = keep.shape[1]
    step = tiles // 2
    block = pl.BlockSpec((1, step, 256, 512), lambda t: (0, t, 0, 0))
    return pl.pallas_call(
        halves_body,
        grid=(2,),
        in_specs=[block] * 2,
        out_specs=pl.BlockSpec((step, 256, 512), lambda t: (t, 0, 0)),
        out_shape=shape((tiles, 256, 512), bf16),
        compiler_params=params(),
        cost_estimate=cost(2.5),
        name="halves",
    )(keep, recv)


def quarters_body(split, direct, idx, keep, recv, other, *outs):
    def block(at):
        total = keep[0, at].astype(f32) + recv[0, at].astype(f32) + other[at].astype(f32)
        return total.astype(bf16)

    ctx, one = idx[3], 1 + idx[0]
    for k in range(4):
        if not split:
            outs[0][k] = block(k)
        elif direct:
            outs[k][...] = block(ctx ^ k)
        else:
            outs[k // 2][k % 2] = block(ctx ^ (3, one, 3 - one, 0)[k])


def quarters_call(idx, keep, recv, other, direct):
    split = lax.axis_size("ctx") == 4
    rows = keep.shape[1] * 256 // 4
    block = pl.BlockSpec((1, 4, rows, 512), lambda i, idx: (1, 0, 0, 0))
    quarter = pl.BlockSpec((4, rows, 512), lambda i, idx: (0, 0, 0))
    if not split:
        out_specs, out_shape = quarter, shape((4, rows, 512), bf16)
    elif direct:
        out_specs = [pl.BlockSpec((rows, 512), lambda i, idx: (0, 0))] * 4
        out_shape = [shape((rows, 512), bf16)] * 4
    else:
        out_specs = [pl.BlockSpec((2, rows, 512), lambda i, idx: (0, 0, 0))] * 2
        out_shape = [shape((2, rows, 512), bf16)] * 2
    return pl.pallas_call(
        functools.partial(quarters_body, split, direct),
        grid_spec=pltpu.PrefetchScalarGridSpec(
            num_scalar_prefetch=1,
            grid=(1,),
            in_specs=[block] * 2 + [quarter],
            out_specs=out_specs,
        ),
        out_shape=out_shape,
        compiler_params=params(),
        cost_estimate=cost(3.8),
        name="quarters",
    )(
        idx,
        keep.reshape(2, 4, rows, 512),
        recv.reshape(2, 4, rows, 512),
        other.reshape(4, rows, 512),
    )


def regroup_body(direct, idx, *refs):
    one = 1 + idx[0]
    for k in range(4):
        refs[4][idx[3] ^ (k if direct else (0, 3 - one, one, 3)[k])] = refs[k][...]


def regroup_call(idx, *parts, direct):
    rows = parts[0].shape[0]
    return pl.pallas_call(
        functools.partial(regroup_body, direct),
        grid_spec=pltpu.PrefetchScalarGridSpec(
            num_scalar_prefetch=1,
            grid=(1,),
            in_specs=[pl.BlockSpec((rows, 512), lambda i, idx: (0, 0))] * 4,
            out_specs=pl.BlockSpec((4, rows, 512), lambda i, idx: (0, 0, 0)),
        ),
        out_shape=shape((4, rows, 512), bf16),
        compiler_params=params(),
        cost_estimate=cost(3.0),
        name="regroup",
    )(idx, *parts)


def swap_body(*refs):
    for k, ref in enumerate(refs[:-1]):
        refs[-1][k] = ref[0]


def swap_call(pieces, tiles):
    operands = [(piece, t) for t in tiles for piece in pieces]
    return pl.pallas_call(
        swap_body,
        grid=(1,),
        in_specs=[
            pl.BlockSpec((1, TILE, 512), lambda i, t=t: (t, 0, 0)) for _, t in operands
        ],
        out_specs=pl.BlockSpec((len(operands), TILE, 512), lambda i: (0, 0, 0)),
        out_shape=shape((len(operands), TILE, 512), bf16),
        compiler_params=params(),
        cost_estimate=cost(2.5),
        name="swap",
    )(*[piece for piece, _ in operands])


def norm_parts(x):
    center = x - jnp.mean(x, axis=-1, keepdims=True)
    inverse = lax.rsqrt(jnp.mean(center * center, axis=-1, keepdims=True) + epsilon)
    return center * inverse, inverse


def vectors_body(pos_ref, *refs):
    at = 0
    for ref in refs[:-1]:
        value = ref[...].astype(f32)
        count = value.shape[0] // HALF
        refs[-1][at : at + count, :] = value.reshape(count, HALF)
        at += count
    refs[-1][at : at + 1, : pos_ref.shape[1]] = pos_ref[...].astype(f32)


def vectors_call(positions, *vectors):
    count = sum(v.shape[0] // HALF for v in vectors) + 1
    return pl.pallas_call(
        vectors_body,
        out_shape=shape((count, HALF), f32),
        compiler_params=params(),
        cost_estimate=cost(1.4),
        name="vectors",
    )(positions, *vectors)


def vector(refs, core, i):
    mine, theirs = refs[0][i : i + 1, :], refs[1][i : i + 1, :]
    first = core == 0
    return jnp.concatenate(
        [jnp.where(first, mine, theirs), jnp.where(first, theirs, mine)], axis=1
    )


def slice_body(idx, in_ref, out_ref):
    out_ref[...] = in_ref[...]


def slice_call(idx, w, width):
    step = width // 2
    return pl.pallas_call(
        slice_body,
        grid_spec=pltpu.PrefetchScalarGridSpec(
            num_scalar_prefetch=1,
            grid=(2,),
            in_specs=[pl.BlockSpec((w.shape[0], step), lambda i, idx: (0, 2 * (1 - idx[0]) + i))],
            out_specs=pl.BlockSpec((w.shape[0], step), lambda i, idx: (0, i)),
        ),
        out_shape=shape((w.shape[0], width), w.dtype),
        compiler_params=params(),
        cost_estimate=cost(3.4),
        name="slice",
    )(idx, w)


def collect_body(idx, *refs):
    share = refs[0].shape[-2]
    parts = [ref[k] for ref in refs[:-1] for k in range(ref.shape[0])]
    for k, part in enumerate(parts):
        at = pl.ds(pl.multiple_of((idx[3] ^ k) * share, share), share)
        refs[-1][:, :, at, :] = part


def collect_call(idx, *parts):
    share = parts[0].shape[-2]
    count = sum(part.shape[0] for part in parts)
    whole = lambda dims: pl.BlockSpec(dims, lambda i, idx: (0,) * len(dims))
    return pl.pallas_call(
        collect_body,
        grid_spec=pltpu.PrefetchScalarGridSpec(
            num_scalar_prefetch=1,
            grid=(1,),
            in_specs=[whole(part.shape) for part in parts],
            out_specs=whole((2, 2, share * count, D)),
        ),
        out_shape=shape((2, 2, share * count, D), bf16),
        compiler_params=params(),
        cost_estimate=cost(2.3),
        name="collect",
    )(idx, *parts)


def rows_of(core):
    return pl.ds(pl.multiple_of(core * HALF, HALF), HALF)


def place_of(bit, value):
    return jnp.where(bit == value, 1, 0)


def spread_rows(ref, tile, grad, m, core, two, lanes):
    at = pl.ds(pl.multiple_of(jnp.where(core == m, TILE, 0), TILE), TILE)
    for r in range(2):
        ref[place_of(two, r), tile, at, lanes] = grad[r * TILE : (r + 1) * TILE]


def unit_body(fresh, idx, *refs):
    refs = list(refs)
    if fresh:
        x_refs, vecs = refs[:2], refs[2:4]
        refs = refs[4:]
    else:
        a_ref, refs = refs[0], refs[3:]
    dy_refs, wu_mine, wu_recv, wd_ref, bu_ref, *refs = refs[:2], *refs[2:]
    if fresh:
        a_ref, *refs = refs
    send_ref, keep_ref, act_ref, dup_ref, bias_ref, wu_ref = refs
    core, one, two = idx[0], idx[1], idx[2]
    chunk = 256
    unit, half = pl.program_id(0) // 2, pl.program_id(0) % 2

    if fresh:

        @pl.when(pl.program_id(0) == 0)
        def _():
            gain, shift = vector(vecs, core, 2), vector(vecs, core, 3)
            for i in range(2 * ROW // chunk):
                at = slice(i % 2 * chunk, (i % 2 + 1) * chunk)
                normal, _ = norm_parts(x_refs[i // 2][at, :].astype(f32))
                a_ref[i * chunk : (i + 1) * chunk, :] = (normal * gain + shift).astype(bf16)
    wu_ref[rows_of(core), :] = wu_mine[...]
    wu_ref[rows_of(1 - core), :] = wu_recv[...]
    bias = jnp.zeros((1, chunk), f32)
    for i in range(2 * ROW // chunk):
        at, at_dy = slice(i * chunk, (i + 1) * chunk), slice(i % 2 * chunk, (i % 2 + 1) * chunk)
        up = dot(a_ref[at, :], wu_ref[...]) + bu_ref[...]
        grad = dot_nt(dy_refs[i // 2][at_dy, :], wd_ref[...])
        cdf = 0.5 * (1.0 + lax.erf(up * (0.5**0.5)))
        density = jnp.exp(-0.5 * up * up) * (1.0 / math.sqrt(2.0 * math.pi))
        act_ref[at, :] = (up * cdf).astype(bf16)
        dup = (grad * (cdf + up * density)).astype(bf16)
        dup_ref[at, :] = dup
        bias = bias + jnp.sum(dup.astype(f32), axis=0, keepdims=True)
    bias_ref[...] = bias
    lanes = lanes_of(one ^ (1 - half), chunk)
    for out, p in ((send_ref, 1 - one), (keep_ref, one)):
        for m in range(2):
            left = a_ref[:, lanes_of(2 * m + p, chunk)]
            grad = dot_tn(left, dup_ref[...]).astype(bf16)
            spread_rows(out, 2 * unit, grad, m, core, two, lanes)
    down = dot_tn(act_ref[:ROW, :], dy_refs[0][...]) + dot_tn(act_ref[ROW:, :], dy_refs[1][...])
    down = down.astype(bf16)
    for step, out in ((0, send_ref), (1, keep_ref)):

        @pl.when(half == step)
        def _(out=out):
            for r in range(2):
                out[place_of(two, r), 2 * unit + 1, :, :] = down[:, r * HALF : (r + 1) * HALF]


def unit_call(idx, first, source, dys, up_mine, up_recv, w_down, b_up, olds):
    fresh = isinstance(source, tuple)
    rows = 2 * ROW

    def sub(s, idx):
        return 2 * (first + s // 2) + (idx[1] ^ (1 - s % 2))

    def whole(dims):
        return pl.BlockSpec(dims, lambda s, idx: (0,) * len(dims))

    column = pl.BlockSpec((rows, 256), lambda s, idx: (0, sub(s, idx)))
    grads = whole((2, 4, 256, 512))
    if fresh:
        own, other, vectors = source
        operands = [own, other, *vectors]
        in_specs = [whole(v.shape) for v in operands]
        out_specs, out_shape = [whole((rows, D))], [shape((rows, D), bf16)]
        aliases = {}
    else:
        operands = [source, *olds]
        in_specs = [whole((rows, D))] + [pl.BlockSpec(memory_space=pl.ANY)] * 2
        out_specs, out_shape = [], []
        aliases = {2: 2, 3: 3}
    return pl.pallas_call(
        functools.partial(unit_body, fresh),
        grid_spec=pltpu.PrefetchScalarGridSpec(
            num_scalar_prefetch=1,
            grid=(4,),
            in_specs=in_specs
            + [
                whole((ROW, D)),
                whole((ROW, D)),
                pl.BlockSpec((HALF, 256), lambda s, idx: (0, idx[0] * 8 + sub(s, idx))),
                pl.BlockSpec((HALF, 256), lambda s, idx: (0, sub(s, idx))),
                pl.BlockSpec((256, D), lambda s, idx: (sub(s, idx), 0)),
                pl.BlockSpec((1, 256), lambda s, idx: (0, sub(s, idx))),
            ],
            out_specs=out_specs
            + [
                grads,
                grads,
                column,
                column,
                pl.BlockSpec((1, 256), lambda s, idx: (0, sub(s, idx) - 2 * first)),
            ],
            scratch_shapes=[pltpu.VMEM((D, 256), bf16)],
        ),
        out_shape=out_shape
        + [
            shape((2, 4, 256, 512), bf16),
            shape((2, 4, 256, 512), bf16),
            shape((rows, FF // 2), bf16),
            shape((rows, FF // 2), bf16),
            shape((1, 1024), f32),
        ],
        input_output_aliases=aliases,
        compiler_params=params(),
        cost_estimate=cost(18),
        name="feed_forward",
    )(idx, *operands, *dys, up_mine, up_recv, w_down, b_up)


def rotated(field, cosine, sine, direction):
    lane = lax.broadcasted_iota(jnp.int32, field.shape, 1) % HD
    partner = jnp.where(
        lane < ROT // 2,
        pltpu.roll(field, PAIR - ROT // 2, 1),
        pltpu.roll(field, ROT // 2, 1),
    )
    return field * cosine + (direction * sine) * partner


def whole_qkv(core, mine, recv_ref, w_ref):
    for t in range(3):
        w_ref[rows_of(core), t * HALF : (t + 1) * HALF] = mine[t][...]
    w_ref[rows_of(1 - core), :] = recv_ref[...]


def qkv_specs():
    return [
        pl.BlockSpec((HALF, HALF), lambda i, idx, t=t: (0, 2 * t + idx[0])) for t in range(3)
    ] + [pl.BlockSpec((HALF, 3 * HALF), lambda i, idx: (0, 0))]


def qkv_bias(vecs, core, t):
    def of(c):
        owner, row = (2 * t + c) // 3, 6 + (2 * t + c) % 3
        return vecs[0 if owner == c else 1][row : row + 1, :]

    return jnp.where(core == 0, of(0), of(1))


def qkv_rows(x, core, vecs, w_ref, table, a_ref, outs):
    normal, _ = norm_parts(x.astype(f32))
    a = (normal * vector(vecs, core, 0) + vector(vecs, core, 1)).astype(bf16)
    a_ref[...] = a
    cosine, sine = table[0][...], table[1][...]
    for t, ref in enumerate(outs):
        if ref is None:
            continue
        part = slice(t * HALF, (t + 1) * HALF)
        lin = dot(a, w_ref[:, part]) + qkv_bias(vecs, core, t)
        if t == 2:
            ref[...] = lin.astype(bf16)
            continue
        for j in range(PAIRS):
            lanes = slice(j * PAIR, (j + 1) * PAIR)
            ref[:, lanes] = rotated(lin[:, lanes], cosine, sine, 1.0).astype(bf16)


def qkv_own_body(idx, *refs):
    xs, dys, vecs, weights, recv_ref = refs[0:2], refs[2:4], refs[4:6], refs[6:9], refs[9]
    wp_ref, pos_ref, tables = refs[10], refs[11], refs[12:14]
    a1, q1, k1, v1, d1, w_out, w_ref = refs[14:]
    step, core = pl.program_id(0), idx[0]

    @pl.when(step == 0)
    def _():
        whole_qkv(core, weights, recv_ref, w_ref)
        w_out[...] = w_ref[...]

    for j in range(2):

        @pl.when(step // 2 == j)
        def _(j=j):
            qkv_rows(xs[j][...], core, vecs, w_ref, tables, a1, (q1, k1, v1))
            dol = dot_nt(dys[j][...], wp_ref[...])
            glob_n, rows = pos_ref.shape[1], dol.shape[0]
            row = lax.broadcasted_iota(jnp.int32, (rows, glob_n), 0)
            row = row + idx[3] * ROW + step % 2 * rows
            hits = jnp.sum((row == pos_ref[j : j + 1, :]).astype(f32), axis=1, keepdims=True)
            d1[...] = jnp.where(hits > 0.0, 0.0, dol).astype(bf16)


def qkv_more_body(idx, *refs):
    prevs, globs, vecs, w_ref, wp_ref = refs[0:2], refs[2], refs[3:5], refs[5], refs[6]
    before, far = refs[7:9], refs[9:11]
    a2, k2, v2, a3, q3, k3, v3, d3 = refs[11:]
    step, core = pl.program_id(0), idx[0]
    for j in range(2):

        @pl.when(step // 2 == j)
        def _(j=j):
            qkv_rows(prevs[j][...], core, vecs, w_ref, before, a2, (None, k2, v2))

    @pl.when(step == 4)
    def _():
        x = jnp.concatenate([globs[0, 0], globs[1, 0]], axis=0)
        qkv_rows(x, core, vecs, w_ref, far, a3, (q3, k3, v3))
        dy = jnp.concatenate([globs[0, 1], globs[1, 1]], axis=0)
        d3[...] = dot_nt(dy, wp_ref[...]).astype(bf16)


def clamped(i, low, count):
    return jnp.clip(i - low, 0, count - 1)


def qkv_block(low, count, width, period=None):
    def at(i, idx):
        block = clamped(i, low, count)
        return (block % period if period else block, 0)

    return pl.BlockSpec((256, width), at)


def whole_block(dims):
    return pl.BlockSpec(dims, lambda i, idx: (0,) * len(dims))


def qkv_own_call(idx, xs, dys, vectors, mine, recv, w_proj, positions, tables):
    rows = 2 * ROW
    third = qkv_block(0, 4, HALF)
    return pl.pallas_call(
        qkv_own_body,
        grid_spec=pltpu.PrefetchScalarGridSpec(
            num_scalar_prefetch=1,
            grid=(4,),
            in_specs=[qkv_block(0, 2, D), qkv_block(2, 2, D)] * 2
            + [whole_block(v.shape) for v in vectors]
            + qkv_specs()
            + [whole_block(w_proj.shape), whole_block(positions.shape)]
            + [qkv_block(0, 4, PAIR, 2)] * 2,
            out_specs=[qkv_block(0, 4, D)] + [third] * 4 + [whole_block((D, 3 * HALF))],
            scratch_shapes=[pltpu.VMEM((D, 3 * HALF), bf16)],
        ),
        out_shape=[shape((rows, D), bf16)]
        + [shape((rows, HALF), bf16)] * 4
        + [shape((D, 3 * HALF), bf16)],
        compiler_params=params(),
        cost_estimate=cost(11),
        name="qkv_own",
    )(idx, *xs, *dys, *vectors, mine, mine, mine, recv, w_proj, positions, *tables)


def qkv_more_call(idx, prevs, globs, vectors, w, w_proj, before, far):
    rows, glob_n = 2 * ROW, 2 * globs.shape[2]
    third, glob = qkv_block(0, 4, HALF), whole_block((glob_n, HALF))
    return pl.pallas_call(
        qkv_more_body,
        grid_spec=pltpu.PrefetchScalarGridSpec(
            num_scalar_prefetch=1,
            grid=(5,),
            in_specs=[qkv_block(0, 2, D), qkv_block(2, 2, D)]
            + [whole_block(v.shape) for v in (globs, *vectors, w, w_proj)]
            + [qkv_block(0, 4, PAIR, 2)] * 2
            + [whole_block((glob_n, PAIR))] * 2,
            out_specs=[qkv_block(0, 4, D), third, third, whole_block((glob_n, D))] + [glob] * 4,
        ),
        out_shape=[shape((rows, D), bf16)]
        + [shape((rows, HALF), bf16)] * 2
        + [shape((glob_n, D), bf16)]
        + [shape((glob_n, HALF), bf16)] * 4,
        compiler_params=params(),
        cost_estimate=cost(10),
        name="qkv_more",
    )(idx, *prevs, globs, *vectors, w, w_proj, *before, *far)


def heads_beside(block_t):
    dim = lax.broadcasted_iota(jnp.int32, block_t.shape, 0)
    zero = jnp.zeros_like(block_t)
    return jnp.concatenate(
        [jnp.where(dim < HD, block_t, zero), jnp.where(dim < HD, zero, block_t)], axis=1
    )


def heads_below(block):
    dim = lax.broadcasted_iota(jnp.int32, block.shape, 1)
    zero = jnp.zeros_like(block)
    return jnp.concatenate(
        [jnp.where(dim < HD, block, zero), jnp.where(dim < HD, zero, block)], axis=0
    )


def heads_back(both):
    n = both.shape[1] // 2
    dim = lax.broadcasted_iota(jnp.int32, (PAIR, n), 0)
    return jnp.where(dim < HD, both[:, :n], both[:, n:])


def near_body(
    info,
    q_ref,
    k_ref,
    v_ref,
    dol_ref,
    kp_ref,
    vp_ref,
    kg_ref,
    vg_ref,
    glob_ref,
    cos_ref,
    sin_ref,
    cosp_ref,
    sinp_ref,
    cosg_ref,
    sing_ref,
    *rest,
):
    o_ref, dq_ref, dk_ref, dv_ref, dkp_ref, dvp_ref, dkg_ref, dvg_ref, dk_acc, dv_acc = rest
    scale = HD**-0.5
    base = info[0]
    absent = jnp.where(base == 0, f32(negative), f32(0.0))
    keys = jnp.concatenate([kp_ref[...], k_ref[...]], axis=0)
    values = jnp.concatenate([vp_ref[...], v_ref[...]], axis=0)
    keys_t = keys.T
    values_t = values.T
    gkeys, gvalues = kg_ref[...], vg_ref[...]
    glob_n = gkeys.shape[0]
    gkeys_t = gkeys.astype(f32).T.astype(bf16)
    gvalues_t = gvalues.astype(f32).T.astype(bf16)
    keys_values = jnp.concatenate([keys, values], axis=1)
    gkeys_values = jnp.concatenate([gkeys, gvalues], axis=1)
    query = (q_ref[...].astype(f32) * scale).astype(bf16)
    query_t = query.T
    dol = dol_ref[...]
    dol_t = dol.T
    two = 2 * TILE
    window = WIN + TILE
    cosine, sine = cos_ref[...], sin_ref[...]
    row = lax.broadcasted_iota(jnp.int32, (TILE, two), 0)
    lane = lax.broadcasted_iota(jnp.int32, (TILE, two), 1) % TILE
    glane = lax.broadcasted_iota(jnp.int32, (glob_n, two), 1) % TILE
    gpos = jnp.concatenate([glob_ref[0], glob_ref[0]], axis=1)
    dkg = jnp.zeros((glob_n, PAIR), f32)
    dvg = jnp.zeros((glob_n, PAIR), f32)
    kk, vv = [None] * 8, [None] * 8
    def products(t):
        rows = slice(t * TILE, (t + 1) * TILE)
        q_beside = heads_beside(query_t[:, rows])
        d_beside = heads_beside(dol_t[:, rows])
        blank = jnp.zeros_like(q_beside)
        right = jnp.concatenate(
            [
                jnp.concatenate([q_beside, blank], axis=1),
                jnp.concatenate([blank, d_beside], axis=1),
            ],
            axis=0,
        )
        return dot(keys_values[t * TILE : t * TILE + window], right), dot(gkeys_values, right)

    ahead = products(0)
    for t in range(ROW // TILE):
        rows = slice(t * TILE, (t + 1) * TILE)
        span = slice(t * TILE, t * TILE + window)
        cut = WIN - t * TILE
        q_beside = heads_beside(query_t[:, rows])
        d_beside = heads_beside(dol_t[:, rows])
        q_below = heads_below(query[rows])
        d_below = heads_below(dol[rows])
        both, far_both = ahead
        if t + 1 < ROW // TILE:
            ahead = products(t + 1)
        score, d_prob = both[:, :two], both[:, two:]
        far, d_far = far_both[:, :two], far_both[:, two:]
        parts = [
            jnp.where(row > lane, score[:TILE] + absent, negative),
        ]
        if cut > TILE:
            parts.append(score[TILE:cut] + absent)
        parts.append(score[cut:WIN])
        if t == 0:
            parts.pop()
        parts.append(jnp.where(row <= lane, score[WIN:], negative))
        score = jnp.concatenate(parts, axis=0)
        far = jnp.where(base + t * TILE + glane - gpos >= WIN, far, negative)
        top = jnp.maximum(
            jnp.max(score, axis=0, keepdims=True), jnp.max(far, axis=0, keepdims=True)
        )
        prob = jnp.exp(score - top)
        far_prob = jnp.exp(far - top)
        total = jnp.sum(prob, axis=0, keepdims=True) + jnp.sum(far_prob, axis=0, keepdims=True)
        delta = jnp.sum(prob * d_prob, axis=0, keepdims=True) + jnp.sum(
            far_prob * d_far, axis=0, keepdims=True
        )
        inverse = 1.0 / total
        delta = delta * inverse
        prob = prob * inverse
        far_prob = far_prob * inverse
        low, far_low = prob.astype(bf16), far_prob.astype(bf16)
        d_score = (prob * (d_prob - delta)).astype(bf16)
        d_far = (far_prob * (d_far - delta)).astype(bf16)
        out_t = dot(values_t[:, span], low) + dot(gvalues_t, far_low)
        o_ref[rows, :] = heads_back(out_t).T.astype(bf16)
        dq_t = dot(keys_t[:, span], d_score) + dot(gkeys_t, d_far)
        dq = heads_back(dq_t).T * scale
        dq_ref[rows, :] = rotated(dq, cosine[rows], sine[rows], -1.0).astype(bf16)
        tk, tv = dot(d_score, q_below), dot(low, d_below)
        for b in range(5):
            bk, bv = tk[b * TILE : (b + 1) * TILE], tv[b * TILE : (b + 1) * TILE]
            kk[t + b] = bk if kk[t + b] is None else kk[t + b] + bk
            vv[t + b] = bv if vv[t + b] is None else vv[t + b] + bv
        dkg = dkg + dot(d_far, q_below)
        dvg = dvg + dot(far_low, d_below)
    for b in range(8):
        dk_acc[b * TILE : (b + 1) * TILE, :] = kk[b]
        dv_acc[b * TILE : (b + 1) * TILE, :] = vv[b]
    dk_ref[...] = dk_acc[ROW:, :]
    dv_ref[...] = dv_acc[ROW:, :]
    dkp_ref[...] = rotated(dk_acc[:ROW, :], cosp_ref[...], sinp_ref[...], -1.0).astype(bf16)
    dvp_ref[...] = dv_acc[:ROW, :].astype(bf16)
    dkg_ref[...] = rotated(dkg, cosg_ref[...], sing_ref[...], -1.0).astype(bf16)
    dvg_ref[...] = dvg.astype(bf16)


def near_call(info, j, q, k, v, dol, k2, v2, kg, vg, glob_wide, tables, before, far):
    glob_n = glob_wide.shape[1]
    own = pl.BlockSpec((ROW, PAIR), lambda h, info: (j, h))
    glob = pl.BlockSpec((glob_n, PAIR), lambda h, info: (j, h))
    table = pl.BlockSpec((ROW, PAIR), lambda h, info: (0, 0))
    gtable = pl.BlockSpec((glob_n, PAIR), lambda h, info: (j, 0))
    own_out = pl.BlockSpec((ROW, PAIR), lambda h, info: (0, h))
    glob_out = pl.BlockSpec((glob_n, PAIR), lambda h, info: (0, h))
    own_low, own_high = shape((ROW, HALF), bf16), shape((ROW, HALF), f32)
    glob_low = shape((glob_n, HALF), bf16)
    return pl.pallas_call(
        near_body,
        grid_spec=pltpu.PrefetchScalarGridSpec(
            num_scalar_prefetch=1,
            grid=(PAIRS,),
            in_specs=[own] * 6
            + [glob] * 2
            + [pl.BlockSpec((1, glob_n, PAIR), lambda h, info: (j, 0, 0))]
            + [table] * 4
            + [gtable] * 2,
            out_specs=[own_out] * 6 + [glob_out] * 2,
            scratch_shapes=[pltpu.VMEM((2 * ROW, PAIR), f32)] * 2,
        ),
        out_shape=[own_low, own_low, own_high, own_high, own_low, own_low, glob_low, glob_low],
        compiler_params=params(),
        cost_estimate=cost(17.5),
        name="near",
    )(info, q, k, v, dol, k2, v2, kg, vg, glob_wide, *tables, *before, *far)


def glob_first_body(info, qg_ref, k_ref, v_ref, glob_ref, out_ref):
    glob_n = qg_ref.shape[0]
    key_pos = info[0] + lax.broadcasted_iota(jnp.int32, (ROW, 2 * glob_n), 0)
    mask = key_pos <= glob_ref[0][0:1]
    lane = lax.broadcasted_iota(jnp.int32, (HD, 2 * glob_n), 1)
    for h in range(HALF // PAIR):
        lanes = slice(h * PAIR, (h + 1) * PAIR)
        query = qg_ref[:, lanes].astype(f32) * HD**-0.5
        beside = heads_beside(query.T).astype(bf16)
        masked = jnp.where(mask, dot(k_ref[:, lanes], beside), negative)
        top = jnp.max(masked, axis=0, keepdims=True)
        prob = jnp.where(mask, jnp.exp(masked - top), 0.0)
        total = jnp.sum(prob, axis=0, keepdims=True)
        both = dot(v_ref[:, lanes].T, prob.astype(bf16))
        out_ref[h, 0:HD, :] = jnp.where(lane < glob_n, both[:HD], both[HD:])
        out_ref[h, HD : HD + 1, :] = top
        out_ref[h, HD + 1 : HD + 2, :] = total
        out_ref[h, HD + 2 : HD + 8, :] = jnp.zeros((6, 2 * glob_n), f32)


def glob_first_call(info, qg, k, v, glob_row):
    glob_n = glob_row.shape[2] // 2
    own = pl.BlockSpec((ROW, HALF), lambda j, info: (j, 0))
    pairs = HALF // PAIR
    return pl.pallas_call(
        glob_first_body,
        grid_spec=pltpu.PrefetchScalarGridSpec(
            num_scalar_prefetch=1,
            grid=(2,),
            in_specs=[
                pl.BlockSpec((glob_n, HALF), lambda j, info: (j, 0)),
                own,
                own,
                pl.BlockSpec((1, 8, 2 * glob_n), lambda j, info: (j, 0, 0)),
            ],
            out_specs=pl.BlockSpec((pairs, HD + 8, 2 * glob_n), lambda j, info: (j, 0, 0)),
        ),
        out_shape=shape((2 * pairs, HD + 8, 2 * glob_n), f32),
        compiler_params=params(),
        cost_estimate=cost(4),
        name="glob_first",
    )(info, qg, k, v, glob_row)


def merged(first, second):
    top_a, top_b = first[:, HD : HD + 1], second[:, HD : HD + 1]
    top = jnp.maximum(top_a, top_b)
    weight_a, weight_b = jnp.exp(top_a - top), jnp.exp(top_b - top)
    total = first[:, HD + 1 : HD + 2] * weight_a + second[:, HD + 1 : HD + 2] * weight_b
    out = first[:, :HD] * weight_a + second[:, :HD] * weight_b
    return jnp.concatenate([out, top, total, first[:, HD + 2 :]], axis=1)


def glob_second_body(
    info,
    qg_ref,
    dolg_ref,
    k_ref,
    v_ref,
    glob_ref,
    cos_ref,
    sin_ref,
    cosg_ref,
    sing_ref,
    *rest,
):
    near, rest = rest[:6], rest[6:]
    stat_refs, (o_ref, dk_ref, dv_ref, dqg_ref) = rest[:-4], rest[-4:]
    first = pl.program_id(0) == 0
    scale = HD**-0.5
    glob_n = qg_ref.shape[0]
    key_pos = info[0] + lax.broadcasted_iota(jnp.int32, (ROW, 2 * glob_n), 0)
    positions = glob_ref[0][0:1]
    mask = key_pos <= positions
    place = (key_pos[:, :glob_n] == positions[:, :glob_n]).astype(f32)
    hit = jnp.sum(place, axis=1, keepdims=True) > 0.0
    place = place.astype(bf16)
    cosine, sine = cos_ref[...], sin_ref[...]
    cosine_g, sine_g = cosg_ref[...], sing_ref[...]
    for h in range(HALF // PAIR):
        lanes = slice(h * PAIR, (h + 1) * PAIR)
        keys, values = k_ref[:, lanes], v_ref[:, lanes]
        query = qg_ref[:, lanes].astype(f32) * scale
        q_beside = heads_beside(query.T).astype(bf16)
        q_below = heads_below(query.astype(bf16))
        dol = dolg_ref[:, lanes]
        dol_t = dol.astype(f32).T
        d_beside = heads_beside(dol_t).astype(bf16)
        d_below = heads_below(dol)
        tops = [ref[h, HD : HD + 1, :] for ref in stat_refs]
        top = functools.reduce(jnp.maximum, tops)
        weights = [jnp.exp(part - top) for part in tops]
        total = sum(w * ref[h, HD + 1 : HD + 2, :] for w, ref in zip(weights, stat_refs))
        out_t = sum(w * ref[h, 0:HD, :] for w, ref in zip(weights, stat_refs)) * (1.0 / total)
        lse = top + jnp.log(total)
        delta = jnp.sum(
            out_t * jnp.concatenate([dol_t[:HD], dol_t[HD:]], axis=1), axis=0, keepdims=True
        )
        score = jnp.where(mask, dot(keys, q_beside), negative)
        prob = jnp.where(mask, jnp.exp(score - lse), 0.0)
        d_score = (prob * (dot(values, d_beside) - delta)).astype(bf16)
        near_o, near_dk, near_dv = (
            jnp.where(first, near[i][:, lanes], near[i + 1][:, lanes]) for i in (0, 2, 4)
        )
        dk = near_dk + dot(d_score, q_below)
        dv = near_dv + dot(prob.astype(bf16), d_below)
        dk_ref[:, lanes] = rotated(dk, cosine, sine, -1.0).astype(bf16)
        dv_ref[:, lanes] = dv.astype(bf16)
        dq_both = dot(keys.T, d_score)
        dq_t = jnp.concatenate([dq_both[:HD, :glob_n], dq_both[HD:, glob_n:]], axis=0)
        dqg_ref[:, lanes] = rotated(dq_t.T * scale, cosine_g, sine_g, -1.0).astype(bf16)
        rows = jnp.concatenate([out_t[:, :glob_n], out_t[:, glob_n:]], axis=0).T.astype(bf16)
        o_ref[:, lanes] = jnp.where(hit, dot(place, rows).astype(bf16), near_o)


def glob_second_call(info, qg, dolg, k, v, stats, glob_row, near, tables, far):
    glob_n = glob_row.shape[2] // 2
    pairs = HALF // PAIR
    rows = k.shape[0]
    own = pl.BlockSpec((ROW, HALF), lambda j, info: (j, 0))
    glob = pl.BlockSpec((glob_n, HALF), lambda j, info: (j, 0))
    table = pl.BlockSpec((ROW, PAIR), lambda j, info: (0, 0))
    gtable = pl.BlockSpec((glob_n, PAIR), lambda j, info: (j, 0))
    return pl.pallas_call(
        glob_second_body,
        grid_spec=pltpu.PrefetchScalarGridSpec(
            num_scalar_prefetch=1,
            grid=(2,),
            in_specs=[
                glob,
                glob,
                own,
                own,
                pl.BlockSpec((1, 8, 2 * glob_n), lambda j, info: (j, 0, 0)),
                table,
                table,
                gtable,
                gtable,
            ]
            + [pl.BlockSpec((ROW, HALF), lambda j, info: (0, 0))] * 6
            + [pl.BlockSpec((pairs, HD + 8, 2 * glob_n), lambda j, info: (j, 0, 0))] * len(stats),
            out_specs=[own, own, own, glob],
        ),
        out_shape=[shape((rows, HALF), bf16)] * 3 + [shape((2 * glob_n, HALF), bf16)],
        compiler_params=params(),
        cost_estimate=cost(8),
        name="glob_second",
    )(info, qg, dolg, k, v, glob_row, *tables, *far, *near, *stats)


def weights_body(tiles, idx, *refs):
    core, two = idx[0], idx[2]

    def run(at, ref):
        for tile in (at, at + 1):
            kind, operands = tiles[tile]
            if kind == "rows":
                total = sum(dot_tn(refs[left][...], refs[right][...]) for left, right in operands)
                total = total.astype(bf16)
                for r in range(2):
                    ref[place_of(two, r), tile, :, :] = total[:, r * HALF : (r + 1) * HALF]
                continue
            for m in range(2):
                total = None
                for left, right in operands:
                    term = dot_tn(refs[left + m][...], refs[right][...])
                    total = term if total is None else total + term
                spread_rows(ref, tile, total.astype(bf16), m, core, two, slice(None))

    for at in range(0, len(tiles), 2):
        for half in range(2):

            @pl.when(pl.program_id(0) == at + half)
            def _(at=at, half=half):
                run(at, refs[len(refs) - 2 + half])


def weights_call(idx, tiles):
    specs, operands, table, lefts = [], [], [], {}

    def add(array, spec):
        specs.append(spec)
        operands.append(array)
        return len(operands) - 1

    def whole(array):
        return add(array, pl.BlockSpec(array.shape, lambda s, idx: (0, 0)))

    def part(s, idx):
        return idx[1] ^ (1 - s % 2)

    def left_of(array, rows, j):
        if (id(array), rows, j) not in lefts:
            specs = [
                pl.BlockSpec((rows, 256), lambda s, idx, m=m: (j, 2 * m + part(s, idx)))
                for m in range(2)
            ]
            lefts[id(array), rows, j] = [add(array, spec) for spec in specs][0]
        return lefts[id(array), rows, j]

    for kind, products in tiles:
        if kind == "rows":
            pairs = []
            for j, (left, right) in enumerate(products):
                spec = pl.BlockSpec((right.shape[0], 256), lambda s, idx, j=j: (j, part(s, idx)))
                pairs.append((add(left, spec), whole(right)))
        else:
            pairs = []
            for left, *rights in products:
                for j, right in enumerate(rights):
                    pairs.append((left_of(left, right.shape[0], j), whole(right)))
        table.append((kind, tuple(pairs)))
    count = len(tiles)
    out = pl.BlockSpec((2, count, 256, 512), lambda s, idx: (0, 0, 0, 0))
    return pl.pallas_call(
        functools.partial(weights_body, tuple(table)),
        grid_spec=pltpu.PrefetchScalarGridSpec(
            num_scalar_prefetch=1, grid=(count,), in_specs=specs, out_specs=[out] * 2
        ),
        out_shape=[shape((2, count, 256, 512), bf16)] * 2,
        compiler_params=params(),
        cost_estimate=cost(16),
        name="weight_grads",
    )(idx, *operands)


def input_body(idx, *refs):
    x_ref, xo_ref, xp_ref, xop_ref, glob_ref = refs[:5]
    vecs, core = refs[5:7], idx[0]
    w_ref, up_mine, up_recv = refs[7:10]
    dqs, dk1, dv1, dkps, dvps, dqg = refs[10:12], refs[12], refs[13], refs[14:16], refs[16:18], refs[18]
    dkgs, dvgs, dup_ref = refs[19:21], refs[21:23], refs[23]
    mine, other, sums_a, sums_m, bias_ref, wu_ref = refs[24:]
    step = pl.program_id(0)

    @pl.when(step == 0)
    def _():
        sums_a[...] = jnp.zeros_like(sums_a)
        sums_m[...] = jnp.zeros_like(sums_m)
        bias_ref[...] = jnp.zeros_like(bias_ref)
        wu_ref[rows_of(idx[0]), :] = up_mine[...]
        wu_ref[rows_of(1 - idx[0]), :] = up_recv[...]

    def gather(sums, grad, normal):
        sums[0:1, :] += jnp.sum(grad * normal, axis=0, keepdims=True)
        sums[1:2, :] += jnp.sum(grad, axis=0, keepdims=True)

    def attn(x, parts):
        grad = None
        for t, part in enumerate(parts):
            if part is None:
                continue
            lanes = slice(t * HALF, (t + 1) * HALF)
            term = dot_nt(part, w_ref[:, lanes])
            grad = term if grad is None else grad + term
            bias_ref[0:1, lanes] += jnp.sum(part.astype(f32), axis=0, keepdims=True)
        normal, _ = norm_parts(x.astype(f32))
        gather(sums_a, grad, normal)
        return grad * vector(vecs, core, 0), normal

    def own_rows(x, dq, out):
        g, normal = attn(x[...], (dq[...], dk1[...], dv1[...]))
        grad = dot_nt(dup_ref[...], wu_ref[...])
        gather(sums_m, grad, normal)
        out[...] = (g + grad * vector(vecs, core, 2)).astype(bf16)

    @pl.when(step < 2)
    def _():
        own_rows(x_ref, dqs[0], mine)

    @pl.when((step >= 2) & (step < 4))
    def _():
        own_rows(xo_ref, dqs[1], other)

    @pl.when((step >= 4) & (step < 6))
    def _():
        mine[...] = attn(xp_ref[...], (None, dkps[0][...], dvps[0][...]))[0].astype(bf16)

    @pl.when((step >= 6) & (step < 8))
    def _():
        other[...] = attn(xop_ref[...], (None, dkps[1][...], dvps[1][...]))[0].astype(bf16)

    @pl.when(step == 8)
    def _():
        rows = jnp.concatenate([glob_ref[0, 0], glob_ref[1, 0]], axis=0)
        dkg, dvg = (jnp.concatenate([v[0][...], v[1][...]], axis=0) for v in (dkgs, dvgs))
        grad = attn(rows, (dqg[...], dkg, dvg))[0].astype(bf16)
        glob_n = glob_ref.shape[2]
        mine[:glob_n, :] = grad[:glob_n]
        other[:glob_n, :] = grad[glob_n:]


def input_call(idx, xs, prevs, globs, vectors, w_qkv, up_mine, up_recv, grads):
    step, rows, glob_n = 256, 2 * ROW, 2 * globs.shape[2]
    part = pl.BlockSpec((2, 1, *globs.shape[2:]), lambda i, idx: (0, 0, 0, 0))

    def mine_at(i):
        return jnp.where(i < 4, jnp.minimum(i, 1), jnp.where(i < 8, jnp.minimum(i - 2, 3), 4))

    def other_at(i):
        return jnp.where(i < 6, clamped(i, 2, 2), jnp.where(i < 8, i - 4, 4))


    def block(low, count, width):
        return pl.BlockSpec((step, width), lambda i, idx: (clamped(i, low, count), 0))

    whole = lambda rows, width: pl.BlockSpec((rows, width), lambda i, idx: (0, 0))
    return pl.pallas_call(
        input_body,
        grid_spec=pltpu.PrefetchScalarGridSpec(
            num_scalar_prefetch=1,
            grid=(9,),
            in_specs=[block(2 * j, 2, D) for j in range(4)]
            + [part]
            + [whole(*v.shape) for v in vectors]
            + [whole(*w_qkv.shape)]
            + [
                pl.BlockSpec((HALF, FF // 2), lambda i, idx: (0, idx[0])),
                whole(HALF, FF // 2),
            ]
            + [block(0, 2, HALF), block(2, 2, HALF)]
            + [block(0, 4, HALF)] * 2
            + [block(4, 2, HALF), block(6, 2, HALF)] * 2
            + [whole(glob_n, HALF)]
            + [whole(glob_n // 2, HALF)] * 4
            + [block(0, 4, FF // 2)],
            out_specs=[
                pl.BlockSpec((step, D), lambda i, idx: (mine_at(i), 0)),
                pl.BlockSpec((step, D), lambda i, idx: (other_at(i), 0)),
                whole(8, D),
                whole(8, D),
                whole(8, 3 * HALF),
            ],
            scratch_shapes=[pltpu.VMEM((D, FF // 2), bf16)],
        ),
        out_shape=[shape((rows + step, D), bf16)] * 2
        + [
            shape((8, D), f32),
            shape((8, D), f32),
            shape((8, 3 * HALF), f32),
        ],
        compiler_params=params(),
        cost_estimate=cost(24),
        name="input_grads",
    )(
        idx,
        *xs,
        *prevs,
        globs,
        *vectors,
        w_qkv,
        up_mine,
        up_recv,
        *grads,
    )


def result_body(act_ref, wd_ref, ol_ref, wp_ref, mine_ref, other_ref):
    part = (dot(act_ref[...], wd_ref[...]) + dot(ol_ref[...], wp_ref[...])).astype(bf16)
    half = pl.num_programs(0) // 2

    @pl.when(pl.program_id(0) < half)
    def _():
        mine_ref[...] = part

    @pl.when(pl.program_id(0) >= half)
    def _():
        other_ref[...] = part


def result_call(act, w_down, ol, w_proj):
    rows, step = act.shape[0], 256
    half = rows // step // 2
    return pl.pallas_call(
        result_body,
        grid=(rows // step,),
        in_specs=[
            pl.BlockSpec((step, act.shape[1]), lambda i: (i, 0)),
            pl.BlockSpec(w_down.shape, lambda i: (0, 0)),
            pl.BlockSpec((step, HALF), lambda i: (i, 0)),
            pl.BlockSpec(w_proj.shape, lambda i: (0, 0)),
        ],
        out_specs=[
            pl.BlockSpec((step, D), lambda i: (jnp.minimum(i, half - 1), 0)),
            pl.BlockSpec((step, D), lambda i: (jnp.maximum(i - half, 0), 0)),
        ],
        out_shape=[shape((rows // 2, D), bf16)] * 2,
        compiler_params=params(),
        cost_estimate=cost(10.3),
        name="result",
    )(act, w_down, ol, w_proj)


def place_body(spreads, rows, n_alias, idx, *refs):
    pieces, swapped = refs[:4], refs[4]
    outs = list(refs[5 + n_alias :])
    spread_out, rows_out = outs[0], outs[1]
    one, two = idx[1], idx[2]
    for i in range(max(len(spreads), len(rows))):
        for h in range(2):

            @pl.when((pl.program_id(0) == i) & (pl.program_id(1) == h))
            def _(i=i, h=h):
                if i < len(spreads):
                    for k in range(4):
                        if h:
                            block = 2 * (two ^ (k // 2)) + (one ^ (k % 2))
                            part = swapped[4 * i + k]
                        else:
                            block = 2 * (one ^ (k // 2)) + (two ^ (k % 2))
                            part = pieces[k][spreads[i], TILE:, :]
                        spread_out[pl.ds(pl.multiple_of(block * TILE, TILE), TILE), :] = (
                            part.astype(f32)
                        )
                if i < len(rows):
                    for beside in range(2):
                        part = pieces[2 * h + beside][rows[i]]
                        rows_out[:, lanes_of(two ^ beside, HALF)] = part.astype(f32)


def place_call(idx, work, spreads, rows, spread_target, rows_target):
    targets = [spread_target, rows_target]
    alias = [buf for buf, _, _ in targets if buf is not None]
    aliases, at = {}, 6
    for out, (buf, _, _) in enumerate(targets):
        if buf is not None:
            aliases[at] = out
            at += 1

    def spread_index(i, h, idx):
        return 0, spread_target[2](i, idx[0] ^ h)

    def rows_index(i, h, idx):
        last = len(rows) - 1
        i, h = jnp.where(i > last, last, i), jnp.where(i > last, 1, h)
        return rows_target[2](i, idx[1] ^ h), 0

    whole = lambda array: pl.BlockSpec(array.shape, lambda i, h, idx: (0, 0, 0))
    operands = [*work.pieces, work.swapped]
    return pl.pallas_call(
        functools.partial(place_body, spreads, rows, len(alias)),
        grid_spec=pltpu.PrefetchScalarGridSpec(
            num_scalar_prefetch=1,
            grid=(len(spreads), 2),
            in_specs=[whole(array) for array in operands]
            + [pl.BlockSpec(memory_space=pl.ANY)] * len(alias),
            out_specs=[pl.BlockSpec((HALF, 512), spread_index), pl.BlockSpec((256, D), rows_index)],
        ),
        out_shape=[shape(dims, f32) for _, dims, _ in targets],
        input_output_aliases=aliases,
        compiler_params=params(),
        cost_estimate=cost(7.0),
        name="place",
    )(idx, *operands, *alias)


def rotary_tables(positions):
    lane = jnp.arange(PAIR, dtype=jnp.int32) % HD
    half = ROT // 2
    freqs = rotary_base ** (-2.0 * (lane % half).astype(f32) / ROT)
    angles = positions.astype(f32)[:, None] * freqs[None, :]
    active = (lane < ROT)[None, :]
    sign = jnp.where(lane < half, -1.0, 1.0)[None, :]
    return jnp.where(active, jnp.cos(angles), 1.0), jnp.where(active, jnp.sin(angles) * sign, 0.0)


def per_device(
    tokens,
    cotangent,
    global_pos,
    attn_gain,
    attn_shift,
    mlp_gain,
    mlp_shift,
    qkv_weight,
    qkv_bias,
    proj_weight,
    proj_bias,
    up_weight,
    up_bias,
    down_weight,
    down_bias,
):
    n_ctx = lax.axis_size("ctx")
    core = lax.axis_index("fsdp")
    seq = lax.axis_index("seq")
    ctx = lax.axis_index("ctx")
    x_bit, y_bit = seq & 1, seq >> 1
    base = ctx * ROW
    own_x = tokens[0]
    own_dy = cotangent[0]
    glob_n = global_pos.shape[1]
    share = glob_n // n_ctx
    info = jnp.stack([base]).astype(jnp.int32)
    one, two = jnp.where(core == 0, x_bit, y_bit), jnp.where(core == 0, y_bit, x_bit)
    idx = jnp.stack([core, one, two, ctx]).astype(jnp.int32)
    order = Order()

    other_x = pair(own_x)
    up_recv = pair(slice_call(idx, up_weight, FF // 2))
    other_dy = pair(own_dy)
    mine = vectors_call(
        global_pos, attn_gain, attn_shift, mlp_gain, mlp_shift, proj_bias, down_bias, qkv_bias
    )
    vectors = (mine, pair(mine))
    row_pos = base + jnp.arange(ROW, dtype=jnp.int32)
    own_glob = lax.dynamic_slice_in_dim(global_pos[0], ctx * share, share, 0)
    pick = (own_glob[:, None] == row_pos[None, :]).astype(bf16)
    picked = jnp.stack([dot(pick, own_x), dot(pick, own_dy)]).astype(bf16)
    picked = jnp.stack([picked, pair(picked)])[None]
    pos_pair = jnp.concatenate([v[9:10, :glob_n] for v in vectors]).astype(jnp.int32)
    bias_up = up_bias.astype(f32).reshape(1, FF // 2)
    picked, first_x = lax.optimization_barrier((picked, own_x))
    picks, distances = [picked], doubling("ctx")
    beside = exchange(picked, "ctx", distances[0])
    prev_x = shifted(first_x, 1)

    xs, dys = (own_x, other_x), (own_dy, other_dy)
    a_mlp, send, keep, act, dup, sums = unit_call(
        idx,
        0,
        (first_x, other_x, vectors),
        dys,
        up_weight,
        up_recv,
        down_weight,
        bias_up,
        None,
    )
    order.mark(sums)
    up_sums = [sums.reshape(2, 512)]
    work0 = Reduction(order, idx, send, keep, True)
    picks.append(order.land(beside))
    for distance in distances[1:]:
        picked = order.mark(jnp.concatenate(picks, axis=0))
        picks.append(exchange(picked, "ctx", distance))
    w_in = order.gate(qkv_weight)
    w_in = order.mark(
        jnp.concatenate(
            [
                lax.dynamic_slice_in_dim(w_in, (2 * t + 1 - core) * HALF, HALF, 1)
                for t in range(3)
            ],
            axis=1,
        )
    )
    qkv_recv = pair(w_in)
    send, keep, act, dup, sums = unit_call(
        idx,
        2,
        order.gate(a_mlp),
        dys,
        up_weight,
        up_recv,
        down_weight,
        bias_up,
        (act, dup),
    )
    order.mark(sums)
    up_sums.append(sums.reshape(2, 512))
    prev_x, qkv_recv = order.land(prev_x, qkv_recv)
    other_prev = pair(prev_x)
    if n_ctx == 4:
        globs = collect_call(idx, *order.gate(*picks))
    else:
        picked = jnp.concatenate(picks, axis=0)
        picked = jnp.take(picked, jnp.arange(n_ctx, dtype=jnp.int32) ^ ctx, axis=0)
        globs = jnp.transpose(picked, (1, 2, 0, 3, 4)).reshape(2, 2, glob_n, D)
    order.mark(globs)
    pos_pair = order.gate(pos_pair)
    tables = rotary_tables(row_pos)
    before = rotary_tables(row_pos - ROW)
    far = rotary_tables(pos_pair.reshape(-1))
    glob_row = jnp.broadcast_to(
        jnp.concatenate([pos_pair, pos_pair], axis=1)[:, None, :], (2, 8, 2 * glob_n)
    )
    glob_wide = jnp.broadcast_to(pos_pair[:, :, None], (2, glob_n, PAIR))
    tables, before, far, glob_row, glob_wide, other_prev, _ = lax.optimization_barrier(
        (tables, before, far, glob_row, glob_wide, other_prev, order.token)
    )
    order.mark(glob_wide)
    prevs = (prev_x, other_prev)
    work0.second()

    a1, q1, k1, v1, dol, w_qkv = qkv_own_call(
        idx,
        (order.gate(own_x), other_x),
        dys,
        vectors,
        qkv_weight,
        qkv_recv,
        proj_weight,
        pos_pair,
        tables,
    )
    order.mark(dol)
    work0.over_ctx()
    work1 = Reduction(order, idx, order.gate(send), keep, True)
    a2, k2, v2, a3, q3, k3, v3, dolg = qkv_more_call(
        idx, (order.gate(prev_x), other_prev), globs, vectors, w_qkv, proj_weight, before, far
    )
    order.mark(q3)
    stats = order.mark(glob_first_call(info, q3, k1, v1, glob_row))
    beside = exchange(stats, "ctx", 1)

    def near_of(j):
        outs = near_call(
            info, j, order.gate(q1), k1, v1, dol, k2, v2, k3, v3, glob_wide, tables, before, far
        )
        order.mark(outs[-1])
        return outs

    near0 = near_of(0)
    work1.second()
    for distance in distances[1:]:
        stats = order.mark(merged(*order.gate(stats, beside)))
        beside = exchange(stats, "ctx", distance)
    work0.ctx_sum()
    near1 = near_of(1)
    stats = order.land(stats, beside)
    near, dqs, dks, dvs, dkps, dvps, dkgs, dvgs = zip(near0, near1)
    ol, dk1, dv1, dqg = glob_second_call(
        info,
        order.gate(q3),
        dolg,
        k1,
        v1,
        stats,
        glob_row,
        (*near, *dks, *dvs),
        tables,
        far,
    )
    order.mark(dqg)
    work0.regroup()
    work0.to_beside()
    work0.to_across()
    work1.over_ctx()
    send, keep = weights_call(
        idx,
        (
            ("spread", ((a1, order.gate(dv1)), (a2, *dvps), (a3, *dvgs))),
            ("rows", ((ol, own_dy), (ol, other_dy))),
            ("spread", ((a1, *dqs), (a3, dqg))),
            ("spread", ((a1, dk1), (a2, *dkps), (a3, *dkgs))),
        ),
    )
    order.mark(send)
    work2 = Reduction(order, idx, send, keep, False)
    work0.beside, work0.across = order.land(work0.beside, work0.across)
    work1.ctx_sum()

    g_mine, g_other, sums_a, sums_m, bias = input_call(
        idx,
        (order.gate(own_x), other_x),
        prevs,
        globs,
        vectors,
        w_qkv,
        up_weight,
        up_recv,
        (*dqs, dk1, dv1, *dkps, *dvps, dqg, *dkgs, *dvgs, dup),
    )
    order.mark(bias)
    work2.second()
    work1.regroup()
    work0.to_both()
    work1.to_beside()
    work1.to_across()
    part, part_other = result_call(order.gate(act), down_weight, ol, proj_weight)
    order.mark(part)
    work2.over_ctx()
    g_beside = pair(order.gate(g_other))
    work2.ctx_half()
    prev_mine, glob_mine, g_beside = order.gate(
        g_mine[ROW : 2 * ROW], g_mine[2 * ROW : 2 * ROW + glob_n], g_beside
    )
    glob_sum = order.mark(added(glob_mine, g_beside[2 * ROW : 2 * ROW + glob_n]))
    prev_sum = order.mark(added(prev_mine, g_beside[ROW : 2 * ROW]))
    part_beside = pair(order.gate(part_other))
    work0.swap([0, 2])
    work2.ctx_sum()

    def place_units(work, first, up_out, down_out):
        up_out, down_out = place_call(
            idx,
            work,
            (0, 2),
            (1, 3),
            (up_out, (HALF, FF), lambda i, c: c * 4 + first + i),
            (down_out, (FF // 2, D), lambda i, p: (first + i) * 2 + p),
        )
        order.mark(up_out[:8, :128])
        return up_out, down_out

    own, part, part_beside = order.gate(own_x, part, part_beside)
    result = own.astype(f32) + part.astype(f32) + part_beside.astype(f32)
    first = core == 0
    for i in (4, 5):
        rows = [v[i : i + 1] for v in vectors]
        result = result + jnp.concatenate(
            [jnp.where(first, rows[0], rows[1]), jnp.where(first, rows[1], rows[0])], axis=1
        )
    layer_out = order.mark(result.astype(bf16))[None]
    beside = exchange(order.gate(glob_sum), "ctx", 1)
    up_out, down_out = place_units(work0, 0, None, None)
    work2.ctx_rest()
    work1.to_both()
    for distance in doubling("ctx")[1:]:
        glob_sum = order.mark(added(*order.gate(glob_sum, beside)))
        beside = exchange(glob_sum, "ctx", distance)

    dy_sum = jnp.sum(order.gate(own_dy).astype(f32), axis=0)
    qkv_sum = bias[0].reshape(3, 1, HALF)
    mine = jnp.arange(2, dtype=jnp.int32)[None, :, None] == core
    qkv_sum = jnp.where(mine, qkv_sum, 0.0).reshape(2, 3, 512)
    split = jnp.concatenate(
        [
            sums_a[:2].reshape(2, 2, 512).swapaxes(0, 1),
            sums_m[:2].reshape(2, 2, 512).swapaxes(0, 1),
            dy_sum.reshape(2, 1, 512),
            qkv_sum,
        ],
        axis=1,
    )
    kept = lax.dynamic_index_in_dim(split, core, 0, False)
    given = pair(order.mark(lax.dynamic_index_in_dim(split, 1 - core, 0, False)))
    work2.regroup()
    work2.to_beside()
    work2.to_across()
    kept, given = order.gate(kept, given)
    total = order.mark(jnp.concatenate([kept + given] + up_sums, axis=0))
    steps = [(axis, distance) for axis in ("seq", "ctx") for distance in doubling(axis)]
    glob_sum, beside = order.gate(glob_sum, beside)
    glob_sum = order.mark(added(glob_sum, beside))
    from_prev = shifted(order.gate(prev_sum), -1)
    work1.swap([0, 2])
    work2.to_both()
    up_out, down_out = place_units(work1, 2, up_out, down_out)
    for step in steps[:-2]:
        total = order.mark(total + order.gate(exchange(total, *step)))
    place = (row_pos[:, None] == global_pos[0][None, :]).astype(bf16)
    own, mine, g_beside, from_prev, glob_sum = order.gate(
        own_x, g_mine, g_beside, from_prev, glob_sum
    )
    g = (
        mine[:ROW].astype(f32)
        + g_beside[:ROW].astype(f32)
        + from_prev.astype(f32)
        + dot(place, glob_sum)
    )
    normal, inverse = norm_parts(own.astype(f32))
    lower = inverse * (
        g
        - jnp.mean(g, axis=-1, keepdims=True)
        - normal * jnp.mean(g * normal, axis=-1, keepdims=True)
    )
    tokens_grad = order.mark(own_dy.astype(f32) + lower)[None]
    for step in steps[-2:]:
        total = order.mark(total + order.gate(exchange(total, *step)))
    work2.swap([0, 2, 3])
    qkv_out, proj_out = place_call(
        idx,
        work2,
        (0, 2, 3),
        (1,),
        (None, (HALF, 3 * D), lambda i, c: 2 * ((i + 2) % 3) + c),
        (None, (HALF, D), lambda i, p: p),
    )
    return (
        layer_out,
        tokens_grad,
        total[0],
        total[1],
        total[2],
        total[3],
        qkv_out,
        total[5:8].reshape(-1),
        proj_out,
        total[4],
        up_out,
        total[8:12].reshape(-1),
        down_out,
        total[4],
    )


def solution(mesh):
    rows = P(("seq", "fsdp"), "ctx", None)
    vector, matrix = P("fsdp"), P("fsdp", None)
    return jax.shard_map(
        per_device,
        mesh=mesh,
        in_specs=(
            rows,
            rows,
            P(("seq", "fsdp"), None),
            vector,
            vector,
            vector,
            vector,
            matrix,
            vector,
            matrix,
            vector,
            matrix,
            vector,
            matrix,
            vector,
        ),
        out_specs=(
            rows,
            rows,
            vector,
            vector,
            vector,
            vector,
            matrix,
            vector,
            matrix,
            vector,
            matrix,
            vector,
            matrix,
            vector,
        ),
        check_vma=False,
    )
```

```python
import functools
import math

import jax
import jax.numpy as jnp
from jax import lax
from jax.experimental import pallas as pl
from jax.experimental.pallas import tpu as pltpu
from jax.sharding import PartitionSpec as P

D = 1024
H = 16
HD = 64
ROT = 16
WIN = 512
FF = 4096
HALF = D // 2
PAIR = 2 * HD
ROW = 512
TILE = 128

epsilon = 1e-05
negative = -1e30
rotary_base = 10000.0
f32 = jnp.float32
bf16 = jnp.bfloat16
VMEM = 62 * 2**20
RATE = 3.6e6
FLOPS = 4.6e9
PAIRS = HALF // PAIR


def shape(dims, dtype):
    return jax.ShapeDtypeStruct(dims, dtype)


def params():
    return pltpu.CompilerParams(vmem_limit_bytes=VMEM)


def cost(microseconds):
    return pl.CostEstimate(flops=int(microseconds * FLOPS), bytes_accessed=int(microseconds * RATE), transcendentals=int(microseconds * 1e7))


def dot(left, right):
    return jnp.dot(left, right, preferred_element_type=f32)


def dot_nt(left, right):
    return lax.dot_general(left, right, (((1,), (1,)), ((), ())), preferred_element_type=f32)


def dot_tn(left, right):
    return lax.dot_general(left, right, (((0,), (0,)), ((), ())), preferred_element_type=f32)


def lanes_of(block, width):
    return pl.ds(pl.multiple_of(block * width, width), width)


def pair(block):
    return lax.ppermute(block, "fsdp", [(0, 1), (1, 0)])


def exchange(block, axis, distance):
    return lax.ppermute(block, axis, [(i, i ^ distance) for i in range(lax.axis_size(axis))])


def shifted(block, distance):
    devices = range(lax.axis_size("ctx"))
    return lax.ppermute(
        block, "ctx", [(i - distance, i) for i in devices if i - distance in devices]
    )


def doubling(axis):
    distance, out = 1, []
    while distance < lax.axis_size(axis):
        out.append(distance)
        distance *= 2
    return out


def crossed(block, turn, axis="seq"):
    route = []
    for at in range(lax.axis_size(axis)):
        for core in range(2):
            route.append((2 * at + core, 2 * (at ^ (1 + (core ^ turn))) + core))
    return lax.ppermute(block, (axis, "fsdp"), route)


def added(*parts):
    total = parts[0].astype(f32)
    for part in parts[1:]:
        total = total + part.astype(f32)
    return total.astype(bf16)


class Order:
    def __init__(self):
        self.token = None

    def gate(self, *arrays):
        if self.token is None:
            return arrays if len(arrays) > 1 else arrays[0]
        out = lax.optimization_barrier((*arrays, self.token))[:-1]
        return out if len(out) > 1 else out[0]

    def mark(self, array):
        self.token = array
        return array

    def land(self, *arrays):
        arrays = self.gate(*arrays)
        self.mark(arrays[0] if isinstance(arrays, (tuple, list)) else arrays)
        return arrays


class Reduction:
    def __init__(self, order, idx, send, keep, direct):
        self.order, self.idx, self.keep, self.direct = order, idx, keep, direct
        self.tiles = keep.shape[1]
        self.split = lax.axis_size("ctx") == 4
        self.recv = crossed(send, 0)

    def second(self):
        self.keep, self.recv = self.order.gate(self.keep, self.recv)
        self.other = crossed(self.order.mark(halves_call(self.keep, self.recv)), 1)

    def over_ctx(self):
        parts = self.order.gate(self.keep, self.recv, self.other)
        outs = quarters_call(self.idx, *parts, self.direct)
        if not self.split:
            self.total = lax.psum(self.order.mark(outs), "ctx")
        elif self.direct:
            self.own = self.order.mark(outs[0])
            self.recv = [exchange(part, "ctx", k + 1) for k, part in enumerate(outs[1:])]
        else:
            send, self.half = outs
            self.recv = crossed(self.order.mark(send), 0, "ctx")

    def ctx_half(self):
        if self.split and not self.direct:
            self.half, self.recv = self.order.gate(self.half, self.recv)
            far = self.order.mark(added(self.half[0], self.recv[0]))
            self.other = crossed(far, 1, "ctx")

    def ctx_sum(self):
        if not self.split:
            return
        if self.direct:
            self.own = self.order.mark(added(*self.order.gate(self.own, *self.recv)))
            self.recv = [exchange(self.own, "ctx", k) for k in (1, 2, 3)]
        else:
            half, recv, other = self.order.gate(self.half, self.recv, self.other)
            self.own = self.order.mark(added(half[1], recv[1], other))
            self.recv = [crossed(self.own, 1, "ctx"), crossed(self.own, 0, "ctx")]

    def ctx_rest(self):
        if self.split and not self.direct:
            self.recv[0] = self.order.land(self.recv[0])
            self.recv.append(crossed(self.recv[0], 0, "ctx"))

    def regroup(self, *first):
        if self.split:
            parts, first = lax.optimization_barrier(
                (self.order.gate(self.own, *self.recv), first)
            )
            self.total = self.order.mark(regroup_call(self.idx, *parts, direct=self.direct))
        self.total = self.total.reshape(self.tiles, 256, 512)
        return first

    def to_beside(self):
        self.beside = crossed(self.order.gate(self.total), 1)

    def to_across(self):
        self.across = crossed(self.order.gate(self.total), 0)

    def to_both(self):
        self.beside = self.order.land(self.beside)
        self.both = crossed(self.beside, 0)

    def swap(self, tiles, *first):
        pieces = (self.total, self.beside, self.across, self.both)
        self.pieces, first = lax.optimization_barrier((self.order.gate(*pieces), first))
        self.swapped = pair(self.order.mark(swap_call(self.pieces, tiles)))
        return first


def halves_body(keep, recv, out):
    out[...] = (keep[0].astype(f32) + recv[0].astype(f32)).astype(bf16)


def halves_call(keep, recv):
    tiles = keep.shape[1]
    step = tiles // 2
    block = pl.BlockSpec((1, step, 256, 512), lambda t: (0, t, 0, 0))
    return pl.pallas_call(
        halves_body,
        grid=(2,),
        in_specs=[block] * 2,
        out_specs=pl.BlockSpec((step, 256, 512), lambda t: (t, 0, 0)),
        out_shape=shape((tiles, 256, 512), bf16),
        compiler_params=params(),
        cost_estimate=cost(2.5),
        name="halves",
    )(keep, recv)


def quarters_body(split, direct, idx, keep, recv, other, *outs):
    def block(at):
        total = keep[0, at].astype(f32) + recv[0, at].astype(f32) + other[at].astype(f32)
        return total.astype(bf16)

    ctx, one = idx[3], 1 + idx[0]
    for k in range(4):
        if not split:
            outs[0][k] = block(k)
        elif direct:
            outs[k][...] = block(ctx ^ k)
        else:
            outs[k // 2][k % 2] = block(ctx ^ (3, one, 3 - one, 0)[k])


def quarters_call(idx, keep, recv, other, direct):
    split = lax.axis_size("ctx") == 4
    rows = keep.shape[1] * 256 // 4
    block = pl.BlockSpec((1, 4, rows, 512), lambda i, idx: (1, 0, 0, 0))
    quarter = pl.BlockSpec((4, rows, 512), lambda i, idx: (0, 0, 0))
    if not split:
        out_specs, out_shape = quarter, shape((4, rows, 512), bf16)
    elif direct:
        out_specs = [pl.BlockSpec((rows, 512), lambda i, idx: (0, 0))] * 4
        out_shape = [shape((rows, 512), bf16)] * 4
    else:
        out_specs = [pl.BlockSpec((2, rows, 512), lambda i, idx: (0, 0, 0))] * 2
        out_shape = [shape((2, rows, 512), bf16)] * 2
    return pl.pallas_call(
        functools.partial(quarters_body, split, direct),
        grid_spec=pltpu.PrefetchScalarGridSpec(
            num_scalar_prefetch=1,
            grid=(1,),
            in_specs=[block] * 2 + [quarter],
            out_specs=out_specs,
        ),
        out_shape=out_shape,
        compiler_params=params(),
        cost_estimate=cost(3.8),
        name="quarters",
    )(
        idx,
        keep.reshape(2, 4, rows, 512),
        recv.reshape(2, 4, rows, 512),
        other.reshape(4, rows, 512),
    )


def regroup_body(direct, idx, *refs):
    one = 1 + idx[0]
    for k in range(4):
        refs[4][idx[3] ^ (k if direct else (0, 3 - one, one, 3)[k])] = refs[k][...]


def regroup_call(idx, *parts, direct):
    rows = parts[0].shape[0]
    return pl.pallas_call(
        functools.partial(regroup_body, direct),
        grid_spec=pltpu.PrefetchScalarGridSpec(
            num_scalar_prefetch=1,
            grid=(1,),
            in_specs=[pl.BlockSpec((rows, 512), lambda i, idx: (0, 0))] * 4,
            out_specs=pl.BlockSpec((4, rows, 512), lambda i, idx: (0, 0, 0)),
        ),
        out_shape=shape((4, rows, 512), bf16),
        compiler_params=params(),
        cost_estimate=cost(3.0),
        name="regroup",
    )(idx, *parts)


def swap_body(*refs):
    for k, ref in enumerate(refs[:-1]):
        refs[-1][k] = ref[0]


def swap_call(pieces, tiles):
    operands = [(piece, t) for t in tiles for piece in pieces]
    return pl.pallas_call(
        swap_body,
        grid=(1,),
        in_specs=[
            pl.BlockSpec((1, TILE, 512), lambda i, t=t: (t, 0, 0)) for _, t in operands
        ],
        out_specs=pl.BlockSpec((len(operands), TILE, 512), lambda i: (0, 0, 0)),
        out_shape=shape((len(operands), TILE, 512), bf16),
        compiler_params=params(),
        cost_estimate=cost(2.5),
        name="swap",
    )(*[piece for piece, _ in operands])


def norm_parts(x):
    center = x - jnp.mean(x, axis=-1, keepdims=True)
    inverse = lax.rsqrt(jnp.mean(center * center, axis=-1, keepdims=True) + epsilon)
    return center * inverse, inverse


def vectors_body(pos_ref, *refs):
    at = 0
    for ref in refs[:-1]:
        value = ref[...].astype(f32)
        count = value.shape[0] // HALF
        refs[-1][at : at + count, :] = value.reshape(count, HALF)
        at += count
    refs[-1][at : at + 1, : pos_ref.shape[1]] = pos_ref[...].astype(f32)


def vectors_call(positions, *vectors):
    count = sum(v.shape[0] // HALF for v in vectors) + 1
    return pl.pallas_call(
        vectors_body,
        out_shape=shape((count, HALF), f32),
        compiler_params=params(),
        cost_estimate=cost(1.4),
        name="vectors",
    )(positions, *vectors)


def vector(refs, core, i):
    mine, theirs = refs[0][i : i + 1, :], refs[1][i : i + 1, :]
    first = core == 0
    return jnp.concatenate(
        [jnp.where(first, mine, theirs), jnp.where(first, theirs, mine)], axis=1
    )


def slice_body(idx, in_ref, out_ref):
    out_ref[...] = in_ref[...]


def slice_call(idx, w, width):
    step = width // 2
    return pl.pallas_call(
        slice_body,
        grid_spec=pltpu.PrefetchScalarGridSpec(
            num_scalar_prefetch=1,
            grid=(2,),
            in_specs=[pl.BlockSpec((w.shape[0], step), lambda i, idx: (0, 2 * (1 - idx[0]) + i))],
            out_specs=pl.BlockSpec((w.shape[0], step), lambda i, idx: (0, i)),
        ),
        out_shape=shape((w.shape[0], width), w.dtype),
        compiler_params=params(),
        cost_estimate=cost(3.4),
        name="slice",
    )(idx, w)


def collect_body(idx, *refs):
    share = refs[0].shape[-2]
    parts = [ref[k] for ref in refs[:-1] for k in range(ref.shape[0])]
    for k, part in enumerate(parts):
        at = pl.ds(pl.multiple_of((idx[3] ^ k) * share, share), share)
        refs[-1][:, :, at, :] = part


def collect_call(idx, *parts):
    share = parts[0].shape[-2]
    count = sum(part.shape[0] for part in parts)
    whole = lambda dims: pl.BlockSpec(dims, lambda i, idx: (0,) * len(dims))
    return pl.pallas_call(
        collect_body,
        grid_spec=pltpu.PrefetchScalarGridSpec(
            num_scalar_prefetch=1,
            grid=(1,),
            in_specs=[whole(part.shape) for part in parts],
            out_specs=whole((2, 2, share * count, D)),
        ),
        out_shape=shape((2, 2, share * count, D), bf16),
        compiler_params=params(),
        cost_estimate=cost(2.3),
        name="collect",
    )(idx, *parts)


def rows_of(core):
    return pl.ds(pl.multiple_of(core * HALF, HALF), HALF)


def place_of(bit, value):
    return jnp.where(bit == value, 1, 0)


def spread_rows(ref, tile, grad, m, core, two, lanes):
    at = pl.ds(pl.multiple_of(jnp.where(core == m, TILE, 0), TILE), TILE)
    for r in range(2):
        ref[place_of(two, r), tile, at, lanes] = grad[r * TILE : (r + 1) * TILE]


def unit_body(fresh, idx, *refs):
    refs = list(refs)
    if fresh:
        x_refs, vecs = refs[:2], refs[2:4]
        refs = refs[4:]
    else:
        a_ref, refs = refs[0], refs[3:]
    dy_refs, wu_mine, wu_recv, wd_ref, bu_ref, *refs = refs[:2], *refs[2:]
    if fresh:
        a_ref, *refs = refs
    send_ref, keep_ref, act_ref, dup_ref, bias_ref, wu_ref = refs
    core, one, two = idx[0], idx[1], idx[2]
    chunk = 256
    unit, half = pl.program_id(0) // 2, pl.program_id(0) % 2

    if fresh:

        @pl.when(pl.program_id(0) == 0)
        def _():
            gain, shift = vector(vecs, core, 2), vector(vecs, core, 3)
            for i in range(2 * ROW // chunk):
                at = slice(i % 2 * chunk, (i % 2 + 1) * chunk)
                normal, _ = norm_parts(x_refs[i // 2][at, :].astype(f32))
                a_ref[i * chunk : (i + 1) * chunk, :] = (normal * gain + shift).astype(bf16)
    wu_ref[rows_of(core), :] = wu_mine[...]
    wu_ref[rows_of(1 - core), :] = wu_recv[...]
    bias = jnp.zeros((1, chunk), f32)
    for i in range(2 * ROW // chunk):
        at, at_dy = slice(i * chunk, (i + 1) * chunk), slice(i % 2 * chunk, (i % 2 + 1) * chunk)
        up = dot(a_ref[at, :], wu_ref[...]) + bu_ref[...]
        grad = dot_nt(dy_refs[i // 2][at_dy, :], wd_ref[...])
        cdf = 0.5 * (1.0 + lax.erf(up * (0.5**0.5)))
        density = jnp.exp(-0.5 * up * up) * (1.0 / math.sqrt(2.0 * math.pi))
        act_ref[at, :] = (up * cdf).astype(bf16)
        dup = (grad * (cdf + up * density)).astype(bf16)
        dup_ref[at, :] = dup
        bias = bias + jnp.sum(dup.astype(f32), axis=0, keepdims=True)
    bias_ref[...] = bias
    lanes = lanes_of(one ^ (1 - half), chunk)
    for out, p in ((send_ref, 1 - one), (keep_ref, one)):
        for m in range(2):
            left = a_ref[:, lanes_of(2 * m + p, chunk)]
            grad = dot_tn(left, dup_ref[...]).astype(bf16)
            spread_rows(out, 2 * unit, grad, m, core, two, lanes)
    down = dot_tn(act_ref[:ROW, :], dy_refs[0][...]) + dot_tn(act_ref[ROW:, :], dy_refs[1][...])
    down = down.astype(bf16)
    for step, out in ((0, send_ref), (1, keep_ref)):

        @pl.when(half == step)
        def _(out=out):
            for r in range(2):
                out[place_of(two, r), 2 * unit + 1, :, :] = down[:, r * HALF : (r + 1) * HALF]


def unit_call(idx, first, source, dys, up_mine, up_recv, w_down, b_up, olds):
    fresh = isinstance(source, tuple)
    rows = 2 * ROW

    def sub(s, idx):
        return 2 * (first + s // 2) + (idx[1] ^ (1 - s % 2))

    def whole(dims):
        return pl.BlockSpec(dims, lambda s, idx: (0,) * len(dims))

    column = pl.BlockSpec((rows, 256), lambda s, idx: (0, sub(s, idx)))
    grads = whole((2, 4, 256, 512))
    if fresh:
        own, other, vectors = source
        operands = [own, other, *vectors]
        in_specs = [whole(v.shape) for v in operands]
        out_specs, out_shape = [whole((rows, D))], [shape((rows, D), bf16)]
        aliases = {}
    else:
        operands = [source, *olds]
        in_specs = [whole((rows, D))] + [pl.BlockSpec(memory_space=pl.ANY)] * 2
        out_specs, out_shape = [], []
        aliases = {2: 2, 3: 3}
    return pl.pallas_call(
        functools.partial(unit_body, fresh),
        grid_spec=pltpu.PrefetchScalarGridSpec(
            num_scalar_prefetch=1,
            grid=(4,),
            in_specs=in_specs
            + [
                whole((ROW, D)),
                whole((ROW, D)),
                pl.BlockSpec((HALF, 256), lambda s, idx: (0, idx[0] * 8 + sub(s, idx))),
                pl.BlockSpec((HALF, 256), lambda s, idx: (0, sub(s, idx))),
                pl.BlockSpec((256, D), lambda s, idx: (sub(s, idx), 0)),
                pl.BlockSpec((1, 256), lambda s, idx: (0, sub(s, idx))),
            ],
            out_specs=out_specs
            + [
                grads,
                grads,
                column,
                column,
                pl.BlockSpec((1, 256), lambda s, idx: (0, sub(s, idx) - 2 * first)),
            ],
            scratch_shapes=[pltpu.VMEM((D, 256), bf16)],
        ),
        out_shape=out_shape
        + [
            shape((2, 4, 256, 512), bf16),
            shape((2, 4, 256, 512), bf16),
            shape((rows, FF // 2), bf16),
            shape((rows, FF // 2), bf16),
            shape((1, 1024), f32),
        ],
        input_output_aliases=aliases,
        compiler_params=params(),
        cost_estimate=cost(18),
        name="feed_forward",
    )(idx, *operands, *dys, up_mine, up_recv, w_down, b_up)


def rotated(field, cosine, sine, direction):
    lane = lax.broadcasted_iota(jnp.int32, field.shape, 1) % HD
    partner = jnp.where(
        lane < ROT // 2,
        pltpu.roll(field, PAIR - ROT // 2, 1),
        pltpu.roll(field, ROT // 2, 1),
    )
    return field * cosine + (direction * sine) * partner


def whole_qkv(core, mine, recv_ref, w_ref):
    for t in range(3):
        w_ref[rows_of(core), t * HALF : (t + 1) * HALF] = mine[t][...]
    w_ref[rows_of(1 - core), :] = recv_ref[...]


def qkv_specs():
    return [
        pl.BlockSpec((HALF, HALF), lambda i, idx, t=t: (0, 2 * t + idx[0])) for t in range(3)
    ] + [pl.BlockSpec((HALF, 3 * HALF), lambda i, idx: (0, 0))]


def qkv_bias(vecs, core, t):
    def of(c):
        owner, row = (2 * t + c) // 3, 6 + (2 * t + c) % 3
        return vecs[0 if owner == c else 1][row : row + 1, :]

    return jnp.where(core == 0, of(0), of(1))


def qkv_rows(x, core, vecs, w_ref, table, a_ref, outs):
    normal, _ = norm_parts(x.astype(f32))
    a = (normal * vector(vecs, core, 0) + vector(vecs, core, 1)).astype(bf16)
    a_ref[...] = a
    cosine, sine = table[0][...], table[1][...]
    for t, ref in enumerate(outs):
        if ref is None:
            continue
        part = slice(t * HALF, (t + 1) * HALF)
        lin = dot(a, w_ref[:, part]) + qkv_bias(vecs, core, t)
        if t == 2:
            ref[...] = lin.astype(bf16)
            continue
        for j in range(PAIRS):
            lanes = slice(j * PAIR, (j + 1) * PAIR)
            ref[:, lanes] = rotated(lin[:, lanes], cosine, sine, 1.0).astype(bf16)


def qkv_own_body(idx, *refs):
    xs, dys, vecs, weights, recv_ref = refs[0:2], refs[2:4], refs[4:6], refs[6:9], refs[9]
    wp_ref, pos_ref, tables = refs[10], refs[11], refs[12:14]
    a1, q1, k1, v1, d1, w_out, w_ref = refs[14:]
    step, core = pl.program_id(0), idx[0]

    @pl.when(step == 0)
    def _():
        whole_qkv(core, weights, recv_ref, w_ref)
        w_out[...] = w_ref[...]

    for j in range(2):

        @pl.when(step // 2 == j)
        def _(j=j):
            qkv_rows(xs[j][...], core, vecs, w_ref, tables, a1, (q1, k1, v1))
            dol = dot_nt(dys[j][...], wp_ref[...])
            glob_n, rows = pos_ref.shape[1], dol.shape[0]
            row = lax.broadcasted_iota(jnp.int32, (rows, glob_n), 0)
            row = row + idx[3] * ROW + step % 2 * rows
            hits = jnp.sum((row == pos_ref[j : j + 1, :]).astype(f32), axis=1, keepdims=True)
            d1[...] = jnp.where(hits > 0.0, 0.0, dol).astype(bf16)


def qkv_more_body(idx, *refs):
    prevs, globs, vecs, w_ref, wp_ref = refs[0:2], refs[2], refs[3:5], refs[5], refs[6]
    before, far = refs[7:9], refs[9:11]
    a2, k2, v2, a3, q3, k3, v3, d3 = refs[11:]
    step, core = pl.program_id(0), idx[0]
    for j in range(2):

        @pl.when(step // 2 == j)
        def _(j=j):
            qkv_rows(prevs[j][...], core, vecs, w_ref, before, a2, (None, k2, v2))

    @pl.when(step == 4)
    def _():
        x = jnp.concatenate([globs[0, 0], globs[1, 0]], axis=0)
        qkv_rows(x, core, vecs, w_ref, far, a3, (q3, k3, v3))
        dy = jnp.concatenate([globs[0, 1], globs[1, 1]], axis=0)
        d3[...] = dot_nt(dy, wp_ref[...]).astype(bf16)


def clamped(i, low, count):
    return jnp.clip(i - low, 0, count - 1)


def qkv_block(low, count, width, period=None):
    def at(i, idx):
        block = clamped(i, low, count)
        return (block % period if period else block, 0)

    return pl.BlockSpec((256, width), at)


def whole_block(dims):
    return pl.BlockSpec(dims, lambda i, idx: (0,) * len(dims))


def qkv_own_call(idx, xs, dys, vectors, mine, recv, w_proj, positions, tables):
    rows = 2 * ROW
    third = qkv_block(0, 4, HALF)
    return pl.pallas_call(
        qkv_own_body,
        grid_spec=pltpu.PrefetchScalarGridSpec(
            num_scalar_prefetch=1,
            grid=(4,),
            in_specs=[qkv_block(0, 2, D), qkv_block(2, 2, D)] * 2
            + [whole_block(v.shape) for v in vectors]
            + qkv_specs()
            + [whole_block(w_proj.shape), whole_block(positions.shape)]
            + [qkv_block(0, 4, PAIR, 2)] * 2,
            out_specs=[qkv_block(0, 4, D)] + [third] * 4 + [whole_block((D, 3 * HALF))],
            scratch_shapes=[pltpu.VMEM((D, 3 * HALF), bf16)],
        ),
        out_shape=[shape((rows, D), bf16)]
        + [shape((rows, HALF), bf16)] * 4
        + [shape((D, 3 * HALF), bf16)],
        compiler_params=params(),
        cost_estimate=cost(11),
        name="qkv_own",
    )(idx, *xs, *dys, *vectors, mine, mine, mine, recv, w_proj, positions, *tables)


def qkv_more_call(idx, prevs, globs, vectors, w, w_proj, before, far):
    rows, glob_n = 2 * ROW, 2 * globs.shape[2]
    third, glob = qkv_block(0, 4, HALF), whole_block((glob_n, HALF))
    return pl.pallas_call(
        qkv_more_body,
        grid_spec=pltpu.PrefetchScalarGridSpec(
            num_scalar_prefetch=1,
            grid=(5,),
            in_specs=[qkv_block(0, 2, D), qkv_block(2, 2, D)]
            + [whole_block(v.shape) for v in (globs, *vectors, w, w_proj)]
            + [qkv_block(0, 4, PAIR, 2)] * 2
            + [whole_block((glob_n, PAIR))] * 2,
            out_specs=[qkv_block(0, 4, D), third, third, whole_block((glob_n, D))] + [glob] * 4,
        ),
        out_shape=[shape((rows, D), bf16)]
        + [shape((rows, HALF), bf16)] * 2
        + [shape((glob_n, D), bf16)]
        + [shape((glob_n, HALF), bf16)] * 4,
        compiler_params=params(),
        cost_estimate=cost(10),
        name="qkv_more",
    )(idx, *prevs, globs, *vectors, w, w_proj, *before, *far)


def heads_beside(block_t):
    dim = lax.broadcasted_iota(jnp.int32, block_t.shape, 0)
    zero = jnp.zeros_like(block_t)
    return jnp.concatenate(
        [jnp.where(dim < HD, block_t, zero), jnp.where(dim < HD, zero, block_t)], axis=1
    )


def heads_below(block):
    dim = lax.broadcasted_iota(jnp.int32, block.shape, 1)
    zero = jnp.zeros_like(block)
    return jnp.concatenate(
        [jnp.where(dim < HD, block, zero), jnp.where(dim < HD, zero, block)], axis=0
    )


def heads_back(both):
    n = both.shape[1] // 2
    dim = lax.broadcasted_iota(jnp.int32, (PAIR, n), 0)
    return jnp.where(dim < HD, both[:, :n], both[:, n:])


def near_body(
    info,
    q_ref,
    k_ref,
    v_ref,
    dol_ref,
    kp_ref,
    vp_ref,
    kg_ref,
    vg_ref,
    glob_ref,
    cos_ref,
    sin_ref,
    cosp_ref,
    sinp_ref,
    cosg_ref,
    sing_ref,
    *rest,
):
    o_ref, dq_ref, dk_ref, dv_ref, dkp_ref, dvp_ref, dkg_ref, dvg_ref, dk_acc, dv_acc = rest
    scale = HD**-0.5
    base = info[0]
    absent = jnp.where(base == 0, f32(negative), f32(0.0))
    keys = jnp.concatenate([kp_ref[...], k_ref[...]], axis=0)
    values = jnp.concatenate([vp_ref[...], v_ref[...]], axis=0)
    keys_t = keys.T
    values_t = values.T
    gkeys, gvalues = kg_ref[...], vg_ref[...]
    glob_n = gkeys.shape[0]
    gkeys_t = gkeys.astype(f32).T.astype(bf16)
    gvalues_t = gvalues.astype(f32).T.astype(bf16)
    keys_values = jnp.concatenate([keys, values], axis=1)
    gkeys_values = jnp.concatenate([gkeys, gvalues], axis=1)
    query = (q_ref[...].astype(f32) * scale).astype(bf16)
    query_t = query.T
    dol = dol_ref[...]
    dol_t = dol.T
    two = 2 * TILE
    window = WIN + TILE
    cosine, sine = cos_ref[...], sin_ref[...]
    row = lax.broadcasted_iota(jnp.int32, (TILE, two), 0)
    lane = lax.broadcasted_iota(jnp.int32, (TILE, two), 1) % TILE
    glane = lax.broadcasted_iota(jnp.int32, (glob_n, two), 1) % TILE
    gpos = jnp.concatenate([glob_ref[0], glob_ref[0]], axis=1)
    dkg = jnp.zeros((glob_n, PAIR), f32)
    dvg = jnp.zeros((glob_n, PAIR), f32)
    kk, vv = [None] * 8, [None] * 8
    def products(t):
        rows = slice(t * TILE, (t + 1) * TILE)
        q_beside = heads_beside(query_t[:, rows])
        d_beside = heads_beside(dol_t[:, rows])
        blank = jnp.zeros_like(q_beside)
        right = jnp.concatenate(
            [
                jnp.concatenate([q_beside, blank], axis=1),
                jnp.concatenate([blank, d_beside], axis=1),
            ],
            axis=0,
        )
        return dot(keys_values[t * TILE : t * TILE + window], right), dot(gkeys_values, right)

    ahead = products(0)
    for t in range(ROW // TILE):
        rows = slice(t * TILE, (t + 1) * TILE)
        span = slice(t * TILE, t * TILE + window)
        cut = WIN - t * TILE
        q_beside = heads_beside(query_t[:, rows])
        d_beside = heads_beside(dol_t[:, rows])
        q_below = heads_below(query[rows])
        d_below = heads_below(dol[rows])
        both, far_both = ahead
        if t + 1 < ROW // TILE:
            ahead = products(t + 1)
        score, d_prob = both[:, :two], both[:, two:]
        far, d_far = far_both[:, :two], far_both[:, two:]
        parts = [
            jnp.where(row > lane, score[:TILE] + absent, negative),
        ]
        if cut > TILE:
            parts.append(score[TILE:cut] + absent)
        parts.append(score[cut:WIN])
        if t == 0:
            parts.pop()
        parts.append(jnp.where(row <= lane, score[WIN:], negative))
        score = jnp.concatenate(parts, axis=0)
        far = jnp.where(base + t * TILE + glane - gpos >= WIN, far, negative)
        top = jnp.maximum(
            jnp.max(score, axis=0, keepdims=True), jnp.max(far, axis=0, keepdims=True)
        )
        prob = jnp.exp(score - top)
        far_prob = jnp.exp(far - top)
        total = jnp.sum(prob, axis=0, keepdims=True) + jnp.sum(far_prob, axis=0, keepdims=True)
        delta = jnp.sum(prob * d_prob, axis=0, keepdims=True) + jnp.sum(
            far_prob * d_far, axis=0, keepdims=True
        )
        inverse = 1.0 / total
        delta = delta * inverse
        prob = prob * inverse
        far_prob = far_prob * inverse
        low, far_low = prob.astype(bf16), far_prob.astype(bf16)
        d_score = (prob * (d_prob - delta)).astype(bf16)
        d_far = (far_prob * (d_far - delta)).astype(bf16)
        out_t = dot(values_t[:, span], low) + dot(gvalues_t, far_low)
        o_ref[rows, :] = heads_back(out_t).T.astype(bf16)
        dq_t = dot(keys_t[:, span], d_score) + dot(gkeys_t, d_far)
        dq = heads_back(dq_t).T * scale
        dq_ref[rows, :] = rotated(dq, cosine[rows], sine[rows], -1.0).astype(bf16)
        tk, tv = dot(d_score, q_below), dot(low, d_below)
        for b in range(5):
            bk, bv = tk[b * TILE : (b + 1) * TILE], tv[b * TILE : (b + 1) * TILE]
            kk[t + b] = bk if kk[t + b] is None else kk[t + b] + bk
            vv[t + b] = bv if vv[t + b] is None else vv[t + b] + bv
        dkg = dkg + dot(d_far, q_below)
        dvg = dvg + dot(far_low, d_below)
    for b in range(8):
        dk_acc[b * TILE : (b + 1) * TILE, :] = kk[b]
        dv_acc[b * TILE : (b + 1) * TILE, :] = vv[b]
    dk_ref[...] = dk_acc[ROW:, :]
    dv_ref[...] = dv_acc[ROW:, :]
    dkp_ref[...] = rotated(dk_acc[:ROW, :], cosp_ref[...], sinp_ref[...], -1.0).astype(bf16)
    dvp_ref[...] = dv_acc[:ROW, :].astype(bf16)
    dkg_ref[...] = rotated(dkg, cosg_ref[...], sing_ref[...], -1.0).astype(bf16)
    dvg_ref[...] = dvg.astype(bf16)


def near_call(info, j, q, k, v, dol, k2, v2, kg, vg, glob_wide, tables, before, far):
    glob_n = glob_wide.shape[1]
    own = pl.BlockSpec((ROW, PAIR), lambda h, info: (j, h))
    glob = pl.BlockSpec((glob_n, PAIR), lambda h, info: (j, h))
    table = pl.BlockSpec((ROW, PAIR), lambda h, info: (0, 0))
    gtable = pl.BlockSpec((glob_n, PAIR), lambda h, info: (j, 0))
    own_out = pl.BlockSpec((ROW, PAIR), lambda h, info: (0, h))
    glob_out = pl.BlockSpec((glob_n, PAIR), lambda h, info: (0, h))
    own_low, own_high = shape((ROW, HALF), bf16), shape((ROW, HALF), f32)
    glob_low = shape((glob_n, HALF), bf16)
    return pl.pallas_call(
        near_body,
        grid_spec=pltpu.PrefetchScalarGridSpec(
            num_scalar_prefetch=1,
            grid=(PAIRS,),
            in_specs=[own] * 6
            + [glob] * 2
            + [pl.BlockSpec((1, glob_n, PAIR), lambda h, info: (j, 0, 0))]
            + [table] * 4
            + [gtable] * 2,
            out_specs=[own_out] * 6 + [glob_out] * 2,
            scratch_shapes=[pltpu.VMEM((2 * ROW, PAIR), f32)] * 2,
        ),
        out_shape=[own_low, own_low, own_high, own_high, own_low, own_low, glob_low, glob_low],
        compiler_params=params(),
        cost_estimate=cost(17.5),
        name="near",
    )(info, q, k, v, dol, k2, v2, kg, vg, glob_wide, *tables, *before, *far)


def glob_first_body(info, qg_ref, k_ref, v_ref, glob_ref, out_ref):
    glob_n = qg_ref.shape[0]
    key_pos = info[0] + lax.broadcasted_iota(jnp.int32, (ROW, 2 * glob_n), 0)
    mask = key_pos <= glob_ref[0][0:1]
    lane = lax.broadcasted_iota(jnp.int32, (HD, 2 * glob_n), 1)
    for h in range(HALF // PAIR):
        lanes = slice(h * PAIR, (h + 1) * PAIR)
        query = qg_ref[:, lanes].astype(f32) * HD**-0.5
        beside = heads_beside(query.T).astype(bf16)
        masked = jnp.where(mask, dot(k_ref[:, lanes], beside), negative)
        top = jnp.max(masked, axis=0, keepdims=True)
        prob = jnp.where(mask, jnp.exp(masked - top), 0.0)
        total = jnp.sum(prob, axis=0, keepdims=True)
        both = dot(v_ref[:, lanes].T, prob.astype(bf16))
        out_ref[h, 0:HD, :] = jnp.where(lane < glob_n, both[:HD], both[HD:])
        out_ref[h, HD : HD + 1, :] = top
        out_ref[h, HD + 1 : HD + 2, :] = total
        out_ref[h, HD + 2 : HD + 8, :] = jnp.zeros((6, 2 * glob_n), f32)


def glob_first_call(info, qg, k, v, glob_row):
    glob_n = glob_row.shape[2] // 2
    own = pl.BlockSpec((ROW, HALF), lambda j, info: (j, 0))
    pairs = HALF // PAIR
    return pl.pallas_call(
        glob_first_body,
        grid_spec=pltpu.PrefetchScalarGridSpec(
            num_scalar_prefetch=1,
            grid=(2,),
            in_specs=[
                pl.BlockSpec((glob_n, HALF), lambda j, info: (j, 0)),
                own,
                own,
                pl.BlockSpec((1, 8, 2 * glob_n), lambda j, info: (j, 0, 0)),
            ],
            out_specs=pl.BlockSpec((pairs, HD + 8, 2 * glob_n), lambda j, info: (j, 0, 0)),
        ),
        out_shape=shape((2 * pairs, HD + 8, 2 * glob_n), f32),
        compiler_params=params(),
        cost_estimate=cost(4),
        name="glob_first",
    )(info, qg, k, v, glob_row)


def merged(first, second):
    top_a, top_b = first[:, HD : HD + 1], second[:, HD : HD + 1]
    top = jnp.maximum(top_a, top_b)
    weight_a, weight_b = jnp.exp(top_a - top), jnp.exp(top_b - top)
    total = first[:, HD + 1 : HD + 2] * weight_a + second[:, HD + 1 : HD + 2] * weight_b
    out = first[:, :HD] * weight_a + second[:, :HD] * weight_b
    return jnp.concatenate([out, top, total, first[:, HD + 2 :]], axis=1)


def glob_second_body(
    info,
    qg_ref,
    dolg_ref,
    k_ref,
    v_ref,
    glob_ref,
    cos_ref,
    sin_ref,
    cosg_ref,
    sing_ref,
    *rest,
):
    near, rest = rest[:6], rest[6:]
    stat_refs, (o_ref, dk_ref, dv_ref, dqg_ref) = rest[:-4], rest[-4:]
    first = pl.program_id(0) == 0
    scale = HD**-0.5
    glob_n = qg_ref.shape[0]
    key_pos = info[0] + lax.broadcasted_iota(jnp.int32, (ROW, 2 * glob_n), 0)
    positions = glob_ref[0][0:1]
    mask = key_pos <= positions
    place = (key_pos[:, :glob_n] == positions[:, :glob_n]).astype(f32)
    hit = jnp.sum(place, axis=1, keepdims=True) > 0.0
    place = place.astype(bf16)
    cosine, sine = cos_ref[...], sin_ref[...]
    cosine_g, sine_g = cosg_ref[...], sing_ref[...]
    for h in range(HALF // PAIR):
        lanes = slice(h * PAIR, (h + 1) * PAIR)
        keys, values = k_ref[:, lanes], v_ref[:, lanes]
        query = qg_ref[:, lanes].astype(f32) * scale
        q_beside = heads_beside(query.T).astype(bf16)
        q_below = heads_below(query.astype(bf16))
        dol = dolg_ref[:, lanes]
        dol_t = dol.astype(f32).T
        d_beside = heads_beside(dol_t).astype(bf16)
        d_below = heads_below(dol)
        tops = [ref[h, HD : HD + 1, :] for ref in stat_refs]
        top = functools.reduce(jnp.maximum, tops)
        weights = [jnp.exp(part - top) for part in tops]
        total = sum(w * ref[h, HD + 1 : HD + 2, :] for w, ref in zip(weights, stat_refs))
        out_t = sum(w * ref[h, 0:HD, :] for w, ref in zip(weights, stat_refs)) * (1.0 / total)
        lse = top + jnp.log(total)
        delta = jnp.sum(
            out_t * jnp.concatenate([dol_t[:HD], dol_t[HD:]], axis=1), axis=0, keepdims=True
        )
        score = jnp.where(mask, dot(keys, q_beside), negative)
        prob = jnp.where(mask, jnp.exp(score - lse), 0.0)
        d_score = (prob * (dot(values, d_beside) - delta)).astype(bf16)
        near_o, near_dk, near_dv = (
            jnp.where(first, near[i][:, lanes], near[i + 1][:, lanes]) for i in (0, 2, 4)
        )
        dk = near_dk + dot(d_score, q_below)
        dv = near_dv + dot(prob.astype(bf16), d_below)
        dk_ref[:, lanes] = rotated(dk, cosine, sine, -1.0).astype(bf16)
        dv_ref[:, lanes] = dv.astype(bf16)
        dq_both = dot(keys.T, d_score)
        dq_t = jnp.concatenate([dq_both[:HD, :glob_n], dq_both[HD:, glob_n:]], axis=0)
        dqg_ref[:, lanes] = rotated(dq_t.T * scale, cosine_g, sine_g, -1.0).astype(bf16)
        rows = jnp.concatenate([out_t[:, :glob_n], out_t[:, glob_n:]], axis=0).T.astype(bf16)
        o_ref[:, lanes] = jnp.where(hit, dot(place, rows).astype(bf16), near_o)


def glob_second_call(info, qg, dolg, k, v, stats, glob_row, near, tables, far):
    glob_n = glob_row.shape[2] // 2
    pairs = HALF // PAIR
    rows = k.shape[0]
    own = pl.BlockSpec((ROW, HALF), lambda j, info: (j, 0))
    glob = pl.BlockSpec((glob_n, HALF), lambda j, info: (j, 0))
    table = pl.BlockSpec((ROW, PAIR), lambda j, info: (0, 0))
    gtable = pl.BlockSpec((glob_n, PAIR), lambda j, info: (j, 0))
    return pl.pallas_call(
        glob_second_body,
        grid_spec=pltpu.PrefetchScalarGridSpec(
            num_scalar_prefetch=1,
            grid=(2,),
            in_specs=[
                glob,
                glob,
                own,
                own,
                pl.BlockSpec((1, 8, 2 * glob_n), lambda j, info: (j, 0, 0)),
                table,
                table,
                gtable,
                gtable,
            ]
            + [pl.BlockSpec((ROW, HALF), lambda j, info: (0, 0))] * 6
            + [pl.BlockSpec((pairs, HD + 8, 2 * glob_n), lambda j, info: (j, 0, 0))] * len(stats),
            out_specs=[own, own, own, glob],
        ),
        out_shape=[shape((rows, HALF), bf16)] * 3 + [shape((2 * glob_n, HALF), bf16)],
        compiler_params=params(),
        cost_estimate=cost(8),
        name="glob_second",
    )(info, qg, dolg, k, v, glob_row, *tables, *far, *near, *stats)


def weights_body(tiles, idx, *refs):
    core, two = idx[0], idx[2]

    def run(at, ref):
        for tile in (at, at + 1):
            kind, operands = tiles[tile]
            if kind == "rows":
                total = sum(dot_tn(refs[left][...], refs[right][...]) for left, right in operands)
                total = total.astype(bf16)
                for r in range(2):
                    ref[place_of(two, r), tile, :, :] = total[:, r * HALF : (r + 1) * HALF]
                continue
            for m in range(2):
                total = None
                for left, right in operands:
                    term = dot_tn(refs[left + m][...], refs[right][...])
                    total = term if total is None else total + term
                spread_rows(ref, tile, total.astype(bf16), m, core, two, slice(None))

    for at in range(0, len(tiles), 2):
        for half in range(2):

            @pl.when(pl.program_id(0) == at + half)
            def _(at=at, half=half):
                run(at, refs[len(refs) - 2 + half])


def weights_call(idx, tiles):
    specs, operands, table, lefts = [], [], [], {}

    def add(array, spec):
        specs.append(spec)
        operands.append(array)
        return len(operands) - 1

    def whole(array):
        return add(array, pl.BlockSpec(array.shape, lambda s, idx: (0, 0)))

    def part(s, idx):
        return idx[1] ^ (1 - s % 2)

    def left_of(array, rows, j):
        if (id(array), rows, j) not in lefts:
            specs = [
                pl.BlockSpec((rows, 256), lambda s, idx, m=m: (j, 2 * m + part(s, idx)))
                for m in range(2)
            ]
            lefts[id(array), rows, j] = [add(array, spec) for spec in specs][0]
        return lefts[id(array), rows, j]

    for kind, products in tiles:
        if kind == "rows":
            pairs = []
            for j, (left, right) in enumerate(products):
                spec = pl.BlockSpec((right.shape[0], 256), lambda s, idx, j=j: (j, part(s, idx)))
                pairs.append((add(left, spec), whole(right)))
        else:
            pairs = []
            for left, *rights in products:
                for j, right in enumerate(rights):
                    pairs.append((left_of(left, right.shape[0], j), whole(right)))
        table.append((kind, tuple(pairs)))
    count = len(tiles)
    out = pl.BlockSpec((2, count, 256, 512), lambda s, idx: (0, 0, 0, 0))
    return pl.pallas_call(
        functools.partial(weights_body, tuple(table)),
        grid_spec=pltpu.PrefetchScalarGridSpec(
            num_scalar_prefetch=1, grid=(count,), in_specs=specs, out_specs=[out] * 2
        ),
        out_shape=[shape((2, count, 256, 512), bf16)] * 2,
        compiler_params=params(),
        cost_estimate=cost(16),
        name="weight_grads",
    )(idx, *operands)


def input_body(idx, *refs):
    x_ref, xo_ref, xp_ref, xop_ref, glob_ref = refs[:5]
    vecs, core = refs[5:7], idx[0]
    w_ref, up_mine, up_recv = refs[7:10]
    dqs, dk1, dv1, dkps, dvps, dqg = refs[10:12], refs[12], refs[13], refs[14:16], refs[16:18], refs[18]
    dkgs, dvgs, dup_ref = refs[19:21], refs[21:23], refs[23]
    mine, other, sums_a, sums_m, bias_ref, wu_ref = refs[24:]
    step = pl.program_id(0)

    @pl.when(step == 0)
    def _():
        sums_a[...] = jnp.zeros_like(sums_a)
        sums_m[...] = jnp.zeros_like(sums_m)
        bias_ref[...] = jnp.zeros_like(bias_ref)
        wu_ref[rows_of(idx[0]), :] = up_mine[...]
        wu_ref[rows_of(1 - idx[0]), :] = up_recv[...]

    def gather(sums, grad, normal):
        sums[0:1, :] += jnp.sum(grad * normal, axis=0, keepdims=True)
        sums[1:2, :] += jnp.sum(grad, axis=0, keepdims=True)

    def attn(x, parts):
        grad = None
        for t, part in enumerate(parts):
            if part is None:
                continue
            lanes = slice(t * HALF, (t + 1) * HALF)
            term = dot_nt(part, w_ref[:, lanes])
            grad = term if grad is None else grad + term
            bias_ref[0:1, lanes] += jnp.sum(part.astype(f32), axis=0, keepdims=True)
        normal, _ = norm_parts(x.astype(f32))
        gather(sums_a, grad, normal)
        return grad * vector(vecs, core, 0), normal

    def own_rows(x, dq, out):
        g, normal = attn(x[...], (dq[...], dk1[...], dv1[...]))
        grad = dot_nt(dup_ref[...], wu_ref[...])
        gather(sums_m, grad, normal)
        out[...] = (g + grad * vector(vecs, core, 2)).astype(bf16)

    @pl.when(step < 2)
    def _():
        own_rows(x_ref, dqs[0], mine)

    @pl.when((step >= 2) & (step < 4))
    def _():
        own_rows(xo_ref, dqs[1], other)

    @pl.when((step >= 4) & (step < 6))
    def _():
        mine[...] = attn(xp_ref[...], (None, dkps[0][...], dvps[0][...]))[0].astype(bf16)

    @pl.when((step >= 6) & (step < 8))
    def _():
        other[...] = attn(xop_ref[...], (None, dkps[1][...], dvps[1][...]))[0].astype(bf16)

    @pl.when(step == 8)
    def _():
        rows = jnp.concatenate([glob_ref[0, 0], glob_ref[1, 0]], axis=0)
        dkg, dvg = (jnp.concatenate([v[0][...], v[1][...]], axis=0) for v in (dkgs, dvgs))
        grad = attn(rows, (dqg[...], dkg, dvg))[0].astype(bf16)
        glob_n = glob_ref.shape[2]
        mine[:glob_n, :] = grad[:glob_n]
        other[:glob_n, :] = grad[glob_n:]


def input_call(idx, xs, prevs, globs, vectors, w_qkv, up_mine, up_recv, grads):
    step, rows, glob_n = 256, 2 * ROW, 2 * globs.shape[2]
    part = pl.BlockSpec((2, 1, *globs.shape[2:]), lambda i, idx: (0, 0, 0, 0))

    def mine_at(i):
        return jnp.where(i < 4, jnp.minimum(i, 1), jnp.where(i < 8, jnp.minimum(i - 2, 3), 4))

    def other_at(i):
        return jnp.where(i < 6, clamped(i, 2, 2), jnp.where(i < 8, i - 4, 4))


    def block(low, count, width):
        return pl.BlockSpec((step, width), lambda i, idx: (clamped(i, low, count), 0))

    whole = lambda rows, width: pl.BlockSpec((rows, width), lambda i, idx: (0, 0))
    return pl.pallas_call(
        input_body,
        grid_spec=pltpu.PrefetchScalarGridSpec(
            num_scalar_prefetch=1,
            grid=(9,),
            in_specs=[block(2 * j, 2, D) for j in range(4)]
            + [part]
            + [whole(*v.shape) for v in vectors]
            + [whole(*w_qkv.shape)]
            + [
                pl.BlockSpec((HALF, FF // 2), lambda i, idx: (0, idx[0])),
                whole(HALF, FF // 2),
            ]
            + [block(0, 2, HALF), block(2, 2, HALF)]
            + [block(0, 4, HALF)] * 2
            + [block(4, 2, HALF), block(6, 2, HALF)] * 2
            + [whole(glob_n, HALF)]
            + [whole(glob_n // 2, HALF)] * 4
            + [block(0, 4, FF // 2)],
            out_specs=[
                pl.BlockSpec((step, D), lambda i, idx: (mine_at(i), 0)),
                pl.BlockSpec((step, D), lambda i, idx: (other_at(i), 0)),
                whole(8, D),
                whole(8, D),
                whole(8, 3 * HALF),
            ],
            scratch_shapes=[pltpu.VMEM((D, FF // 2), bf16)],
        ),
        out_shape=[shape((rows + step, D), bf16)] * 2
        + [
            shape((8, D), f32),
            shape((8, D), f32),
            shape((8, 3 * HALF), f32),
        ],
        compiler_params=params(),
        cost_estimate=cost(24),
        name="input_grads",
    )(
        idx,
        *xs,
        *prevs,
        globs,
        *vectors,
        w_qkv,
        up_mine,
        up_recv,
        *grads,
    )


def result_body(act_ref, wd_ref, ol_ref, wp_ref, mine_ref, other_ref):
    part = (dot(act_ref[...], wd_ref[...]) + dot(ol_ref[...], wp_ref[...])).astype(bf16)
    half = pl.num_programs(0) // 2

    @pl.when(pl.program_id(0) < half)
    def _():
        mine_ref[...] = part

    @pl.when(pl.program_id(0) >= half)
    def _():
        other_ref[...] = part


def result_call(act, w_down, ol, w_proj):
    rows, step = act.shape[0], 256
    half = rows // step // 2
    return pl.pallas_call(
        result_body,
        grid=(rows // step,),
        in_specs=[
            pl.BlockSpec((step, act.shape[1]), lambda i: (i, 0)),
            pl.BlockSpec(w_down.shape, lambda i: (0, 0)),
            pl.BlockSpec((step, HALF), lambda i: (i, 0)),
            pl.BlockSpec(w_proj.shape, lambda i: (0, 0)),
        ],
        out_specs=[
            pl.BlockSpec((step, D), lambda i: (jnp.minimum(i, half - 1), 0)),
            pl.BlockSpec((step, D), lambda i: (jnp.maximum(i - half, 0), 0)),
        ],
        out_shape=[shape((rows // 2, D), bf16)] * 2,
        compiler_params=params(),
        cost_estimate=cost(10.3),
        name="result",
    )(act, w_down, ol, w_proj)


def place_body(spreads, rows, n_alias, idx, *refs):
    pieces, swapped = refs[:4], refs[4]
    outs = list(refs[5 + n_alias :])
    spread_out, rows_out = outs[0], outs[1]
    one, two = idx[1], idx[2]
    for i in range(max(len(spreads), len(rows))):
        for h in range(2):

            @pl.when((pl.program_id(0) == i) & (pl.program_id(1) == h))
            def _(i=i, h=h):
                if i < len(spreads):
                    for k in range(4):
                        if h:
                            block = 2 * (two ^ (k // 2)) + (one ^ (k % 2))
                            part = swapped[4 * i + k]
                        else:
                            block = 2 * (one ^ (k // 2)) + (two ^ (k % 2))
                            part = pieces[k][spreads[i], TILE:, :]
                        spread_out[pl.ds(pl.multiple_of(block * TILE, TILE), TILE), :] = (
                            part.astype(f32)
                        )
                if i < len(rows):
                    for beside in range(2):
                        part = pieces[2 * h + beside][rows[i]]
                        rows_out[:, lanes_of(two ^ beside, HALF)] = part.astype(f32)


def place_call(idx, work, spreads, rows, spread_target, rows_target):
    targets = [spread_target, rows_target]
    alias = [buf for buf, _, _ in targets if buf is not None]
    aliases, at = {}, 6
    for out, (buf, _, _) in enumerate(targets):
        if buf is not None:
            aliases[at] = out
            at += 1

    def spread_index(i, h, idx):
        return 0, spread_target[2](i, idx[0] ^ h)

    def rows_index(i, h, idx):
        last = len(rows) - 1
        i, h = jnp.where(i > last, last, i), jnp.where(i > last, 1, h)
        return rows_target[2](i, idx[1] ^ h), 0

    whole = lambda array: pl.BlockSpec(array.shape, lambda i, h, idx: (0, 0, 0))
    operands = [*work.pieces, work.swapped]
    return pl.pallas_call(
        functools.partial(place_body, spreads, rows, len(alias)),
        grid_spec=pltpu.PrefetchScalarGridSpec(
            num_scalar_prefetch=1,
            grid=(len(spreads), 2),
            in_specs=[whole(array) for array in operands]
            + [pl.BlockSpec(memory_space=pl.ANY)] * len(alias),
            out_specs=[pl.BlockSpec((HALF, 512), spread_index), pl.BlockSpec((256, D), rows_index)],
        ),
        out_shape=[shape(dims, f32) for _, dims, _ in targets],
        input_output_aliases=aliases,
        compiler_params=params(),
        cost_estimate=cost(7.0),
        name="place",
    )(idx, *operands, *alias)


def rotary_tables(positions):
    lane = jnp.arange(PAIR, dtype=jnp.int32) % HD
    half = ROT // 2
    freqs = rotary_base ** (-2.0 * (lane % half).astype(f32) / ROT)
    angles = positions.astype(f32)[:, None] * freqs[None, :]
    active = (lane < ROT)[None, :]
    sign = jnp.where(lane < half, -1.0, 1.0)[None, :]
    return jnp.where(active, jnp.cos(angles), 1.0), jnp.where(active, jnp.sin(angles) * sign, 0.0)


def per_device(
    tokens,
    cotangent,
    global_pos,
    attn_gain,
    attn_shift,
    mlp_gain,
    mlp_shift,
    qkv_weight,
    qkv_bias,
    proj_weight,
    proj_bias,
    up_weight,
    up_bias,
    down_weight,
    down_bias,
):
    n_ctx = lax.axis_size("ctx")
    core = lax.axis_index("fsdp")
    seq = lax.axis_index("seq")
    ctx = lax.axis_index("ctx")
    x_bit, y_bit = seq & 1, seq >> 1
    base = ctx * ROW
    own_x = tokens[0]
    own_dy = cotangent[0]
    glob_n = global_pos.shape[1]
    share = glob_n // n_ctx
    info = jnp.stack([base]).astype(jnp.int32)
    one, two = jnp.where(core == 0, x_bit, y_bit), jnp.where(core == 0, y_bit, x_bit)
    idx = jnp.stack([core, one, two, ctx]).astype(jnp.int32)
    order = Order()

    other_x = pair(own_x)
    up_recv = pair(slice_call(idx, up_weight, FF // 2))
    other_dy = pair(own_dy)
    mine = vectors_call(
        global_pos, attn_gain, attn_shift, mlp_gain, mlp_shift, proj_bias, down_bias, qkv_bias
    )
    vectors = (mine, pair(mine))
    row_pos = base + jnp.arange(ROW, dtype=jnp.int32)
    own_glob = lax.dynamic_slice_in_dim(global_pos[0], ctx * share, share, 0)
    pick = (own_glob[:, None] == row_pos[None, :]).astype(bf16)
    picked = jnp.stack([dot(pick, own_x), dot(pick, own_dy)]).astype(bf16)
    picked = jnp.stack([picked, pair(picked)])[None]
    pos_pair = jnp.concatenate([v[9:10, :glob_n] for v in vectors]).astype(jnp.int32)
    bias_up = up_bias.astype(f32).reshape(1, FF // 2)
    picked, first_x = lax.optimization_barrier((picked, own_x))
    picks, distances = [picked], doubling("ctx")
    beside = exchange(picked, "ctx", distances[0])
    prev_x = shifted(first_x, 1)

    xs, dys = (own_x, other_x), (own_dy, other_dy)
    a_mlp, send, keep, act, dup, sums = unit_call(
        idx,
        0,
        (first_x, other_x, vectors),
        dys,
        up_weight,
        up_recv,
        down_weight,
        bias_up,
        None,
    )
    order.mark(sums)
    up_sums = [sums.reshape(2, 512)]
    work0 = Reduction(order, idx, send, keep, True)
    picks.append(order.land(beside))
    for distance in distances[1:]:
        picked = order.mark(jnp.concatenate(picks, axis=0))
        picks.append(exchange(picked, "ctx", distance))
    w_in = order.gate(qkv_weight)
    w_in = order.mark(
        jnp.concatenate(
            [
                lax.dynamic_slice_in_dim(w_in, (2 * t + 1 - core) * HALF, HALF, 1)
                for t in range(3)
            ],
            axis=1,
        )
    )
    qkv_recv = pair(w_in)
    send, keep, act, dup, sums = unit_call(
        idx,
        2,
        order.gate(a_mlp),
        dys,
        up_weight,
        up_recv,
        down_weight,
        bias_up,
        (act, dup),
    )
    order.mark(sums)
    up_sums.append(sums.reshape(2, 512))
    prev_x, qkv_recv = order.land(prev_x, qkv_recv)
    other_prev = pair(prev_x)
    if n_ctx == 4:
        globs = collect_call(idx, *order.gate(*picks))
    else:
        picked = jnp.concatenate(picks, axis=0)
        picked = jnp.take(picked, jnp.arange(n_ctx, dtype=jnp.int32) ^ ctx, axis=0)
        globs = jnp.transpose(picked, (1, 2, 0, 3, 4)).reshape(2, 2, glob_n, D)
    order.mark(globs)
    pos_pair = order.gate(pos_pair)
    tables = rotary_tables(row_pos)
    before = rotary_tables(row_pos - ROW)
    far = rotary_tables(pos_pair.reshape(-1))
    glob_row = jnp.broadcast_to(
        jnp.concatenate([pos_pair, pos_pair], axis=1)[:, None, :], (2, 8, 2 * glob_n)
    )
    glob_wide = jnp.broadcast_to(pos_pair[:, :, None], (2, glob_n, PAIR))
    tables, before, far, glob_row, glob_wide, other_prev, _ = lax.optimization_barrier(
        (tables, before, far, glob_row, glob_wide, other_prev, order.token)
    )
    order.mark(glob_wide)
    prevs = (prev_x, other_prev)
    work0.second()

    a1, q1, k1, v1, dol, w_qkv = qkv_own_call(
        idx,
        (order.gate(own_x), other_x),
        dys,
        vectors,
        qkv_weight,
        qkv_recv,
        proj_weight,
        pos_pair,
        tables,
    )
    order.mark(dol)
    work0.over_ctx()
    work1 = Reduction(order, idx, order.gate(send), keep, True)
    a2, k2, v2, a3, q3, k3, v3, dolg = qkv_more_call(
        idx, (order.gate(prev_x), other_prev), globs, vectors, w_qkv, proj_weight, before, far
    )
    order.mark(q3)
    stats = order.mark(glob_first_call(info, q3, k1, v1, glob_row))
    beside = exchange(stats, "ctx", 1)

    def near_of(j):
        outs = near_call(
            info, j, order.gate(q1), k1, v1, dol, k2, v2, k3, v3, glob_wide, tables, before, far
        )
        order.mark(outs[-1])
        return outs

    near0 = near_of(0)
    work1.second()
    for distance in distances[1:]:
        stats = order.mark(merged(*order.gate(stats, beside)))
        beside = exchange(stats, "ctx", distance)
    work0.ctx_sum()
    near1 = near_of(1)
    stats = order.land(stats, beside)
    near, dqs, dks, dvs, dkps, dvps, dkgs, dvgs = zip(near0, near1)
    ol, dk1, dv1, dqg = glob_second_call(
        info,
        order.gate(q3),
        dolg,
        k1,
        v1,
        stats,
        glob_row,
        (*near, *dks, *dvs),
        tables,
        far,
    )
    order.mark(dqg)
    work0.regroup()
    work0.to_beside()
    work0.to_across()
    work1.over_ctx()
    send, keep = weights_call(
        idx,
        (
            ("spread", ((a1, order.gate(dv1)), (a2, *dvps), (a3, *dvgs))),
            ("rows", ((ol, own_dy), (ol, other_dy))),
            ("spread", ((a1, *dqs), (a3, dqg))),
            ("spread", ((a1, dk1), (a2, *dkps), (a3, *dkgs))),
        ),
    )
    order.mark(send)
    work2 = Reduction(order, idx, send, keep, False)
    work0.beside, work0.across = order.land(work0.beside, work0.across)
    work1.ctx_sum()

    g_mine, g_other, sums_a, sums_m, bias = input_call(
        idx,
        (order.gate(own_x), other_x),
        prevs,
        globs,
        vectors,
        w_qkv,
        up_weight,
        up_recv,
        (*dqs, dk1, dv1, *dkps, *dvps, dqg, *dkgs, *dvgs, dup),
    )
    order.mark(bias)
    work2.second()
    work1.regroup()
    work0.to_both()
    work1.to_beside()
    work1.to_across()
    part, part_other = result_call(order.gate(act), down_weight, ol, proj_weight)
    order.mark(part)
    work2.over_ctx()
    g_beside = pair(order.gate(g_other))
    work2.ctx_half()
    prev_mine, glob_mine, g_beside = order.gate(
        g_mine[ROW : 2 * ROW], g_mine[2 * ROW : 2 * ROW + glob_n], g_beside
    )
    glob_sum = order.mark(added(glob_mine, g_beside[2 * ROW : 2 * ROW + glob_n]))
    prev_sum = order.mark(added(prev_mine, g_beside[ROW : 2 * ROW]))
    part_beside = pair(order.gate(part_other))
    work0.swap([0, 2])
    work2.ctx_sum()

    def place_units(work, first, up_out, down_out):
        up_out, down_out = place_call(
            idx,
            work,
            (0, 2),
            (1, 3),
            (up_out, (HALF, FF), lambda i, c: c * 4 + first + i),
            (down_out, (FF // 2, D), lambda i, p: (first + i) * 2 + p),
        )
        order.mark(up_out[:8, :128])
        return up_out, down_out

    own, part, part_beside = order.gate(own_x, part, part_beside)
    result = own.astype(f32) + part.astype(f32) + part_beside.astype(f32)
    first = core == 0
    for i in (4, 5):
        rows = [v[i : i + 1] for v in vectors]
        result = result + jnp.concatenate(
            [jnp.where(first, rows[0], rows[1]), jnp.where(first, rows[1], rows[0])], axis=1
        )
    layer_out = order.mark(result.astype(bf16))[None]
    beside = exchange(order.gate(glob_sum), "ctx", 1)
    up_out, down_out = place_units(work0, 0, None, None)
    work2.ctx_rest()
    work1.to_both()
    for distance in doubling("ctx")[1:]:
        glob_sum = order.mark(added(*order.gate(glob_sum, beside)))
        beside = exchange(glob_sum, "ctx", distance)

    dy_sum = jnp.sum(order.gate(own_dy).astype(f32), axis=0)
    qkv_sum = bias[0].reshape(3, 1, HALF)
    mine = jnp.arange(2, dtype=jnp.int32)[None, :, None] == core
    qkv_sum = jnp.where(mine, qkv_sum, 0.0).reshape(2, 3, 512)
    split = jnp.concatenate(
        [
            sums_a[:2].reshape(2, 2, 512).swapaxes(0, 1),
            sums_m[:2].reshape(2, 2, 512).swapaxes(0, 1),
            dy_sum.reshape(2, 1, 512),
            qkv_sum,
        ],
        axis=1,
    )
    kept = lax.dynamic_index_in_dim(split, core, 0, False)
    given = pair(order.mark(lax.dynamic_index_in_dim(split, 1 - core, 0, False)))
    work2.regroup()
    work2.to_beside()
    kept, given = order.gate(kept, given)
    total = order.mark(jnp.concatenate([kept + given] + up_sums, axis=0))
    steps = [(axis, distance) for axis in ("ctx", "seq") for distance in doubling(axis)]
    glob_sum, beside = order.gate(glob_sum, beside)
    glob_sum = order.mark(added(glob_sum, beside))
    prev_sum, work2.total = lax.optimization_barrier((prev_sum, work2.total))
    from_prev = shifted(order.gate(prev_sum), -1)
    work1.swap([0, 2])
    work2.total, work2.beside = lax.optimization_barrier((work2.total, work2.beside))
    work2.to_both()
    work2.to_across()
    up_out, down_out = place_units(work1, 2, up_out, down_out)
    for step in steps[:-2]:
        total = order.mark(total + order.gate(exchange(total, *step)))
    place = (row_pos[:, None] == global_pos[0][None, :]).astype(bf16)
    own, mine, g_beside, from_prev, glob_sum = order.gate(
        own_x, g_mine, g_beside, from_prev, glob_sum
    )
    g = (
        mine[:ROW].astype(f32)
        + g_beside[:ROW].astype(f32)
        + from_prev.astype(f32)
        + dot(place, glob_sum)
    )
    normal, inverse = norm_parts(own.astype(f32))
    lower = inverse * (
        g
        - jnp.mean(g, axis=-1, keepdims=True)
        - normal * jnp.mean(g * normal, axis=-1, keepdims=True)
    )
    tokens_grad = order.mark(own_dy.astype(f32) + lower)[None]
    for step in steps[-2:]:
        total = order.mark(total + order.gate(exchange(total, *step)))
    work2.swap([0, 2, 3])
    qkv_out, proj_out = place_call(
        idx,
        work2,
        (0, 2, 3),
        (1,),
        (None, (HALF, 3 * D), lambda i, c: 2 * ((i + 2) % 3) + c),
        (None, (HALF, D), lambda i, p: p),
    )
    return (
        layer_out,
        tokens_grad,
        total[0],
        total[1],
        total[2],
        total[3],
        qkv_out,
        total[5:8].reshape(-1),
        proj_out,
        total[4],
        up_out,
        total[8:12].reshape(-1),
        down_out,
        total[4],
    )


def solution(mesh):
    rows = P(("seq", "fsdp"), "ctx", None)
    vector, matrix = P("fsdp"), P("fsdp", None)
    return jax.shard_map(
        per_device,
        mesh=mesh,
        in_specs=(
            rows,
            rows,
            P(("seq", "fsdp"), None),
            vector,
            vector,
            vector,
            vector,
            matrix,
            vector,
            matrix,
            vector,
            matrix,
            vector,
            matrix,
            vector,
        ),
        out_specs=(
            rows,
            rows,
            vector,
            vector,
            vector,
            vector,
            matrix,
            vector,
            matrix,
            vector,
            matrix,
            vector,
            matrix,
            vector,
        ),
        check_vma=False,
    )
```
